512 devices in a mesh: dp: 64 (over x, z), mp: 8 (over y, core).
Axes of the slice: x: 4, y: 4, z: 16, core: 2. Of those that a mesh axis runs over, the one named last changes fastest.
Arguments:
- features: bfloat16 [32768, 1536], P('dp'), may hold values from -36 to 36
- frame_start: int32 [64], P('dp'), may hold values from 0 to 384
- chan_start: int32 [64], P('dp'), may hold values from 0 to 1344
- master_weight: float32 [1536, 6144], P('dp', 'mp'), may hold values from -0.15625 to 0.15625
- row_moment: float32 [1536], P('dp'), may hold values from 0.1 to 3
- col_moment: float32 [6144], P('mp'), may hold values from 0.1 to 3
- out_grad: bfloat16 [32768, 6144], P('dp', 'mp'), may hold values from -36 to 36
Outputs:
- new_master: float32 [1536, 6144], P('dp', 'mp')
- row_state: float32 [1536], P('dp')
- col_state: float32 [6144], P('mp')
- compute_weight: bfloat16 [1536, 6144], P(None, 'mp')
The draws below stay inside these ranges and needn't reach their ends.
All inputs are finite; a program needn't handle non-finite values.
Results may differ from the reference program's by a relative error of at most 0.0023.
The reference program's roundings to bfloat16 on the way (of `masked`, `weight_low` and `dpre`) count: a program that leaves them out, or rounds other values in their place, can miss the bound.
Values may be sent and summed in bfloat16 or wider, within the bound.
A program may use at most 64 MiB of HBM per device.

```python
import math
import jax
import jax.numpy as jnp
from jax import lax

D = 1536
FF = 6144
TOK_DEV = 512
TMASK = 128
FMASK = 192
UTTS = 64
TOKENS = 32768


def column_scales(key, count):
    spread = jax.random.uniform(key, (count,), jnp.float32)
    ramp = 1.0 + 2.0 * jnp.arange(count, dtype=jnp.float32) / count
    return jnp.exp(spread * jnp.log(10.0)) * ramp / 5.0


def draw_features(key, part):
    key = jax.random.fold_in(key, 11)
    scale_key, value_key = jax.random.split(key)
    scales = column_scales(scale_key, D)
    values = jnp.clip(jax.random.normal(value_key, (TOKENS, D), jnp.float32), -6.0, 6.0)
    return (values * scales[None, :]).astype(jnp.bfloat16)


def draw_out_grad(key, part):
    key = jax.random.fold_in(key, 23)
    scale_key, value_key = jax.random.split(key)
    scales = column_scales(scale_key, FF)
    values = jnp.clip(jax.random.normal(value_key, (TOKENS, FF), jnp.float32), -6.0, 6.0)
    return (values * scales[None, :]).astype(jnp.bfloat16)


def plant(result, rng, least, top_value):
    dims = result.shape
    spot = [jax.random.randint(jax.random.fold_in(rng, axis), (), 0, dims[axis]) for axis in range(len(dims))]
    result = result.at[tuple(spot)].set(least)
    longest = dims.index(max(dims))
    spot[longest] = (spot[longest] + 1) % dims[longest]
    return result.at[tuple(spot)].set(top_value)


def block_scale(key, extent, cuts, least, largest):
    def one(dim, shards_of):
        draws = jax.random.uniform(jax.random.fold_in(jax.random.fold_in(key, 6), dim), (shards_of,), jnp.float32, least / len(cuts), largest / len(cuts))
        return jnp.repeat(jnp.exp(draws), extent[dim] // shards_of).reshape((-1,) + (1,) * (len(extent) - dim - 1))

    loudness = one(*cuts[0])
    for cut in cuts[1:]:
        loudness = loudness * one(*cut)
    return loudness


def normal_values(stream_key, shape, width, limit, cuts=(), held_as=jnp.bfloat16):
    array = jax.random.normal(stream_key, shape, jnp.float32) * width
    if len(cuts) > 0:
        array = block_scale(stream_key, shape, cuts, -0.22, 0.18) * array
    return jnp.clip(array, min=-limit, max=limit).astype(held_as)


def setup_inputs(seed: int = 0) -> dict:
    key_list = jax.random.split(jax.random.key(seed), 8)
    features = draw_features(jax.random.fold_in(key_list[7], 71), 0)
    frame_start = plant(jax.random.randint(key_list[1], (UTTS,), 0, TOK_DEV - TMASK + 1), jax.random.fold_in(key_list[1], 1), 0, TOK_DEV - TMASK).astype(jnp.int32)
    chan_start = plant(jax.random.randint(key_list[2], (UTTS,), 0, D - FMASK + 1), jax.random.fold_in(key_list[2], 1), 0, D - FMASK).astype(jnp.int32)
    master_weight = normal_values(key_list[3], (D, FF), D ** -0.5, 0.15625, ((0, 64), (1, 8)), jnp.float32)
    row_moment = jnp.clip(jnp.exp(math.log(3.0) - 3.4011974 * jax.random.uniform(key_list[4], (D,), jnp.float32) ** block_scale(key_list[4], (D,), ((0, 64),), -0.2, 0.2)), 0.1, 3.0)
    col_moment = jnp.clip(jnp.exp(math.log(3.0) - 3.4011974 * jax.random.uniform(key_list[5], (FF,), jnp.float32) ** block_scale(key_list[5], (FF,), ((0, 8),), -0.2, 0.2)), 0.1, 3.0)
    out_grad = draw_out_grad(jax.random.fold_in(key_list[7], 71), 0)
    return dict(features=features, frame_start=frame_start, chan_start=chan_start, master_weight=master_weight, row_moment=row_moment, col_moment=col_moment, out_grad=out_grad)


epsilon = 1e-06
decay_rate = 0.8
step_rate = 0.01

def reference(features, frame_start, chan_start, master_weight, row_moment, col_moment, out_grad):
    frames = jnp.arange(TOKENS, dtype=jnp.int32)
    utterance = frames // TOK_DEV
    offset = frames - utterance * TOK_DEV
    first_frame = frame_start[utterance]
    time_keep = (offset < first_frame) | (offset >= first_frame + TMASK)
    channel = jnp.arange(D, dtype=jnp.int32)[None, :]
    first_chan = chan_start[utterance][:, None]
    chan_keep = (channel < first_chan) | (channel >= first_chan + FMASK)
    keeper = time_keep[:, None] & chan_keep
    masked = jnp.where(keeper, features, jnp.zeros_like(features))
    weight_low = master_weight.astype(jnp.bfloat16)
    pre = jnp.dot(masked, weight_low, preferred_element_type=jnp.float32)
    sigmoid_pre = jax.nn.sigmoid(pre)
    slope = sigmoid_pre + pre * sigmoid_pre * (1.0 - sigmoid_pre)
    dpre = (out_grad.astype(jnp.float32) * slope).astype(jnp.bfloat16)
    grad = lax.dot_general(masked, dpre, (((0,), (0,)), ((), ())), preferred_element_type=jnp.float32)
    squared = grad * grad
    total = jnp.sum(squared)
    clip = 1.0 / jnp.maximum(1.0, jnp.sqrt(total / (D * FF)))
    row_stat = clip * clip * lax.optimization_barrier(jnp.sum(squared, axis=1)) / FF + epsilon
    col_stat = clip * clip * lax.optimization_barrier(jnp.sum(squared, axis=0)) / D + epsilon
    row_state = decay_rate * row_moment + (1.0 - decay_rate) * row_stat
    col_state = decay_rate * col_moment + (1.0 - decay_rate) * col_stat
    row_mean = jnp.mean(row_state)
    update = clip * grad * lax.rsqrt(row_state[:, None] * col_state[None, :] / row_mean)
    new_master = master_weight - step_rate * update
    return (new_master, row_state, col_state, new_master.astype(jnp.bfloat16))
```

```python
import functools

import jax
import jax.numpy as jnp
from jax import lax
from jax.experimental import pallas as pl
from jax.experimental.pallas import tpu as pltpu
from jax.sharding import PartitionSpec as P

D = 1536
FF = 6144
TMASK = 128
FMASK = 192
NX = 4
NZ = 16
NMP = 8
TOK = 512
ROWS = D // (NX * NZ)
COLS = FF // NMP
HALF = COLS // 2
BLOCK = ROWS * NZ

epsilon = 1e-06
decay_rate = 0.8
step_rate = 0.01

MESH = pl.DeviceIdType.MESH
F32 = jnp.float32
BF16 = jnp.bfloat16


def fold(rows):
    return jnp.concatenate([rows[:, :HALF], rows[:, HALF:]], axis=0)


class Gather:
    def __init__(self, buf, send_sem, recv_sem, x, z, mp):
        self.buf, self.send_sem, self.recv_sem = buf, send_sem, recv_sem
        self.x, self.z, self.mp = x, z, mp

    def copy(self, slot, k, x, z):
        return pltpu.make_async_remote_copy(
            src_ref=self.buf.at[slot],
            dst_ref=self.buf.at[slot],
            send_sem=self.send_sem.at[k],
            recv_sem=self.recv_sem.at[slot],
            device_id=(x * NZ + z, self.mp),
            device_id_type=MESH,
        )

    def slot(self, offset):
        return self.x * NZ + (self.z + offset) % NZ

    def arrived(self, slot):
        self.copy(slot, 0, self.x, self.z).wait_recv()

    def along_x(self, slot, k):
        for d in (1, 3, 2):
            self.copy(slot, k + d - 1, (self.x + d) % NX, self.z).start()

    def near(self, slot, k):
        for i, d in enumerate((2, 1, NZ - 1)):
            self.copy(slot, k + i, self.x, (self.z + d) % NZ).start()

    def start(self):
        own = self.slot(0)
        for i, d in enumerate((8, 4, 12)):
            self.copy(own, i, self.x, (self.z + d) % NZ).start()
        self.near(own, 3)
        self.along_x(own, 15)

    def forward(self):
        for i, d in enumerate((4, 12, 8)):
            slot = self.slot(d)
            self.arrived(slot)
            self.near(slot, 6 + 3 * i)
            self.along_x(slot, 18 + 3 * i)

        def step(t, _):
            far, m = t // 3, t % 3
            offset = 4 * far + 2 * m - 1 - 5 * (m // 2) + NZ
            slot = self.slot(offset)
            self.arrived(slot)
            self.along_x(slot, 27 + 3 * t)
            return 0

        lax.fori_loop(0, 12, step, 0)

    def wait_block(self, x):
        def step(i, _):
            self.arrived(x * NZ + i)
            return 0

        lax.fori_loop(0, NZ, step, 0)

    def finish(self):
        def step(k, _):
            self.copy(0, k, self.x, self.z).wait_send()
            return 0

        lax.fori_loop(0, NX * NZ - 1, step, 0)


def unfold_block(buf, out, x):
    def step(i, _):
        first = buf[x * NZ + 2 * i].astype(F32)
        second = buf[x * NZ + 2 * i + 1].astype(F32)
        rows = pl.ds(pl.multiple_of(x * BLOCK + i * 2 * ROWS, 2 * ROWS), 2 * ROWS)
        out[rows, :HALF] = jnp.concatenate([first[:ROWS], second[:ROWS]], axis=0).astype(BF16)
        out[rows, HALF:] = jnp.concatenate([first[ROWS:], second[ROWS:]], axis=0).astype(BF16)
        return 0

    lax.fori_loop(0, NZ // 2, step, 0)


def exchange(src, dst, send_sem, recv_sem, peers):
    copies = []
    for i, (to, send_at) in enumerate(peers):
        copies.append(
            pltpu.make_async_remote_copy(
                src_ref=src,
                dst_ref=dst.at[i],
                send_sem=send_sem.at[send_at],
                recv_sem=recv_sem.at[send_at],
                device_id=to,
                device_id_type=MESH,
            )
        )
    for copy in copies:
        copy.start()
    for copy in copies:
        copy.wait()


def kernel(
    frame_ref, chan_ref, feat_ref, master_ref, rmom_ref, cmom_ref, grad_ref,
    new_ref, rstate_ref, cstate_ref, low_ref,
    wbuf, weight, nbuf, masked, masked_t, pre, dpre,
    partial, xrecv, summed, lrecv, local, frecv,
    row_src, row_dst, vec, vec_x, vec_f, vec_l,
    ag_send, ag_recv, ag2_send, ag2_recv, rs_send, rs_recv, sc_send, sc_recv,
):
    dp, mp = lax.axis_index("dp"), lax.axis_index("mp")
    x, z = dp // NZ, dp % NZ

    def at(dx, dz):
        return (((x + dx) % NX) * NZ + (z + dz) % NZ, mp)

    x_peers = [at(d, 0) for d in (1, 2, 3)]
    far_peers = [at(0, d) for d in (4, 8, 12)]
    near_peers = [at(0, d) for d in (1, NZ - 1, 2)]
    mp_peers = [(dp, (mp + d) % NMP) for d in range(1, NMP)]

    own = pl.ds(0, ROWS)
    wbuf[dp] = fold(master_ref[own, :]).astype(BF16)

    barrier = pltpu.get_barrier_semaphore()
    greeted = x_peers + far_peers + near_peers + [at(0, NZ - 2)] + mp_peers
    for peer in greeted:
        pl.semaphore_signal(barrier, inc=1, device_id=peer, device_id_type=MESH)
    pl.semaphore_wait(barrier, len(greeted))

    gather = Gather(wbuf, ag_send, ag_recv, x, z, mp)
    gather.start()

    first_frame, first_chan = frame_ref[0], chan_ref[0]
    channel = lax.broadcasted_iota(jnp.int32, (1, D), 1)
    chan_keep = jnp.where((channel < first_chan) | (channel >= first_chan + FMASK), 1.0, 0.0)

    def mask_rows(i, _):
        rows = pl.ds(pl.multiple_of(i * 128, 128), 128)
        offset = lax.broadcasted_iota(jnp.int32, (128, 1), 0) + i * 128
        time_keep = jnp.where((offset < first_frame) | (offset >= first_frame + TMASK), 1.0, 0.0)
        kept = feat_ref[rows, :] * (time_keep * chan_keep).astype(BF16)
        masked[rows, :] = kept
        masked_t[:, rows] = kept.T
        return 0

    lax.fori_loop(0, TOK // 128, mask_rows, 0)

    gather.forward()

    for d in (0, 1, 3, 2):
        block = (x + d) % NX
        if d:
            gather.wait_block(block)
        unfold_block(wbuf, weight, block)
        depth = pl.ds(pl.multiple_of(block * BLOCK, BLOCK), BLOCK)

        def forward_tile(i, _, d=d, depth=depth):
            cols = pl.ds(pl.multiple_of(i * 256, 256), 256)
            term = jnp.dot(masked[:, depth], weight[depth, cols], preferred_element_type=F32)
            if d == 0:
                pre[:, cols] = term
            else:
                total = pre[:, cols] + term
                if d != 2:
                    pre[:, cols] = total
                else:
                    s = jax.nn.sigmoid(total)
                    slope = s + total * s * (1.0 - s)
                    dpre[:, cols] = (grad_ref[:, cols].astype(F32) * slope).astype(BF16)
            return 0

        lax.fori_loop(0, COLS // 256, forward_tile, 0)

    def x_copy(d, cls):
        i = (d - 1) * 4 + cls
        return pltpu.make_async_remote_copy(
            src_ref=partial.at[d, cls],
            dst_ref=xrecv.at[d - 1, cls],
            send_sem=rs_send.at[i],
            recv_sem=rs_recv.at[i],
            device_id=at(d, 0),
            device_id_type=MESH,
        )

    classes = [(z + d) % 4 for d in (2, 1, 3, 0)]
    for d in (2, 1, 3, 0):
        block = (x + d) % NX

        def grad_tile(i, _, d=d, block=block):
            rows = pl.ds(pl.multiple_of(block * BLOCK + i * 4 * ROWS, 32), 4 * ROWS)
            term = jnp.dot(masked_t[rows, :], dpre[...], preferred_element_type=F32)
            for j in range(4):
                partial[d, j, i] = term[j * ROWS : (j + 1) * ROWS]
            return 0

        lax.fori_loop(0, NZ // 4, grad_tile, 0)
        if d:
            for cls in classes:
                x_copy(d, cls).start()

    def near_copy(i):
        return pltpu.make_async_remote_copy(
            src_ref=summed.at[(near_peers[i][0]) % 4],
            dst_ref=lrecv.at[i],
            send_sem=rs_send.at[12 + i],
            recv_sem=rs_recv.at[12 + i],
            device_id=near_peers[i],
            device_id_type=MESH,
        )

    for n, cls in enumerate(classes):
        for d in (1, 3, 2):
            x_copy(d, cls).wait_recv()

        def add_x(j, _, cls=cls):
            summed[cls, j] = partial[0, cls, j] + xrecv[0, cls, j] + xrecv[1, cls, j] + xrecv[2, cls, j]
            return 0

        lax.fori_loop(0, 4, add_x, 0)
        if n < 3:
            near_copy((2, 0, 1)[n]).start()

    for i in (0, 1, 2):
        near_copy(i).wait_recv()
    mine = z % 4

    def far_copy(i):
        return pltpu.make_async_remote_copy(
            src_ref=local.at[(z // 4 + i + 1) % 4],
            dst_ref=frecv.at[i],
            send_sem=rs_send.at[15 + i],
            recv_sem=rs_recv.at[15 + i],
            device_id=far_peers[i],
            device_id_type=MESH,
        )

    for d in (2, 1, 3, 0):
        j = (z // 4 + d) % 4
        local[j] = summed[mine, j] + lrecv[0, j] + lrecv[1, j] + lrecv[2, j]
        if d:
            far_copy(d - 1).start()
    for i in (0, 1, 2):
        far_copy(i).wait_recv()
    grad = local[z // 4] + frecv[0] + frecv[1] + frecv[2]

    squared = grad * grad
    row_lanes = squared[:, :128]
    for i in range(1, COLS // 128):
        row_lanes = row_lanes + squared[:, i * 128 : (i + 1) * 128]
    row_src[...] = row_lanes
    exchange(row_src, row_dst, sc_send, sc_recv, [(p, i) for i, p in enumerate(mp_peers)])
    for i in range(NMP - 1):
        row_lanes = row_lanes + row_dst[i]
    row_total = jnp.sum(row_lanes, axis=1, keepdims=True)

    diag = lax.broadcasted_iota(jnp.int32, (ROWS, ROWS), 0) == lax.broadcasted_iota(jnp.int32, (ROWS, ROWS), 1)
    moment = jnp.sum(jnp.where(diag, rmom_ref[...], 0.0), axis=1, keepdims=True)
    column = jnp.sum(squared, axis=0, keepdims=True)
    pieces = [column[:, i * 128 : (i + 1) * 128] for i in range(COLS // 128)]
    pieces.append(jnp.sum(row_lanes, axis=0, keepdims=True))
    pieces.append(jnp.broadcast_to(jnp.sum(moment, axis=0, keepdims=True) * (1.0 / 128), (1, 128)))
    vec[0] = jnp.concatenate(pieces, axis=0)
    exchange(vec.at[0], vec_x, sc_send, sc_recv, [(p, 7 + i) for i, p in enumerate(x_peers)])
    vec[1] = vec[0] + vec_x[0] + vec_x[1] + vec_x[2]
    exchange(vec.at[1], vec_f, sc_send, sc_recv, [(p, 10 + i) for i, p in enumerate(far_peers)])
    vec[2] = vec[1] + vec_f[0] + vec_f[1] + vec_f[2]
    exchange(vec.at[2], vec_l, sc_send, sc_recv, [(p, 13 + i) for i, p in enumerate(near_peers)])
    sums = vec[2] + vec_l[0] + vec_l[1] + vec_l[2]
    col_total = jnp.concatenate([sums[i : i + 1] for i in range(COLS // 128)], axis=1)
    total = jnp.sum(sums[6:7], axis=1, keepdims=True)
    moments = jnp.sum(sums[7:8], axis=1, keepdims=True)

    clip = 1.0 / jnp.maximum(1.0, jnp.sqrt(total / (D * FF)))
    row_state = decay_rate * moment + (1.0 - decay_rate) * (clip * clip * row_total / FF + epsilon)
    col_state = decay_rate * cmom_ref[...] + (1.0 - decay_rate) * (clip * clip * col_total / D + epsilon)
    row_mean = decay_rate * moments / D + (1.0 - decay_rate) * (clip * clip * (total / FF) / D + epsilon)
    update = clip * grad * lax.rsqrt(row_state * col_state / row_mean)
    updated = master_ref[...] - step_rate * update
    nbuf[dp] = fold(updated).astype(BF16)

    regather = Gather(nbuf, ag2_send, ag2_recv, x, z, mp)
    regather.start()
    new_ref[...] = updated
    rstate_ref[...] = jnp.sum(jnp.where(diag, row_state, 0.0), axis=0, keepdims=True)
    cstate_ref[...] = col_state
    regather.forward()
    for d in (0, 1, 3, 2):
        block = (x + d) % NX
        if d:
            regather.wait_block(block)
        unfold_block(nbuf, low_ref, block)

    gather.finish()
    regather.finish()
    for d in (1, 2, 3):
        for cls in range(4):
            x_copy(d, cls).wait_send()
    for i in range(3):
        near_copy(i).wait_send()
        far_copy(i).wait_send()


def per_device(features, frame_start, chan_start, master_weight, row_moment, col_moment, out_grad):
    vmem = pl.BlockSpec(memory_space=pltpu.VMEM)
    smem = pl.BlockSpec(memory_space=pltpu.SMEM)
    new_master, row_state, col_state, compute_weight = pl.pallas_call(
        kernel,
        name="adafactor_step",
        out_shape=(
            jax.ShapeDtypeStruct((ROWS, COLS), F32),
            jax.ShapeDtypeStruct((1, ROWS), F32),
            jax.ShapeDtypeStruct((1, COLS), F32),
            jax.ShapeDtypeStruct((D, COLS), BF16),
        ),
        in_specs=[smem, smem, vmem, vmem, vmem, vmem, vmem],
        out_specs=(vmem, vmem, vmem, vmem),
        scratch_shapes=[
            pltpu.VMEM((NX * NZ, 2 * ROWS, HALF), BF16),
            pltpu.VMEM((D, COLS), BF16),
            pltpu.VMEM((NX * NZ, 2 * ROWS, HALF), BF16),
            pltpu.VMEM((TOK, D), BF16),
            pltpu.VMEM((D, TOK), BF16),
            pltpu.VMEM((TOK, COLS), F32),
            pltpu.VMEM((TOK, COLS), BF16),
            pltpu.VMEM((NX, 4, 4, ROWS, COLS), F32),
            pltpu.VMEM((NX - 1, 4, 4, ROWS, COLS), F32),
            pltpu.VMEM((4, 4, ROWS, COLS), F32),
            pltpu.VMEM((3, 4, ROWS, COLS), F32),
            pltpu.VMEM((4, ROWS, COLS), F32),
            pltpu.VMEM((3, ROWS, COLS), F32),
            pltpu.VMEM((ROWS, 128), F32),
            pltpu.VMEM((NMP - 1, ROWS, 128), F32),
            pltpu.VMEM((3, 8, 128), F32),
            pltpu.VMEM((3, 8, 128), F32),
            pltpu.VMEM((3, 8, 128), F32),
            pltpu.VMEM((3, 8, 128), F32),
            pltpu.SemaphoreType.DMA((NX * NZ,)),
            pltpu.SemaphoreType.DMA((NX * NZ,)),
            pltpu.SemaphoreType.DMA((NX * NZ,)),
            pltpu.SemaphoreType.DMA((NX * NZ,)),
            pltpu.SemaphoreType.DMA((18,)),
            pltpu.SemaphoreType.DMA((18,)),
            pltpu.SemaphoreType.DMA((16,)),
            pltpu.SemaphoreType.DMA((16,)),
        ],
        compiler_params=pltpu.CompilerParams(collective_id=0, has_side_effects=True, vmem_limit_bytes=56 * 2**20),
    )(
        frame_start, chan_start, features, master_weight, row_moment.reshape(1, ROWS), col_moment.reshape(1, COLS), out_grad
    )
    return new_master, row_state.reshape(ROWS), col_state.reshape(COLS), compute_weight


def solution(mesh):
    placed = (P("dp", None), P("dp"), P("dp"), P("dp", "mp"), P("dp"), P("mp"), P("dp", "mp"))
    return jax.shard_map(
        per_device,
        mesh=mesh,
        in_specs=placed,
        out_specs=(P("dp", "mp"), P("dp"), P("mp"), P(None, "mp")),
        check_vma=False,
    )
```

```python
import functools

import jax
import jax.numpy as jnp
from jax import lax
from jax.experimental import pallas as pl
from jax.experimental.pallas import tpu as pltpu
from jax.sharding import PartitionSpec as P

D = 1536
FF = 6144
TMASK = 128
FMASK = 192
NX = 4
NZ = 16
NMP = 8
TOK = 512
ROWS = D // (NX * NZ)
COLS = FF // NMP
HALF = COLS // 2
BLOCK = ROWS * NZ

epsilon = 1e-06
decay_rate = 0.8
step_rate = 0.01

MESH = pl.DeviceIdType.MESH
F32 = jnp.float32
BF16 = jnp.bfloat16
I16 = jnp.int16


def fold(rows):
    return jnp.concatenate([rows[:, :HALF], rows[:, HALF:]], axis=0)


class Gather:
    def __init__(self, buf, send_sem, recv_sem, x, z, mp):
        self.buf, self.send_sem, self.recv_sem = buf, send_sem, recv_sem
        self.x, self.z, self.mp = x, z, mp

    def copy(self, slot, k, x, z):
        return pltpu.make_async_remote_copy(
            src_ref=self.buf.at[slot],
            dst_ref=self.buf.at[slot],
            send_sem=self.send_sem.at[k],
            recv_sem=self.recv_sem.at[slot],
            device_id=(x * NZ + z, self.mp),
            device_id_type=MESH,
        )

    def slot(self, offset):
        return self.x * NZ + (self.z + offset) % NZ

    def arrived(self, slot):
        self.copy(slot, 0, self.x, self.z).wait_recv()

    def along_x(self, slot, k):
        for i, d in enumerate((1, NX - 1)):
            self.copy(slot, k + i, (self.x + d) % NX, self.z).start()

    def near(self, slot, k):
        for i, d in enumerate((2, 1, NZ - 1)):
            self.copy(slot, k + i, self.x, (self.z + d) % NZ).start()

    def start(self):
        own = self.slot(0)
        for i, d in enumerate((8, 4, 12)):
            self.copy(own, i, self.x, (self.z + d) % NZ).start()
        self.near(own, 3)
        self.along_x(own, 15)

    def forward(self):
        for i, d in enumerate((4, 12, 8)):
            slot = self.slot(d)
            self.arrived(slot)
            self.near(slot, 6 + 3 * i)
            self.along_x(slot, 17 + 2 * i)

        def step(t, _):
            far, m = t // 3, t % 3
            offset = 4 * far + 2 * m - 1 - 5 * (m // 2) + NZ
            slot = self.slot(offset)
            self.arrived(slot)
            self.along_x(slot, 23 + 2 * t)
            return 0

        lax.fori_loop(0, 12, step, 0)

        def relay(t, _):
            far, n = t // 4, t % 4
            owner = (self.z + 4 * far + (n // 2) * (1 - n % 2) - ((n + 1) // 2) * (n % 2) + NZ) % NZ
            side = 1 - 2 * (owner % 2)
            slot = ((self.x - side + NX) % NX) * NZ + owner
            self.arrived(slot)
            self.copy(slot, 47 + t, (self.x + side + NX) % NX, self.z).start()
            return 0

        lax.fori_loop(0, NZ, relay, 0)

    def wait_block(self, d):
        x = (self.x + d) % NX

        def step(i, _):
            if d == 2:
                owner = i
            else:
                owner = 2 * i + (0 if d == 1 else 1)
            self.arrived(x * NZ + owner)
            return 0

        lax.fori_loop(0, NZ if d == 2 else NZ // 2, step, 0)

    def finish(self):
        def step(k, _):
            self.copy(0, k, self.x, self.z).wait_send()
            return 0

        lax.fori_loop(0, NX * NZ - 1, step, 0)


def unfold_block(buf, out, x):
    def step(i, _):
        first = buf[x * NZ + 2 * i].astype(F32)
        second = buf[x * NZ + 2 * i + 1].astype(F32)
        rows = pl.ds(pl.multiple_of(x * BLOCK + i * 2 * ROWS, 2 * ROWS), 2 * ROWS)
        out[rows, :HALF] = jnp.concatenate([first[:ROWS], second[:ROWS]], axis=0).astype(BF16)
        out[rows, HALF:] = jnp.concatenate([first[ROWS:], second[ROWS:]], axis=0).astype(BF16)
        return 0

    lax.fori_loop(0, NZ // 2, step, 0)


def unfold(slot):
    return jnp.concatenate([slot[:ROWS], slot[ROWS:]], axis=1)


def pack(row):
    pieces = [row[:, i * 128 : (i + 1) * 128] for i in range(COLS // 128)]
    return jnp.concatenate(pieces + [jnp.zeros((8 - COLS // 128, 128), F32)], axis=0)


def unpack(tile):
    return jnp.concatenate([tile[i : i + 1] for i in range(COLS // 128)], axis=1)


def peak_of(rows):
    size = jnp.abs(rows)
    return jnp.maximum(jnp.maximum(size[:8], size[8:16]), size[16:24])


def scale_of(peak):
    return jnp.maximum(jnp.max(peak, axis=0, keepdims=True), 1e-30)


def encode(rows, inverse):
    return jnp.round(fold(rows * inverse)).astype(jnp.int32).astype(I16)


def decode(slot, scale):
    return unfold(slot.astype(jnp.int32).astype(F32)) * scale


def exchange(src, dst, send_sem, recv_sem, peers):
    copies = []
    for i, (to, send_at) in enumerate(peers):
        copies.append(
            pltpu.make_async_remote_copy(
                src_ref=src,
                dst_ref=dst.at[i],
                send_sem=send_sem.at[send_at],
                recv_sem=recv_sem.at[send_at],
                device_id=to,
                device_id_type=MESH,
            )
        )
    for copy in copies:
        copy.start()
    for copy in copies:
        copy.wait()


def kernel(
    frame_ref, chan_ref, feat_ref, master_ref, rmom_ref, cmom_ref, grad_ref,
    new_ref, rstate_ref, cstate_ref, low_ref,
    wbuf, weight, nbuf, masked, masked_t, pre, dpre,
    partial, coded, xrecv, summed, near_coded, lrecv, far_coded, frecv, scale_src, scale_dst,
    row_src, row_dst, vec, vec_x, vec_f, vec_l,
    ag_send, ag_recv, ag2_send, ag2_recv, rs_send, rs_recv, sc_send, sc_recv,
):
    dp, mp = lax.axis_index("dp"), lax.axis_index("mp")
    x, z = dp // NZ, dp % NZ

    def at(dx, dz):
        return (((x + dx) % NX) * NZ + (z + dz) % NZ, mp)

    x_peers = [at(d, 0) for d in (1, 2, 3)]
    far_peers = [at(0, d) for d in (4, 8, 12)]
    near_peers = [at(0, d) for d in (1, NZ - 1, 2)]
    mp_peers = [(dp, (mp + d) % NMP) for d in range(1, NMP)]

    own = pl.ds(0, ROWS)
    wbuf[dp] = fold(master_ref[own, :]).astype(BF16)

    barrier = pltpu.get_barrier_semaphore()
    greeted = x_peers + far_peers + near_peers + [at(0, NZ - 2)] + mp_peers
    for peer in greeted:
        pl.semaphore_signal(barrier, inc=1, device_id=peer, device_id_type=MESH)
    pl.semaphore_wait(barrier, len(greeted))

    gather = Gather(wbuf, ag_send, ag_recv, x, z, mp)
    gather.start()

    first_frame, first_chan = frame_ref[0], chan_ref[0]
    channel = lax.broadcasted_iota(jnp.int32, (1, D), 1)
    chan_keep = jnp.where((channel < first_chan) | (channel >= first_chan + FMASK), 1.0, 0.0)

    def mask_rows(i, _):
        rows = pl.ds(pl.multiple_of(i * 128, 128), 128)
        offset = lax.broadcasted_iota(jnp.int32, (128, 1), 0) + i * 128
        time_keep = jnp.where((offset < first_frame) | (offset >= first_frame + TMASK), 1.0, 0.0)
        kept = feat_ref[rows, :] * (time_keep * chan_keep).astype(BF16)
        masked[rows, :] = kept
        masked_t[:, rows] = kept.T
        return 0

    lax.fori_loop(0, TOK // 128, mask_rows, 0)

    gather.forward()

    for d in (0, 1, 3, 2):
        block = (x + d) % NX
        if d:
            gather.wait_block(d)
        unfold_block(wbuf, weight, block)
        depth = pl.ds(pl.multiple_of(block * BLOCK, BLOCK), BLOCK)

        def forward_tile(i, _, d=d, depth=depth):
            cols = pl.ds(pl.multiple_of(i * 256, 256), 256)
            term = jnp.dot(masked[:, depth], weight[depth, cols], preferred_element_type=F32)
            if d == 0:
                pre[:, cols] = term
            else:
                total = pre[:, cols] + term
                if d != 2:
                    pre[:, cols] = total
                else:
                    s = jax.nn.sigmoid(total)
                    slope = s + total * s * (1.0 - s)
                    dpre[:, cols] = (grad_ref[:, cols].astype(F32) * slope).astype(BF16)
            return 0

        lax.fori_loop(0, COLS // 256, forward_tile, 0)

    def remote(src, dst, i, to):
        return pltpu.make_async_remote_copy(
            src_ref=src,
            dst_ref=dst,
            send_sem=rs_send.at[i],
            recv_sem=rs_recv.at[i],
            device_id=to,
            device_id_type=MESH,
        )

    def x_copy(d, cls):
        return remote(coded.at[d - 1, cls], xrecv.at[d - 1, cls], (d - 1) * 4 + cls, at(d, 0))

    def x_scale(d):
        return remote(scale_src.at[d - 1], scale_dst.at[d - 1], 12 + d - 1, at(d, 0))

    def near_copy(i):
        return remote(near_coded.at[i], lrecv.at[i], 15 + i, near_peers[i])

    def near_scale(i):
        return remote(scale_src.at[3 + i], scale_dst.at[3 + i], 18 + i, near_peers[i])

    def far_copy(i):
        return remote(far_coded.at[i], frecv.at[i], 21 + i, far_peers[i])

    def far_scale(i):
        return remote(scale_src.at[6 + i], scale_dst.at[6 + i], 24 + i, far_peers[i])

    classes = [(z + d) % 4 for d in (2, 1, 3, 0)]
    for d in (2, 1, 3, 0):
        block = (x + d) % NX
        held = 0 if d == 0 else 1

        def grad_tile(i, peak, block=block, held=held):
            rows = pl.ds(pl.multiple_of(block * BLOCK + i * 4 * ROWS, 32), 4 * ROWS)
            term = jnp.dot(masked_t[rows, :], dpre[...], preferred_element_type=F32)
            for j in range(4):
                slot = term[j * ROWS : (j + 1) * ROWS]
                partial[held, j, i] = slot
                peak = jnp.maximum(peak, peak_of(slot))
            return peak

        peak = lax.fori_loop(0, NZ // 4, grad_tile, jnp.zeros((8, COLS), F32))
        if d:
            scale = scale_of(peak)
            scale_src[d - 1] = pack(scale * (1.0 / 32767))
            x_scale(d).start()
            inverse = 32767.0 / scale
            for cls in classes:

                def encode_slot(j, _, d=d, cls=cls, inverse=inverse):
                    coded[d - 1, cls, j] = encode(partial[1, cls, j], inverse)
                    return 0

                lax.fori_loop(0, 4, encode_slot, 0)
                x_copy(d, cls).start()

    for d in (1, 2, 3):
        x_scale(d).wait_recv()
    scales = [unpack(scale_dst[i]) for i in range(3)]
    for n, cls in enumerate(classes):
        for d in (2, 1, 3):
            x_copy(d, cls).wait_recv()

        def add_x(j, peak, cls=cls):
            term = partial[0, cls, j]
            for i in range(3):
                term = term + decode(xrecv[i, cls, j], scales[i])
            summed[j] = term
            return jnp.maximum(peak, peak_of(term))

        peak = lax.fori_loop(0, 4, add_x, jnp.zeros((8, COLS), F32))
        if n < 3:
            i = (2, 0, 1)[n]
            scale = scale_of(peak)
            scale_src[3 + i] = pack(scale * (1.0 / 32767))
            near_scale(i).start()
            inverse = 32767.0 / scale

            def encode_near(j, _, i=i, inverse=inverse):
                near_coded[i, j] = encode(summed[j], inverse)
                return 0

            lax.fori_loop(0, 4, encode_near, 0)
            near_copy(i).start()

    for i in range(3):
        near_scale(i).wait_recv()
    scales = [unpack(scale_dst[3 + i]) for i in range(3)]
    for i in (0, 1, 2):
        near_copy(i).wait_recv()
    for d in (2, 1, 3, 0):
        j = (z // 4 + d) % 4
        grad = summed[j]
        for i in range(3):
            grad = grad + decode(lrecv[i, j], scales[i])
        if d:
            scale = scale_of(peak_of(grad))
            scale_src[6 + d - 1] = pack(scale * (1.0 / 32767))
            far_scale(d - 1).start()
            far_coded[d - 1] = encode(grad, 32767.0 / scale)
            far_copy(d - 1).start()
    for i in range(3):
        far_scale(i).wait_recv()
        far_copy(i).wait_recv()
        grad = grad + decode(frecv[i], unpack(scale_dst[6 + i]))

    squared = grad * grad
    row_lanes = squared[:, :128]
    for i in range(1, COLS // 128):
        row_lanes = row_lanes + squared[:, i * 128 : (i + 1) * 128]
    row_src[...] = row_lanes
    exchange(row_src, row_dst, sc_send, sc_recv, [(p, i) for i, p in enumerate(mp_peers)])
    for i in range(NMP - 1):
        row_lanes = row_lanes + row_dst[i]
    row_total = jnp.sum(row_lanes, axis=1, keepdims=True)

    diag = lax.broadcasted_iota(jnp.int32, (ROWS, ROWS), 0) == lax.broadcasted_iota(jnp.int32, (ROWS, ROWS), 1)
    moment = jnp.sum(jnp.where(diag, rmom_ref[...], 0.0), axis=1, keepdims=True)
    column = jnp.sum(squared, axis=0, keepdims=True)
    pieces = [column[:, i * 128 : (i + 1) * 128] for i in range(COLS // 128)]
    pieces.append(jnp.sum(row_lanes, axis=0, keepdims=True))
    pieces.append(jnp.broadcast_to(jnp.sum(moment, axis=0, keepdims=True) * (1.0 / 128), (1, 128)))
    vec[0] = jnp.concatenate(pieces, axis=0)
    exchange(vec.at[0], vec_x, sc_send, sc_recv, [(p, 7 + i) for i, p in enumerate(x_peers)])
    vec[1] = vec[0] + vec_x[0] + vec_x[1] + vec_x[2]
    exchange(vec.at[1], vec_f, sc_send, sc_recv, [(p, 10 + i) for i, p in enumerate(far_peers)])
    vec[2] = vec[1] + vec_f[0] + vec_f[1] + vec_f[2]
    exchange(vec.at[2], vec_l, sc_send, sc_recv, [(p, 13 + i) for i, p in enumerate(near_peers)])
    sums = vec[2] + vec_l[0] + vec_l[1] + vec_l[2]
    col_total = unpack(sums)
    total = jnp.sum(sums[6:7], axis=1, keepdims=True)
    moments = jnp.sum(sums[7:8], axis=1, keepdims=True)

    clip = 1.0 / jnp.maximum(1.0, jnp.sqrt(total / (D * FF)))
    row_state = decay_rate * moment + (1.0 - decay_rate) * (clip * clip * row_total / FF + epsilon)
    col_state = decay_rate * cmom_ref[...] + (1.0 - decay_rate) * (clip * clip * col_total / D + epsilon)
    row_mean = decay_rate * moments / D + (1.0 - decay_rate) * (clip * clip * (total / FF) / D + epsilon)
    update = clip * grad * lax.rsqrt(row_state * col_state / row_mean)
    updated = master_ref[...] - step_rate * update
    nbuf[dp] = fold(updated).astype(BF16)

    regather = Gather(nbuf, ag2_send, ag2_recv, x, z, mp)
    regather.start()
    new_ref[...] = updated
    rstate_ref[...] = jnp.sum(jnp.where(diag, row_state, 0.0), axis=0, keepdims=True)
    cstate_ref[...] = col_state
    regather.forward()
    for d in (0, 1, 3, 2):
        block = (x + d) % NX
        if d:
            regather.wait_block(d)
        unfold_block(nbuf, low_ref, block)

    gather.finish()
    regather.finish()
    for d in (1, 2, 3):
        x_scale(d).wait_send()
        for cls in range(4):
            x_copy(d, cls).wait_send()
    for i in range(3):
        near_scale(i).wait_send()
        near_copy(i).wait_send()
        far_scale(i).wait_send()
        far_copy(i).wait_send()


def per_device(features, frame_start, chan_start, master_weight, row_moment, col_moment, out_grad):
    vmem = pl.BlockSpec(memory_space=pltpu.VMEM)
    smem = pl.BlockSpec(memory_space=pltpu.SMEM)
    new_master, row_state, col_state, compute_weight = pl.pallas_call(
        kernel,
        name="adafactor_step",
        out_shape=(
            jax.ShapeDtypeStruct((ROWS, COLS), F32),
            jax.ShapeDtypeStruct((1, ROWS), F32),
            jax.ShapeDtypeStruct((1, COLS), F32),
            jax.ShapeDtypeStruct((D, COLS), BF16),
        ),
        in_specs=[smem, smem, vmem, vmem, vmem, vmem, vmem],
        out_specs=(vmem, vmem, vmem, vmem),
        scratch_shapes=[
            pltpu.VMEM((NX * NZ, 2 * ROWS, HALF), BF16),
            pltpu.VMEM((D, COLS), BF16),
            pltpu.VMEM((NX * NZ, 2 * ROWS, HALF), BF16),
            pltpu.VMEM((TOK, D), BF16),
            pltpu.VMEM((D, TOK), BF16),
            pltpu.VMEM((TOK, COLS), F32),
            pltpu.VMEM((TOK, COLS), BF16),
            pltpu.VMEM((2, 4, 4, ROWS, COLS), F32),
            pltpu.VMEM((NX - 1, 4, 4, 2 * ROWS, HALF), I16),
            pltpu.VMEM((NX - 1, 4, 4, 2 * ROWS, HALF), I16),
            pltpu.VMEM((4, ROWS, COLS), F32),
            pltpu.VMEM((3, 4, 2 * ROWS, HALF), I16),
            pltpu.VMEM((3, 4, 2 * ROWS, HALF), I16),
            pltpu.VMEM((3, 2 * ROWS, HALF), I16),
            pltpu.VMEM((3, 2 * ROWS, HALF), I16),
            pltpu.VMEM((9, 8, 128), F32),
            pltpu.VMEM((9, 8, 128), F32),
            pltpu.VMEM((ROWS, 128), F32),
            pltpu.VMEM((NMP - 1, ROWS, 128), F32),
            pltpu.VMEM((3, 8, 128), F32),
            pltpu.VMEM((3, 8, 128), F32),
            pltpu.VMEM((3, 8, 128), F32),
            pltpu.VMEM((3, 8, 128), F32),
            pltpu.SemaphoreType.DMA((NX * NZ,)),
            pltpu.SemaphoreType.DMA((NX * NZ,)),
            pltpu.SemaphoreType.DMA((NX * NZ,)),
            pltpu.SemaphoreType.DMA((NX * NZ,)),
            pltpu.SemaphoreType.DMA((27,)),
            pltpu.SemaphoreType.DMA((27,)),
            pltpu.SemaphoreType.DMA((16,)),
            pltpu.SemaphoreType.DMA((16,)),
        ],
        compiler_params=pltpu.CompilerParams(collective_id=0, has_side_effects=True, vmem_limit_bytes=56 * 2**20),
    )(
        frame_start, chan_start, features, master_weight, row_moment.reshape(1, ROWS), col_moment.reshape(1, COLS), out_grad
    )
    return new_master, row_state.reshape(ROWS), col_state.reshape(COLS), compute_weight


def solution(mesh):
    placed = (P("dp", None), P("dp"), P("dp"), P("dp", "mp"), P("dp"), P("mp"), P("dp", "mp"))
    return jax.shard_map(
        per_device,
        mesh=mesh,
        in_specs=placed,
        out_specs=(P("dp", "mp"), P("dp"), P("mp"), P(None, "mp")),
        check_vma=False,
    )
```

```python
import functools

import jax
import jax.numpy as jnp
from jax import lax
from jax.experimental import pallas as pl
from jax.experimental.pallas import tpu as pltpu
from jax.sharding import PartitionSpec as P

D = 1536
FF = 6144
TMASK = 128
FMASK = 192
NX = 4
NZ = 16
NMP = 8
TOK = 512
ROWS = D // (NX * NZ)
COLS = FF // NMP
HALF = COLS // 2
BLOCK = ROWS * NZ

epsilon = 1e-06
decay_rate = 0.8
step_rate = 0.01

MESH = pl.DeviceIdType.MESH
F32 = jnp.float32
BF16 = jnp.bfloat16
I16 = jnp.int16


def fold(rows):
    return jnp.concatenate([rows[:, :HALF], rows[:, HALF:]], axis=0)


class Gather:
    def __init__(self, buf, send_sem, recv_sem, x, z, mp):
        self.buf, self.send_sem, self.recv_sem = buf, send_sem, recv_sem
        self.x, self.z, self.mp = x, z, mp

    def copy(self, slot, k, x, z):
        return pltpu.make_async_remote_copy(
            src_ref=self.buf.at[slot],
            dst_ref=self.buf.at[slot],
            send_sem=self.send_sem.at[k],
            recv_sem=self.recv_sem.at[slot],
            device_id=(x * NZ + z, self.mp),
            device_id_type=MESH,
        )

    def slot(self, offset):
        return self.x * NZ + (self.z + offset) % NZ

    def arrived(self, slot):
        self.copy(slot, 0, self.x, self.z).wait_recv()

    def along_x(self, slot, k):
        for i, d in enumerate((1, NX - 1)):
            self.copy(slot, k + i, (self.x + d) % NX, self.z).start()

    def near(self, slot, k):
        for i, d in enumerate((2, 1, NZ - 1)):
            self.copy(slot, k + i, self.x, (self.z + d) % NZ).start()

    def start(self):
        own = self.slot(0)
        for i, d in enumerate((8, 4, 12)):
            self.copy(own, i, self.x, (self.z + d) % NZ).start()
        self.near(own, 3)
        self.along_x(own, 15)

    def forward(self):
        for i, d in enumerate((4, 12, 8)):
            slot = self.slot(d)
            self.arrived(slot)
            self.near(slot, 6 + 3 * i)
            self.along_x(slot, 17 + 2 * i)

        def step(t, _):
            far, m = t // 3, t % 3
            offset = 4 * far + 2 * m - 1 - 5 * (m // 2) + NZ
            slot = self.slot(offset)
            self.arrived(slot)
            self.along_x(slot, 23 + 2 * t)
            return 0

        lax.fori_loop(0, 12, step, 0)

        def relay(t, _):
            far, n = t // 4, t % 4
            owner = (self.z + 4 * far + (n // 2) * (1 - n % 2) - ((n + 1) // 2) * (n % 2) + NZ) % NZ
            side = 1 - 2 * (owner % 2)
            slot = ((self.x - side + NX) % NX) * NZ + owner
            self.arrived(slot)
            self.copy(slot, 47 + t, (self.x + side + NX) % NX, self.z).start()
            return 0

        lax.fori_loop(0, NZ, relay, 0)

    def wait_block(self, d):
        x = (self.x + d) % NX

        def step(i, _):
            if d == 2:
                owner = i
            else:
                owner = 2 * i + (0 if d == 1 else 1)
            self.arrived(x * NZ + owner)
            return 0

        lax.fori_loop(0, NZ if d == 2 else NZ // 2, step, 0)

    def finish(self):
        def step(k, _):
            self.copy(0, k, self.x, self.z).wait_send()
            return 0

        lax.fori_loop(0, NX * NZ - 1, step, 0)


def unfold_block(buf, out, x):
    def step(i, _):
        first = buf[x * NZ + 2 * i].astype(F32)
        second = buf[x * NZ + 2 * i + 1].astype(F32)
        rows = pl.ds(pl.multiple_of(x * BLOCK + i * 2 * ROWS, 2 * ROWS), 2 * ROWS)
        out[rows, :HALF] = jnp.concatenate([first[:ROWS], second[:ROWS]], axis=0).astype(BF16)
        out[rows, HALF:] = jnp.concatenate([first[ROWS:], second[ROWS:]], axis=0).astype(BF16)
        return 0

    lax.fori_loop(0, NZ // 2, step, 0)


def unfold(slot):
    return jnp.concatenate([slot[:ROWS], slot[ROWS:]], axis=1)


def pack(row):
    pieces = [row[:, i * 128 : (i + 1) * 128] for i in range(COLS // 128)]
    return jnp.concatenate(pieces + [jnp.zeros((8 - COLS // 128, 128), F32)], axis=0)


def unpack(tile):
    return jnp.concatenate([tile[i : i + 1] for i in range(COLS // 128)], axis=1)


def peak_of(rows):
    size = jnp.abs(rows)
    return jnp.maximum(jnp.maximum(size[:8], size[8:16]), size[16:24])


def scale_of(peak):
    return jnp.maximum(jnp.max(peak, axis=0, keepdims=True), 1e-30)


def encode(rows, inverse):
    return jnp.round(fold(rows * inverse)).astype(jnp.int32).astype(I16)


def decode(slot, scale):
    return unfold(slot.astype(jnp.int32).astype(F32)) * scale


def kernel(
    frame_ref, chan_ref, feat_hbm, master_ref, rmom_ref, cmom_ref, grad_hbm,
    new_ref, rstate_ref, cstate_ref, slots_ref,
    wbuf, weight, nbuf, feat, grad_in, masked, masked_t, pre, dpre,
    partial, coded, xrecv, summed, near_coded, lrecv, far_coded, frecv, scale_src, scale_dst,
    row_src, row_dst, vec, vec_z, vec_p,
    ag_send, ag_recv, ag2_send, ag2_recv, rs_send, rs_recv, row_send, row_recv, z_send, z_recv, p_send, p_recv, load_sem,
):
    dp, mp = lax.axis_index("dp"), lax.axis_index("mp")
    x, z = dp // NZ, dp % NZ

    def at(dx, dz):
        return (((x + dx) % NX) * NZ + (z + dz) % NZ, mp)

    near_peers = [at(0, d) for d in (1, NZ - 1, 2)]
    far_peers = [at(0, d) for d in (4, 8, 12)]

    def plane(i):
        return (((x + i // NMP) % NX) * NZ + z, (mp + i % NMP) % NMP)

    barrier = pltpu.get_barrier_semaphore()

    def greet_z(d, _):
        pl.semaphore_signal(barrier, inc=1, device_id=at(0, d), device_id_type=MESH)
        return 0

    def greet_plane(i, _):
        pl.semaphore_signal(barrier, inc=1, device_id=plane(i), device_id_type=MESH)
        return 0

    lax.fori_loop(1, NZ, greet_z, 0)
    lax.fori_loop(1, NX * NMP, greet_plane, 0)

    load_feat = pltpu.make_async_copy(feat_hbm, feat, load_sem.at[0])
    load_grad = pltpu.make_async_copy(grad_hbm, grad_in, load_sem.at[1])
    load_feat.start()
    load_grad.start()

    wbuf[dp] = fold(master_ref[...]).astype(BF16)
    load_feat.wait()

    first_frame, first_chan = frame_ref[0], chan_ref[0]
    channel = lax.broadcasted_iota(jnp.int32, (1, D), 1)
    chan_keep = jnp.where((channel < first_chan) | (channel >= first_chan + FMASK), 1.0, 0.0)

    def mask_rows(i, _):
        rows = pl.ds(pl.multiple_of(i * 128, 128), 128)
        offset = lax.broadcasted_iota(jnp.int32, (128, 1), 0) + i * 128
        time_keep = jnp.where((offset < first_frame) | (offset >= first_frame + TMASK), 1.0, 0.0)
        kept = feat[rows, :] * (time_keep * chan_keep).astype(BF16)
        masked[rows, :] = kept
        masked_t[:, rows] = kept.T
        return 0

    lax.fori_loop(0, TOK // 128, mask_rows, 0)
    pl.semaphore_wait(barrier, NZ - 1 + NX * NMP - 1)

    gather = Gather(wbuf, ag_send, ag_recv, x, z, mp)
    gather.start()
    load_grad.wait()
    diag = lax.broadcasted_iota(jnp.int32, (ROWS, ROWS), 0) == lax.broadcasted_iota(jnp.int32, (ROWS, ROWS), 1)
    moment = jnp.sum(jnp.where(diag, rmom_ref[...].reshape(1, ROWS), 0.0), axis=1, keepdims=True)
    moment_lanes = jnp.broadcast_to(jnp.sum(moment, axis=0, keepdims=True) * (1.0 / 128), (1, 128))
    gather.forward()

    for d in (0, 1, 3, 2):
        block = (x + d) % NX
        if d:
            gather.wait_block(d)
        unfold_block(wbuf, weight, block)
        depth = pl.ds(pl.multiple_of(block * BLOCK, BLOCK), BLOCK)

        def forward_tile(i, _, d=d, depth=depth):
            cols = pl.ds(pl.multiple_of(i * 256, 256), 256)
            term = jnp.dot(masked[:, depth], weight[depth, cols], preferred_element_type=F32)
            if d == 0:
                pre[:, cols] = term
            else:
                total = pre[:, cols] + term
                if d != 2:
                    pre[:, cols] = total
                else:
                    s = jax.nn.sigmoid(total)
                    slope = s + total * s * (1.0 - s)
                    dpre[:, cols] = (grad_in[:, cols].astype(F32) * slope).astype(BF16)
            return 0

        lax.fori_loop(0, COLS // 256, forward_tile, 0)

    def remote(src, dst, i, to):
        return pltpu.make_async_remote_copy(
            src_ref=src,
            dst_ref=dst,
            send_sem=rs_send.at[i],
            recv_sem=rs_recv.at[i],
            device_id=to,
            device_id_type=MESH,
        )

    def x_copy(d, cls):
        return remote(coded.at[d - 1, cls], xrecv.at[d - 1, cls], (d - 1) * 4 + cls, at(d, 0))

    def x_scale(d):
        return remote(scale_src.at[d - 1], scale_dst.at[d - 1], 12 + d - 1, at(d, 0))

    def near_copy(i):
        return remote(near_coded.at[i], lrecv.at[i], 15 + i, near_peers[i])

    def near_scale(i):
        return remote(scale_src.at[3 + i], scale_dst.at[3 + i], 18 + i, near_peers[i])

    def far_copy(i):
        return remote(far_coded.at[i], frecv.at[i], 21 + i, far_peers[i])

    def far_scale(i):
        return remote(scale_src.at[6 + i], scale_dst.at[6 + i], 24 + i, far_peers[i])

    classes = [(z + d) % 4 for d in (2, 1, 3, 0)]
    for d in (2, 1, 3, 0):
        block = (x + d) % NX
        held = 0 if d == 0 else 1

        def grad_tile(i, peak, block=block, held=held):
            rows = pl.ds(pl.multiple_of(block * BLOCK + i * 4 * ROWS, 32), 4 * ROWS)
            term = jnp.dot(masked_t[rows, :], dpre[...], preferred_element_type=F32)
            for j in range(4):
                slot = term[j * ROWS : (j + 1) * ROWS]
                partial[held, j, i] = slot
                peak = jnp.maximum(peak, peak_of(slot))
            return peak

        peak = lax.fori_loop(0, NZ // 4, grad_tile, jnp.zeros((8, COLS), F32))
        if d:
            scale = scale_of(peak)
            scale_src[d - 1] = pack(scale * (1.0 / 32767))
            x_scale(d).start()
            inverse = 32767.0 / scale
            for cls in classes:

                def encode_slot(j, _, d=d, cls=cls, inverse=inverse):
                    coded[d - 1, cls, j] = encode(partial[1, cls, j], inverse)
                    return 0

                lax.fori_loop(0, 4, encode_slot, 0)
                x_copy(d, cls).start()

    for d in (1, 2, 3):
        x_scale(d).wait_recv()
    scales = [unpack(scale_dst[i]) for i in range(3)]
    for n, cls in enumerate(classes):
        for d in (2, 1, 3):
            x_copy(d, cls).wait_recv()

        def add_x(j, peak, cls=cls):
            term = partial[0, cls, j]
            for i in range(3):
                term = term + decode(xrecv[i, cls, j], scales[i])
            summed[j] = term
            return jnp.maximum(peak, peak_of(term))

        peak = lax.fori_loop(0, 4, add_x, jnp.zeros((8, COLS), F32))
        if n < 3:
            i = (2, 0, 1)[n]
            scale = scale_of(peak)
            scale_src[3 + i] = pack(scale * (1.0 / 32767))
            near_scale(i).start()
            inverse = 32767.0 / scale

            def encode_near(j, _, i=i, inverse=inverse):
                near_coded[i, j] = encode(summed[j], inverse)
                return 0

            lax.fori_loop(0, 4, encode_near, 0)
            near_copy(i).start()

    for i in range(3):
        near_scale(i).wait_recv()
    scales = [unpack(scale_dst[3 + i]) for i in range(3)]
    for i in (0, 1, 2):
        near_copy(i).wait_recv()
    for d in (2, 1, 3, 0):
        j = (z // 4 + d) % 4
        grad = summed[j]
        for i in range(3):
            grad = grad + decode(lrecv[i, j], scales[i])
        if d:
            scale = scale_of(peak_of(grad))
            scale_src[6 + d - 1] = pack(scale * (1.0 / 32767))
            far_scale(d - 1).start()
            far_coded[d - 1] = encode(grad, 32767.0 / scale)
            far_copy(d - 1).start()
    for i in range(3):
        far_scale(i).wait_recv()
        far_copy(i).wait_recv()
        grad = grad + decode(frecv[i], unpack(scale_dst[6 + i]))

    squared = grad * grad
    row_lanes = squared[:, :128]
    for i in range(1, COLS // 128):
        row_lanes = row_lanes + squared[:, i * 128 : (i + 1) * 128]
    row_src[...] = row_lanes

    def row_copy(i):
        return pltpu.make_async_remote_copy(
            src_ref=row_src,
            dst_ref=row_dst.at[i - 1],
            send_sem=row_send.at[i - 1],
            recv_sem=row_recv.at[i - 1],
            device_id=plane(i),
            device_id_type=MESH,
        )

    def z_copy(d):
        return pltpu.make_async_remote_copy(
            src_ref=vec.at[0],
            dst_ref=vec_z.at[d - 1],
            send_sem=z_send.at[d - 1],
            recv_sem=z_recv.at[d - 1],
            device_id=at(0, d),
            device_id_type=MESH,
        )

    def plane_copy(i):
        return pltpu.make_async_remote_copy(
            src_ref=vec.at[1],
            dst_ref=vec_p.at[i - 1],
            send_sem=p_send.at[i - 1],
            recv_sem=p_recv.at[i - 1],
            device_id=plane(i),
            device_id_type=MESH,
        )

    def each(low, high, act):
        def step(i, _):
            act(i)
            return 0

        lax.fori_loop(low, high, step, 0)

    column = jnp.sum(squared, axis=0, keepdims=True)
    pieces = [column[:, i * 128 : (i + 1) * 128] for i in range(COLS // 128)]
    pieces += [jnp.sum(row_lanes, axis=0, keepdims=True), moment_lanes]
    vec[0] = jnp.concatenate(pieces, axis=0)
    each(1, NZ, lambda d: z_copy((d * 7 + NZ) % NZ).start())
    each(1, NMP, lambda i: row_copy(i).start())
    each(1, NMP, lambda i: row_copy(i).wait_recv())
    for i in range(NMP - 1):
        row_lanes = row_lanes + row_dst[i]
    row_total = jnp.sum(row_lanes, axis=1, keepdims=True)
    each(1, NZ, lambda d: z_copy(d).wait_recv())
    sums = vec[0]
    for i in range(NZ - 1):
        sums = sums + vec_z[i]
    vec[1] = sums
    each(1, NX * NMP, lambda i: plane_copy(i).start())
    each(1, NX * NMP, lambda i: plane_copy(i).wait_recv())
    norm = sums[6:7] + jnp.sum(vec_p[:, 6, :], axis=0, keepdims=True)
    for i in range(1, NX):
        sums = sums + vec_p[NMP * i - 1]
    col_total = unpack(sums)
    total = jnp.sum(norm, axis=1, keepdims=True)
    moments = jnp.sum(sums[7:8], axis=1, keepdims=True)

    clip = 1.0 / jnp.maximum(1.0, jnp.sqrt(total / (D * FF)))
    row_state = decay_rate * moment + (1.0 - decay_rate) * (clip * clip * row_total / FF + epsilon)
    col_state = decay_rate * cmom_ref[...].reshape(1, COLS) + (1.0 - decay_rate) * (clip * clip * col_total / D + epsilon)
    row_mean = decay_rate * moments / D + (1.0 - decay_rate) * (clip * clip * (total / FF) / D + epsilon)
    update = clip * grad * lax.rsqrt(row_state * col_state / row_mean)
    updated = master_ref[...] - step_rate * update
    nbuf[dp] = fold(updated).astype(BF16)

    regather = Gather(nbuf, ag2_send, ag2_recv, x, z, mp)
    regather.start()
    new_ref[...] = updated
    rstate_ref[...] = jnp.sum(jnp.where(diag, row_state, 0.0), axis=0, keepdims=True).reshape(ROWS)
    cstate_ref[...] = col_state.reshape(COLS)
    regather.forward()

    def leave(d):
        block = pl.ds(((x + d) % NX) * NZ, NZ)
        return pltpu.make_async_copy(nbuf.at[block], slots_ref.at[block], load_sem.at[2 + d])

    for d in (0, 1, 3, 2):
        if d:
            regather.wait_block(d)
        leave(d).start()
    each(1, NMP, lambda i: row_copy(i).wait_send())
    each(1, NZ, lambda d: z_copy(d).wait_send())
    each(1, NX * NMP, lambda i: plane_copy(i).wait_send())
    gather.finish()
    regather.finish()
    for d in (1, 2, 3):
        x_scale(d).wait_send()
        for cls in range(4):
            x_copy(d, cls).wait_send()
    for i in range(3):
        near_scale(i).wait_send()
        near_copy(i).wait_send()
        far_scale(i).wait_send()
        far_copy(i).wait_send()
    for d in range(NX):
        leave(d).wait()


def layout_kernel(slots, new_in, rstate_in, cstate_in, new_out, rstate_out, cstate_out, low):
    @pl.when(pl.program_id(0) == 0)
    def _():
        new_out[...] = new_in[...]
        rstate_out[...] = rstate_in[...]
        cstate_out[...] = cstate_in[...]

    for i in range(slots.shape[0] // 2):
        first, second = slots[2 * i].astype(F32), slots[2 * i + 1].astype(F32)
        rows = slice(2 * ROWS * i, 2 * ROWS * (i + 1))
        low[rows, :HALF] = jnp.concatenate([first[:ROWS], second[:ROWS]], axis=0).astype(BF16)
        low[rows, HALF:] = jnp.concatenate([first[ROWS:], second[ROWS:]], axis=0).astype(BF16)


def per_device(features, frame_start, chan_start, master_weight, row_moment, col_moment, out_grad):
    vmem = pl.BlockSpec(memory_space=pltpu.VMEM)
    smem = pl.BlockSpec(memory_space=pltpu.SMEM)
    small = (
        jax.ShapeDtypeStruct((ROWS, COLS), F32),
        jax.ShapeDtypeStruct((ROWS,), F32),
        jax.ShapeDtypeStruct((COLS,), F32),
    )
    anywhere = pl.BlockSpec(memory_space=pl.ANY)
    new_master, row_state, col_state, slots = pl.pallas_call(
        kernel,
        name="adafactor_step",
        out_shape=small + (jax.ShapeDtypeStruct((NX * NZ, 2 * ROWS, HALF), BF16),),
        in_specs=[smem, smem, anywhere, vmem, vmem, vmem, anywhere],
        out_specs=(vmem, vmem, vmem, anywhere),
        scratch_shapes=[
            pltpu.VMEM((NX * NZ, 2 * ROWS, HALF), BF16),
            pltpu.VMEM((D, COLS), BF16),
            pltpu.VMEM((NX * NZ, 2 * ROWS, HALF), BF16),
            pltpu.VMEM((TOK, D), BF16),
            pltpu.VMEM((TOK, COLS), BF16),
            pltpu.VMEM((TOK, D), BF16),
            pltpu.VMEM((D, TOK), BF16),
            pltpu.VMEM((TOK, COLS), F32),
            pltpu.VMEM((TOK, COLS), BF16),
            pltpu.VMEM((2, 4, 4, ROWS, COLS), F32),
            pltpu.VMEM((NX - 1, 4, 4, 2 * ROWS, HALF), I16),
            pltpu.VMEM((NX - 1, 4, 4, 2 * ROWS, HALF), I16),
            pltpu.VMEM((4, ROWS, COLS), F32),
            pltpu.VMEM((3, 4, 2 * ROWS, HALF), I16),
            pltpu.VMEM((3, 4, 2 * ROWS, HALF), I16),
            pltpu.VMEM((3, 2 * ROWS, HALF), I16),
            pltpu.VMEM((3, 2 * ROWS, HALF), I16),
            pltpu.VMEM((9, 8, 128), F32),
            pltpu.VMEM((9, 8, 128), F32),
            pltpu.VMEM((ROWS, 128), F32),
            pltpu.VMEM((NMP - 1, ROWS, 128), F32),
            pltpu.VMEM((2, 8, 128), F32),
            pltpu.VMEM((NZ - 1, 8, 128), F32),
            pltpu.VMEM((NX * NMP - 1, 8, 128), F32),
            pltpu.SemaphoreType.DMA((NX * NZ,)),
            pltpu.SemaphoreType.DMA((NX * NZ,)),
            pltpu.SemaphoreType.DMA((NX * NZ,)),
            pltpu.SemaphoreType.DMA((NX * NZ,)),
            pltpu.SemaphoreType.DMA((27,)),
            pltpu.SemaphoreType.DMA((27,)),
            pltpu.SemaphoreType.DMA((NMP - 1,)),
            pltpu.SemaphoreType.DMA((NMP - 1,)),
            pltpu.SemaphoreType.DMA((NZ - 1,)),
            pltpu.SemaphoreType.DMA((NZ - 1,)),
            pltpu.SemaphoreType.DMA((NX * NMP - 1,)),
            pltpu.SemaphoreType.DMA((NX * NMP - 1,)),
            pltpu.SemaphoreType.DMA((2 + NX,)),
        ],
        compiler_params=pltpu.CompilerParams(collective_id=0, has_side_effects=True, vmem_limit_bytes=56 * 2**20),
    )(frame_start, chan_start, features, master_weight, row_moment, col_moment, out_grad)

    steps = 8
    slots_step = NX * NZ // steps
    whole = (
        pl.BlockSpec((ROWS, COLS), lambda i: (0, 0)),
        pl.BlockSpec((ROWS,), lambda i: (0,)),
        pl.BlockSpec((COLS,), lambda i: (0,)),
    )
    return pl.pallas_call(
        layout_kernel,
        name="layout",
        grid=(steps,),
        out_shape=small + (jax.ShapeDtypeStruct((D, COLS), BF16),),
        in_specs=[pl.BlockSpec((slots_step, 2 * ROWS, HALF), lambda i: (i, 0, 0)), *whole],
        out_specs=whole + (pl.BlockSpec((D // steps, COLS), lambda i: (i, 0)),),
    )(slots, new_master, row_state, col_state)


def solution(mesh):
    placed = (P("dp", None), P("dp"), P("dp"), P("dp", "mp"), P("dp"), P("mp"), P("dp", "mp"))
    return jax.shard_map(
        per_device,
        mesh=mesh,
        in_specs=placed,
        out_specs=(P("dp", "mp"), P("dp"), P("mp"), P(None, "mp")),
        check_vma=False,
    )
```

```python
import functools

import jax
import jax.numpy as jnp
from jax import lax
from jax.experimental import pallas as pl
from jax.experimental.pallas import tpu as pltpu
from jax.sharding import PartitionSpec as P

D = 1536
FF = 6144
TMASK = 128
FMASK = 192
NX = 4
NZ = 16
NMP = 8
TOK = 512
ROWS = D // (NX * NZ)
COLS = FF // NMP
HALF = COLS // 2
BLOCK = ROWS * NZ

epsilon = 1e-06
decay_rate = 0.8
step_rate = 0.01

MESH = pl.DeviceIdType.MESH
F32 = jnp.float32
BF16 = jnp.bfloat16
I16 = jnp.int16


def fold(rows):
    return jnp.concatenate([rows[:, :HALF], rows[:, HALF:]], axis=0)


class Gather:
    def __init__(self, buf, send_sem, recv_sem, x, z, mp):
        self.buf, self.send_sem, self.recv_sem = buf, send_sem, recv_sem
        self.x, self.z, self.mp = x, z, mp
        self.up, self.down = lax.rem(x + 1, NX), lax.rem(x + NX - 1, NX)
        self.line = [lax.rem(z + o, NZ) for o in range(NZ)]
        odd = lax.rem(z, 2)
        self.relay_from = [self.down + (self.up - self.down) * p for p in (odd, 1 - odd)]
        self.relay_to = [self.up + (self.down - self.up) * p for p in (odd, 1 - odd)]
        self.sent = 0

    def copy(self, slot, k, x, z):
        return pltpu.make_async_remote_copy(
            src_ref=self.buf.at[slot],
            dst_ref=self.buf.at[slot],
            send_sem=self.send_sem.at[k],
            recv_sem=self.recv_sem.at[slot],
            device_id=(x * NZ + z, self.mp),
            device_id_type=MESH,
        )

    def send(self, slot, x, z):
        self.copy(slot, self.sent, x, z).start()
        self.sent += 1

    def slot(self, o):
        return self.x * NZ + self.line[o]

    def arrived(self, slot):
        self.copy(slot, 0, self.x, self.z).wait_recv()

    def along_x(self, o):
        self.send(self.slot(o), self.up, self.z)
        self.send(self.slot(o), self.down, self.z)

    def near(self, o):
        for d in (2, 1, 15):
            self.send(self.slot(o), self.x, self.line[d])

    def relay(self, o):
        slot = self.relay_from[o % 2] * NZ + self.line[o]
        self.arrived(slot)
        self.send(slot, self.relay_to[o % 2], self.z)

    def start(self):
        for d in (8, 4, 12):
            self.send(self.slot(0), self.x, self.line[d])
        self.near(0)
        self.along_x(0)

    def forward(self):
        def far(o):
            self.arrived(self.slot(o))
            self.near(o)
            self.along_x(o)

        def pass_on(*offsets):
            for o in offsets:
                self.arrived(self.slot(o))
                self.along_x(o)

        def relay(*offsets):
            for o in offsets:
                self.relay(o)

        pass_on(15, 1, 14)
        relay(0)
        far(4)
        far(12)
        relay(15, 1, 14)
        far(8)
        relay(4, 12)
        pass_on(3, 5, 2, 11, 13, 10)
        relay(8)
        pass_on(7, 9, 6)
        relay(3, 5, 2, 11, 13, 10, 7, 9, 6)

    def wait_block(self, d):
        x = lax.rem(self.x + d, NX)

        def step(i, _):
            if d == 2:
                owner = i
            else:
                owner = 2 * i + (0 if d == 1 else 1)
            self.arrived(x * NZ + owner)
            return 0

        lax.fori_loop(0, NZ if d == 2 else NZ // 2, step, 0)

    def finish(self):
        def step(k, _):
            self.copy(0, k, self.x, self.z).wait_send()
            return 0

        lax.fori_loop(0, NX * NZ - 1, step, 0)


def unfold_block(buf, out, x):
    def step(i, _):
        first = buf[x * NZ + 2 * i].astype(F32)
        second = buf[x * NZ + 2 * i + 1].astype(F32)
        rows = pl.ds(pl.multiple_of(x * BLOCK + i * 2 * ROWS, 2 * ROWS), 2 * ROWS)
        out[rows, :HALF] = jnp.concatenate([first[:ROWS], second[:ROWS]], axis=0).astype(BF16)
        out[rows, HALF:] = jnp.concatenate([first[ROWS:], second[ROWS:]], axis=0).astype(BF16)
        return 0

    lax.fori_loop(0, NZ // 2, step, 0)


def unfold(slot):
    return jnp.concatenate([slot[:ROWS], slot[ROWS:]], axis=1)


def pack(row):
    pieces = [row[:, i * 128 : (i + 1) * 128] for i in range(COLS // 128)]
    return jnp.concatenate(pieces + [jnp.zeros((8 - COLS // 128, 128), F32)], axis=0)


def unpack(tile):
    return jnp.concatenate([tile[i : i + 1] for i in range(COLS // 128)], axis=1)


def peak_of(rows):
    size = jnp.abs(rows)
    return jnp.maximum(jnp.maximum(size[:8], size[8:16]), size[16:24])


def scale_of(peak):
    return jnp.maximum(jnp.max(peak, axis=0, keepdims=True), 1e-30)


def encode(rows, inverse):
    return jnp.round(fold(rows * inverse)).astype(jnp.int32).astype(I16)


def decode(slot, scale):
    return unfold(slot.astype(jnp.int32).astype(F32)) * scale


def kernel(
    frame_ref, chan_ref, feat_hbm, master_ref, rmom_ref, cmom_ref, grad_hbm,
    new_ref, rstate_ref, cstate_ref, slots_ref,
    wbuf, weight, nbuf, feat, grad_in, masked, masked_t, pre, dpre,
    partial, inverses, coded, xrecv, summed, near_coded, lrecv, far_coded, frecv, scale_src, scale_dst,
    row_src, row_dst, vec, vec_z, vec_p,
    ag_send, ag_recv, ag2_send, ag2_recv, rs_send, rs_recv, row_send, row_recv, z_send, z_recv, p_send, p_recv, load_sem,
):
    dp, mp = lax.axis_index("dp"), lax.axis_index("mp")
    x, z = lax.div(dp, NZ), lax.rem(dp, NZ)

    def at(dx, dz):
        return (lax.rem(x + dx, NX) * NZ + lax.rem(z + dz, NZ), mp)

    near_peers = [at(0, d) for d in (1, NZ - 1, 2)]
    far_peers = [at(0, d) for d in (4, 8, 12)]

    def plane(i):
        return (lax.rem(x + i // NMP, NX) * NZ + z, lax.rem(mp + i % NMP, NMP))

    barrier = pltpu.get_barrier_semaphore()

    greeted = [at(0, d) for d in range(1, NZ)] + [plane(i) for i in range(1, NX * NMP)]
    for peer in greeted:
        pl.semaphore_signal(barrier, inc=1, device_id=peer, device_id_type=MESH)

    load_feat = pltpu.make_async_copy(feat_hbm, feat, load_sem.at[0])
    load_grad = pltpu.make_async_copy(grad_hbm, grad_in, load_sem.at[1])
    load_feat.start()
    load_grad.start()

    wbuf[dp] = fold(master_ref[...]).astype(BF16)
    pl.semaphore_wait(barrier, len(greeted))
    gather = Gather(wbuf, ag_send, ag_recv, x, z, mp)
    gather.start()

    load_feat.wait()
    first_frame, first_chan = frame_ref[0], chan_ref[0]
    channel = lax.broadcasted_iota(jnp.int32, (1, D), 1)
    chan_keep = jnp.where((channel < first_chan) | (channel >= first_chan + FMASK), 1.0, 0.0)

    def mask_rows(i, _):
        rows = pl.ds(pl.multiple_of(i * 128, 128), 128)
        offset = lax.broadcasted_iota(jnp.int32, (128, 1), 0) + i * 128
        time_keep = jnp.where((offset < first_frame) | (offset >= first_frame + TMASK), 1.0, 0.0)
        kept = feat[rows, :] * (time_keep * chan_keep).astype(BF16)
        masked[rows, :] = kept
        masked_t[:, rows] = kept.T
        return 0

    lax.fori_loop(0, TOK // 128, mask_rows, 0)
    load_grad.wait()
    diag = lax.broadcasted_iota(jnp.int32, (ROWS, ROWS), 0) == lax.broadcasted_iota(jnp.int32, (ROWS, ROWS), 1)
    moment = jnp.sum(jnp.where(diag, rmom_ref[...].reshape(1, ROWS), 0.0), axis=1, keepdims=True)
    moment_lanes = jnp.broadcast_to(jnp.sum(moment, axis=0, keepdims=True) * (1.0 / 128), (1, 128))
    gather.forward()

    for d in (0, 1, 3, 2):
        block = lax.rem(x + d, NX)
        if d:
            gather.wait_block(d)
        unfold_block(wbuf, weight, block)
        depth = pl.ds(pl.multiple_of(block * BLOCK, BLOCK), BLOCK)

        def forward_tile(i, _, d=d, depth=depth):
            cols = pl.ds(pl.multiple_of(i * 256, 256), 256)
            term = jnp.dot(masked[:, depth], weight[depth, cols], preferred_element_type=F32)
            if d == 0:
                pre[:, cols] = term
            else:
                total = pre[:, cols] + term
                if d != 2:
                    pre[:, cols] = total
                else:
                    s = jax.nn.sigmoid(total)
                    slope = s + total * s * (1.0 - s)
                    dpre[:, cols] = (grad_in[:, cols].astype(F32) * slope).astype(BF16)
            return 0

        lax.fori_loop(0, COLS // 256, forward_tile, 0)

    def remote(src, dst, i, to):
        return pltpu.make_async_remote_copy(
            src_ref=src,
            dst_ref=dst,
            send_sem=rs_send.at[i],
            recv_sem=rs_recv.at[i],
            device_id=to,
            device_id_type=MESH,
        )

    def x_copy(d, cls):
        return remote(coded.at[d - 1, cls], xrecv.at[d - 1, cls], (d - 1) * 4 + cls, at(d, 0))

    def x_scale(d):
        return remote(scale_src.at[d - 1], scale_dst.at[d - 1], 12 + d - 1, at(d, 0))

    def near_copy(i):
        return remote(near_coded.at[i], lrecv.at[i], 15 + i, near_peers[i])

    def near_scale(i):
        return remote(scale_src.at[3 + i], scale_dst.at[3 + i], 18 + i, near_peers[i])

    def far_copy(i):
        return remote(far_coded.at[i], frecv.at[i], 21 + i, far_peers[i])

    def far_scale(i):
        return remote(scale_src.at[6 + i], scale_dst.at[6 + i], 24 + i, far_peers[i])

    classes = [lax.rem(z + d, 4) for d in (2, 1, 3, 0)]

    def grad_block(d):
        block = lax.rem(x + d, NX)

        def grad_tile(i, peak):
            rows = pl.ds(pl.multiple_of(block * BLOCK + i * 4 * ROWS, 32), 4 * ROWS)
            term = jnp.dot(masked_t[rows, :], dpre[...], preferred_element_type=F32)
            for j in range(4):
                slot = term[j * ROWS : (j + 1) * ROWS]
                partial[d, j, i] = slot
                peak = jnp.maximum(peak, peak_of(slot))
            return peak

        peak = lax.fori_loop(0, NZ // 4, grad_tile, jnp.zeros((8, COLS), F32))
        if d:
            scale = scale_of(peak)
            scale_src[d - 1] = pack(scale * (1.0 / 32767))
            x_scale(d).start()
            inverses[d - 1] = jnp.broadcast_to(32767.0 / scale, (8, COLS))

    def send_class(d, cls):
        inverse = inverses[d - 1][:1]

        def encode_slot(j, _):
            coded[d - 1, cls, j] = encode(partial[d, cls, j], inverse)
            return 0

        lax.fori_loop(0, 4, encode_slot, 0)
        x_copy(d, cls).start()

    for d in (2, 1, 3):
        grad_block(d)
        send_class(d, classes[0])
    grad_block(0)
    for cls in classes[1:]:
        for d in (2, 1, 3):
            send_class(d, cls)

    for d in (1, 2, 3):
        x_scale(d).wait_recv()
    scales = [unpack(scale_dst[i]) for i in range(3)]
    for n, cls in enumerate(classes):
        for d in (2, 1, 3):
            x_copy(d, cls).wait_recv()

        def add_x(j, peak, cls=cls):
            term = partial[0, cls, j]
            for i in range(3):
                term = term + decode(xrecv[i, cls, j], scales[i])
            summed[j] = term
            return jnp.maximum(peak, peak_of(term))

        peak = lax.fori_loop(0, 4, add_x, jnp.zeros((8, COLS), F32))
        if n < 3:
            i = (2, 0, 1)[n]
            scale = scale_of(peak)
            scale_src[3 + i] = pack(scale * (1.0 / 32767))
            near_scale(i).start()
            inverse = 32767.0 / scale

            def encode_near(j, _, i=i, inverse=inverse):
                near_coded[i, j] = encode(summed[j], inverse)
                return 0

            lax.fori_loop(0, 4, encode_near, 0)
            near_copy(i).start()

    for i in range(3):
        near_scale(i).wait_recv()
    scales = [unpack(scale_dst[3 + i]) for i in range(3)]
    for i in (0, 1, 2):
        near_copy(i).wait_recv()
    for d in (2, 1, 3, 0):
        j = lax.rem(lax.div(z, 4) + d, 4)
        grad = summed[j]
        for i in range(3):
            grad = grad + decode(lrecv[i, j], scales[i])
        if d:
            scale = scale_of(peak_of(grad))
            scale_src[6 + d - 1] = pack(scale * (1.0 / 32767))
            far_scale(d - 1).start()
            far_coded[d - 1] = encode(grad, 32767.0 / scale)
            far_copy(d - 1).start()
    for i in range(3):
        far_scale(i).wait_recv()
        far_copy(i).wait_recv()
        grad = grad + decode(frecv[i], unpack(scale_dst[6 + i]))

    squared = grad * grad
    row_lanes = squared[:, :128]
    for i in range(1, COLS // 128):
        row_lanes = row_lanes + squared[:, i * 128 : (i + 1) * 128]
    row_src[...] = row_lanes

    def row_copy(i):
        return pltpu.make_async_remote_copy(
            src_ref=row_src,
            dst_ref=row_dst.at[i - 1],
            send_sem=row_send.at[i - 1],
            recv_sem=row_recv.at[i - 1],
            device_id=plane(i),
            device_id_type=MESH,
        )

    def z_copy(d):
        return pltpu.make_async_remote_copy(
            src_ref=vec.at[0],
            dst_ref=vec_z.at[d - 1],
            send_sem=z_send.at[d - 1],
            recv_sem=z_recv.at[d - 1],
            device_id=at(0, d),
            device_id_type=MESH,
        )

    def plane_copy(i):
        return pltpu.make_async_remote_copy(
            src_ref=vec.at[1],
            dst_ref=vec_p.at[i - 1],
            send_sem=p_send.at[i - 1],
            recv_sem=p_recv.at[i - 1],
            device_id=plane(i),
            device_id_type=MESH,
        )

    def each(low, high, act):
        for i in range(low, high):
            act(i)

    column = jnp.sum(squared, axis=0, keepdims=True)
    pieces = [column[:, i * 128 : (i + 1) * 128] for i in range(COLS // 128)]
    pieces += [jnp.sum(row_lanes, axis=0, keepdims=True), moment_lanes]
    vec[0] = jnp.concatenate(pieces, axis=0)
    each(1, NZ, lambda d: z_copy((d * 7) % NZ).start())
    each(1, NMP, lambda i: row_copy(i).start())
    each(1, NMP, lambda i: row_copy(i).wait_recv())
    for i in range(NMP - 1):
        row_lanes = row_lanes + row_dst[i]
    row_total = jnp.sum(row_lanes, axis=1, keepdims=True)
    each(1, NZ, lambda d: z_copy(d).wait_recv())
    sums = vec[0]
    for i in range(NZ - 1):
        sums = sums + vec_z[i]
    vec[1] = sums
    each(1, NX * NMP, lambda i: plane_copy(i).start())
    each(1, NX * NMP, lambda i: plane_copy(i).wait_recv())
    norm = sums[6:7] + jnp.sum(vec_p[:, 6, :], axis=0, keepdims=True)
    for i in range(1, NX):
        sums = sums + vec_p[NMP * i - 1]
    col_total = unpack(sums)
    total = jnp.sum(norm, axis=1, keepdims=True)
    moments = jnp.sum(sums[7:8], axis=1, keepdims=True)

    clip = 1.0 / jnp.maximum(1.0, jnp.sqrt(total / (D * FF)))
    row_state = decay_rate * moment + (1.0 - decay_rate) * (clip * clip * row_total / FF + epsilon)
    col_state = decay_rate * cmom_ref[...].reshape(1, COLS) + (1.0 - decay_rate) * (clip * clip * col_total / D + epsilon)
    row_mean = decay_rate * moments / D + (1.0 - decay_rate) * (clip * clip * (total / FF) / D + epsilon)
    update = clip * grad * lax.rsqrt(row_state * col_state / row_mean)
    updated = master_ref[...] - step_rate * update
    nbuf[dp] = fold(updated).astype(BF16)

    regather = Gather(nbuf, ag2_send, ag2_recv, x, z, mp)
    regather.start()
    new_ref[...] = updated
    rstate_ref[...] = jnp.sum(jnp.where(diag, row_state, 0.0), axis=0, keepdims=True).reshape(ROWS)
    cstate_ref[...] = col_state.reshape(COLS)
    regather.forward()

    def leave(d):
        block = pl.ds(lax.rem(x + d, NX) * NZ, NZ)
        return pltpu.make_async_copy(nbuf.at[block], slots_ref.at[block], load_sem.at[2 + d])

    for d in (0, 1, 3, 2):
        if d:
            regather.wait_block(d)
        leave(d).start()
    each(1, NMP, lambda i: row_copy(i).wait_send())
    each(1, NZ, lambda d: z_copy(d).wait_send())
    each(1, NX * NMP, lambda i: plane_copy(i).wait_send())
    gather.finish()
    regather.finish()
    for d in (1, 2, 3):
        x_scale(d).wait_send()
        for cls in range(4):
            x_copy(d, cls).wait_send()
    for i in range(3):
        near_scale(i).wait_send()
        near_copy(i).wait_send()
        far_scale(i).wait_send()
        far_copy(i).wait_send()
    for d in range(NX):
        leave(d).wait()


def layout_kernel(slots, new_in, rstate_in, cstate_in, new_out, rstate_out, cstate_out, low):
    @pl.when(pl.program_id(0) == 0)
    def _():
        new_out[...] = new_in[...]
        rstate_out[...] = rstate_in[...]
        cstate_out[...] = cstate_in[...]

    for i in range(slots.shape[0] // 2):
        first, second = slots[2 * i].astype(F32), slots[2 * i + 1].astype(F32)
        rows = slice(2 * ROWS * i, 2 * ROWS * (i + 1))
        low[rows, :HALF] = jnp.concatenate([first[:ROWS], second[:ROWS]], axis=0).astype(BF16)
        low[rows, HALF:] = jnp.concatenate([first[ROWS:], second[ROWS:]], axis=0).astype(BF16)


def per_device(features, frame_start, chan_start, master_weight, row_moment, col_moment, out_grad):
    vmem = pl.BlockSpec(memory_space=pltpu.VMEM)
    smem = pl.BlockSpec(memory_space=pltpu.SMEM)
    small = (
        jax.ShapeDtypeStruct((ROWS, COLS), F32),
        jax.ShapeDtypeStruct((ROWS,), F32),
        jax.ShapeDtypeStruct((COLS,), F32),
    )
    anywhere = pl.BlockSpec(memory_space=pl.ANY)
    new_master, row_state, col_state, slots = pl.pallas_call(
        kernel,
        name="adafactor_step",
        out_shape=small + (jax.ShapeDtypeStruct((NX * NZ, 2 * ROWS, HALF), BF16),),
        in_specs=[smem, smem, anywhere, vmem, vmem, vmem, anywhere],
        out_specs=(vmem, vmem, vmem, anywhere),
        scratch_shapes=[
            pltpu.VMEM((NX * NZ, 2 * ROWS, HALF), BF16),
            pltpu.VMEM((D, COLS), BF16),
            pltpu.VMEM((NX * NZ, 2 * ROWS, HALF), BF16),
            pltpu.VMEM((TOK, D), BF16),
            pltpu.VMEM((TOK, COLS), BF16),
            pltpu.VMEM((TOK, D), BF16),
            pltpu.VMEM((D, TOK), BF16),
            pltpu.VMEM((TOK, COLS), F32),
            pltpu.VMEM((TOK, COLS), BF16),
            pltpu.VMEM((NX, 4, 4, ROWS, COLS), F32),
            pltpu.VMEM((NX - 1, 8, COLS), F32),
            pltpu.VMEM((NX - 1, 4, 4, 2 * ROWS, HALF), I16),
            pltpu.VMEM((NX - 1, 4, 4, 2 * ROWS, HALF), I16),
            pltpu.VMEM((4, ROWS, COLS), F32),
            pltpu.VMEM((3, 4, 2 * ROWS, HALF), I16),
            pltpu.VMEM((3, 4, 2 * ROWS, HALF), I16),
            pltpu.VMEM((3, 2 * ROWS, HALF), I16),
            pltpu.VMEM((3, 2 * ROWS, HALF), I16),
            pltpu.VMEM((9, 8, 128), F32),
            pltpu.VMEM((9, 8, 128), F32),
            pltpu.VMEM((ROWS, 128), F32),
            pltpu.VMEM((NMP - 1, ROWS, 128), F32),
            pltpu.VMEM((2, 8, 128), F32),
            pltpu.VMEM((NZ - 1, 8, 128), F32),
            pltpu.VMEM((NX * NMP - 1, 8, 128), F32),
            pltpu.SemaphoreType.DMA((NX * NZ,)),
            pltpu.SemaphoreType.DMA((NX * NZ,)),
            pltpu.SemaphoreType.DMA((NX * NZ,)),
            pltpu.SemaphoreType.DMA((NX * NZ,)),
            pltpu.SemaphoreType.DMA((27,)),
            pltpu.SemaphoreType.DMA((27,)),
            pltpu.SemaphoreType.DMA((NMP - 1,)),
            pltpu.SemaphoreType.DMA((NMP - 1,)),
            pltpu.SemaphoreType.DMA((NZ - 1,)),
            pltpu.SemaphoreType.DMA((NZ - 1,)),
            pltpu.SemaphoreType.DMA((NX * NMP - 1,)),
            pltpu.SemaphoreType.DMA((NX * NMP - 1,)),
            pltpu.SemaphoreType.DMA((2 + NX,)),
        ],
        compiler_params=pltpu.CompilerParams(collective_id=0, has_side_effects=True, vmem_limit_bytes=56 * 2**20),
    )(frame_start, chan_start, features, master_weight, row_moment, col_moment, out_grad)

    steps = 8
    slots_step = NX * NZ // steps
    whole = (
        pl.BlockSpec((ROWS, COLS), lambda i: (0, 0)),
        pl.BlockSpec((ROWS,), lambda i: (0,)),
        pl.BlockSpec((COLS,), lambda i: (0,)),
    )
    return pl.pallas_call(
        layout_kernel,
        name="layout",
        compiler_params=pltpu.CompilerParams(vmem_limit_bytes=60 * 2**20),
        grid=(steps,),
        out_shape=small + (jax.ShapeDtypeStruct((D, COLS), BF16),),
        in_specs=[pl.BlockSpec((slots_step, 2 * ROWS, HALF), lambda i: (i, 0, 0)), *whole],
        out_specs=whole + (pl.BlockSpec((D // steps, COLS), lambda i: (i, 0)),),
    )(slots, new_master, row_state, col_state)


def solution(mesh):
    placed = (P("dp", None), P("dp"), P("dp"), P("dp", "mp"), P("dp"), P("mp"), P("dp", "mp"))
    return jax.shard_map(
        per_device,
        mesh=mesh,
        in_specs=placed,
        out_specs=(P("dp", "mp"), P("dp"), P("mp"), P(None, "mp")),
        check_vma=False,
    )
```

```python
import functools

import jax
import jax.numpy as jnp
from jax import lax
from jax.experimental import pallas as pl
from jax.experimental.pallas import tpu as pltpu
from jax.sharding import PartitionSpec as P

D = 1536
FF = 6144
TMASK = 128
FMASK = 192
NX = 4
NZ = 16
NMP = 8
TOK = 512
ROWS = D // (NX * NZ)
COLS = FF // NMP
HALF = COLS // 2
BLOCK = ROWS * NZ

epsilon = 1e-06
decay_rate = 0.8
step_rate = 0.01

MESH = pl.DeviceIdType.MESH
F32 = jnp.float32
BF16 = jnp.bfloat16
I16 = jnp.int16


def fold(rows):
    return jnp.concatenate([rows[:, :HALF], rows[:, HALF:]], axis=0)


class Gather:
    def __init__(self, buf, send_sem, recv_sem, x, z, mp):
        self.buf, self.send_sem, self.recv_sem = buf, send_sem, recv_sem
        self.x, self.z, self.mp = x, z, mp
        self.up, self.down = lax.rem(x + 1, NX), lax.rem(x + NX - 1, NX)
        self.line = [lax.rem(z + o, NZ) for o in range(NZ)]
        odd = lax.rem(z, 2)
        self.relay_from = [self.down + (self.up - self.down) * p for p in (odd, 1 - odd)]
        self.relay_to = [self.up + (self.down - self.up) * p for p in (odd, 1 - odd)]
        self.sent = 0

    def copy(self, slot, k, x, z):
        return pltpu.make_async_remote_copy(
            src_ref=self.buf.at[slot],
            dst_ref=self.buf.at[slot],
            send_sem=self.send_sem.at[k],
            recv_sem=self.recv_sem.at[slot],
            device_id=(x * NZ + z, self.mp),
            device_id_type=MESH,
        )

    def send(self, slot, x, z):
        self.copy(slot, self.sent, x, z).start()
        self.sent += 1

    def slot(self, o):
        return self.x * NZ + self.line[o]

    def arrived(self, slot):
        self.copy(slot, 0, self.x, self.z).wait_recv()

    def along_x(self, o):
        self.send(self.slot(o), self.up, self.z)
        self.send(self.slot(o), self.down, self.z)

    def near(self, o):
        for d in (2, 1, 15):
            self.send(self.slot(o), self.x, self.line[d])

    def relay(self, o):
        slot = self.relay_from[o % 2] * NZ + self.line[o]
        self.arrived(slot)
        self.send(slot, self.relay_to[o % 2], self.z)

    def start(self):
        for d in (8, 4, 12):
            self.send(self.slot(0), self.x, self.line[d])
        self.near(0)
        self.along_x(0)

    def far(self, o):
        self.arrived(self.slot(o))
        self.near(o)
        self.along_x(o)

    def pass_on(self, *offsets):
        for o in offsets:
            self.arrived(self.slot(o))
            self.along_x(o)

    def relays(self, *offsets):
        for o in offsets:
            self.relay(o)

    def events(self):
        self.pass_on(15, 1, 14)
        self.relays(0)
        yield
        self.far(4)
        self.far(12)
        self.relays(15, 1, 14)
        self.far(8)
        self.relays(4, 12)
        yield
        self.pass_on(3, 5, 2, 11, 13, 10)
        self.relays(8)
        self.pass_on(7, 9, 6)
        yield
        self.relays(3, 5, 2, 11, 13, 10, 7, 9, 6)
        yield

    def wait_block(self, d):
        x = lax.rem(self.x + d, NX)

        def step(i, _):
            if d == 2:
                owner = i
            else:
                owner = 2 * i + (0 if d == 1 else 1)
            self.arrived(x * NZ + owner)
            return 0

        lax.fori_loop(0, NZ if d == 2 else NZ // 2, step, 0)

    def finish(self):
        def step(k, _):
            self.copy(0, k, self.x, self.z).wait_send()
            return 0

        lax.fori_loop(0, NX * NZ - 1, step, 0)


class Tiles:
    def __init__(self, buf, send_sem, recv_sem, x, z, mp):
        self.buf, self.send_sem, self.recv_sem = buf, send_sem, recv_sem
        self.x, self.z, self.mp = x, z, mp
        self.sent = []

    def index(self, x, z):
        return x * NZ + lax.rem(z, 4) * 4 + lax.div(z, 4)

    def round(self, first, count, k, peers):
        for i, peer in enumerate(peers):
            block = self.buf.at[pl.ds(first, count)]
            copy = pltpu.make_async_remote_copy(
                src_ref=block,
                dst_ref=block,
                send_sem=self.send_sem.at[k + i],
                recv_sem=self.recv_sem.at[k + i],
                device_id=peer,
                device_id_type=MESH,
            )
            copy.start()
            self.sent.append(copy)

    def arrived(self, k):
        for copy in self.sent[k : k + 3]:
            copy.wait_recv()

    def along(self, distances):
        return [(self.x * NZ + lax.rem(self.z + d, NZ), self.mp) for d in distances]

    def far(self):
        self.round(self.index(self.x, self.z), 1, 0, self.along((8, 4, 12)))

    def near(self):
        self.arrived(0)
        self.round(self.x * NZ + lax.rem(self.z, 4) * 4, 4, 3, self.along((2, 1, 15)))

    def across(self):
        self.arrived(3)
        peers = [(lax.rem(self.x + d, NX) * NZ + self.z, self.mp) for d in (2, 1, 3)]
        self.round(self.x * NZ, NZ, 6, peers)

    def finish(self):
        for copy in self.sent:
            copy.wait_send()


def stack(first, second):
    return jnp.concatenate([first, second], axis=0).astype(BF16)


def unfold(slot):
    return jnp.concatenate([slot[:ROWS], slot[ROWS:]], axis=1)


def pack(row, *more):
    pieces = [row[:, i * 128 : (i + 1) * 128] for i in range(COLS // 128)] + list(more)
    if len(pieces) < 8:
        pieces.append(jnp.zeros((8 - len(pieces), 128), F32))
    return jnp.concatenate(pieces, axis=0)


def raw(slot):
    return unfold(slot.astype(jnp.int32).astype(F32))


def unpack(tile):
    return jnp.concatenate([tile[i : i + 1] for i in range(COLS // 128)], axis=1)


def peak_of(rows):
    size = jnp.abs(rows)
    return jnp.maximum(jnp.maximum(size[:8], size[8:16]), size[16:24])


def scale_of(peak):
    return jnp.maximum(jnp.max(peak, axis=0, keepdims=True), 1e-30)


def encode(rows, inverse):
    return jnp.round(fold(rows * inverse)).astype(jnp.int32).astype(I16)


def decode(slot, scale):
    return raw(slot) * scale


def kernel(
    frame_ref, chan_ref, feat_hbm, master_ref, rmom_ref, cmom_ref, grad_hbm,
    new_ref, rstate_ref, cstate_ref, low_ref,
    wbuf, wtile, weight, nbuf, ntile, low, feat, grad_in, masked, masked_t, pre, dpre,
    partial, inverses, coded, xrecv, summed, near_coded, lrecv, far_coded, frecv, scale_src, scale_dst,
    row_src, row_dst, vec, vec_z, vec_p,
    ag_send, ag_recv, ag2_send, ag2_recv, rs_send, rs_recv, row_send, row_recv, z_send, z_recv, p_send, p_recv, wt_send, wt_recv, nt_send, nt_recv, load_sem,
):
    dp, mp = lax.axis_index("dp"), lax.axis_index("mp")
    x, z = lax.div(dp, NZ), lax.rem(dp, NZ)

    def at(dx, dz):
        return (lax.rem(x + dx, NX) * NZ + lax.rem(z + dz, NZ), mp)

    near_peers = [at(0, d) for d in (1, NZ - 1, 2)]
    far_peers = [at(0, d) for d in (4, 8, 12)]

    def plane(i):
        return (lax.rem(x + i // NMP, NX) * NZ + z, lax.rem(mp + i % NMP, NMP))

    barrier = pltpu.get_barrier_semaphore()

    greeted = [at(0, d) for d in range(1, NZ)] + [plane(i) for i in range(1, NX * NMP)]
    for peer in greeted:
        pl.semaphore_signal(barrier, inc=1, device_id=peer, device_id_type=MESH)

    load_feat = pltpu.make_async_copy(feat_hbm, feat, load_sem.at[0])
    load_grad = pltpu.make_async_copy(grad_hbm, grad_in, load_sem.at[1])
    load_feat.start()
    load_grad.start()

    master = master_ref[...]
    peak = scale_of(peak_of(master))
    diag = lax.broadcasted_iota(jnp.int32, (ROWS, 128), 0) == lax.broadcasted_iota(jnp.int32, (ROWS, 128), 1)

    def to_lanes(column):
        return jnp.sum(jnp.where(diag, column, 0.0), axis=0, keepdims=True)

    def to_rows(lanes):
        return jnp.sum(jnp.where(diag, lanes, 0.0), axis=1, keepdims=True)

    moment_lanes = jnp.concatenate([rmom_ref[...].reshape(1, ROWS), jnp.zeros((1, 128 - ROWS), F32)], axis=1)
    wbuf[dp] = encode(master, 32767.0 / peak)
    tiles = Tiles(wtile, wt_send, wt_recv, x, z, mp)
    wtile[tiles.index(x, z)] = pack(peak * (1.0 / 32767), moment_lanes)

    pl.semaphore_wait(barrier, len(greeted))
    tiles.far()
    gather = Gather(wbuf, ag_send, ag_recv, x, z, mp)
    gather.start()

    load_feat.wait()
    first_frame, first_chan = frame_ref[0], chan_ref[0]
    channel = lax.broadcasted_iota(jnp.int32, (1, D), 1)
    chan_keep = jnp.where((channel < first_chan) | (channel >= first_chan + FMASK), 1.0, 0.0)

    def mask_rows(i, _):
        rows = pl.ds(pl.multiple_of(i * 128, 128), 128)
        offset = lax.broadcasted_iota(jnp.int32, (128, 1), 0) + i * 128
        time_keep = jnp.where((offset < first_frame) | (offset >= first_frame + TMASK), 1.0, 0.0)
        kept = feat[rows, :] * (time_keep * chan_keep).astype(BF16)
        masked[rows, :] = kept
        masked_t[:, rows] = kept.T
        return 0

    lax.fori_loop(0, TOK // 128, mask_rows, 0)
    load_grad.wait()
    moment = to_rows(moment_lanes)
    for part, _ in enumerate(gather.events()):
        if part == 1:
            tiles.near()
        elif part == 2:
            tiles.across()
    tiles.arrived(6)

    def weights(slot):
        tile = wtile[tiles.index(lax.div(slot, NZ), lax.rem(slot, NZ))]
        return decode(wbuf[slot], unpack(tile)), tile

    def weight_block(block):
        def step(i, _):
            slot = block * NZ + 2 * i
            rows = pl.ds(pl.multiple_of(slot * ROWS, 2 * ROWS), 2 * ROWS)
            weight[rows, :] = stack(weights(slot)[0], weights(slot + 1)[0])
            return 0

        lax.fori_loop(0, NZ // 2, step, 0)

    for d in (0, 1, 3, 2):
        block = lax.rem(x + d, NX)
        if d:
            gather.wait_block(d)
        weight_block(block)
        depth = pl.ds(pl.multiple_of(block * BLOCK, BLOCK), BLOCK)

        def forward_tile(i, _, d=d, depth=depth):
            cols = pl.ds(pl.multiple_of(i * 256, 256), 256)
            term = jnp.dot(masked[:, depth], weight[depth, cols], preferred_element_type=F32)
            if d == 0:
                pre[:, cols] = term
            else:
                total = pre[:, cols] + term
                if d != 2:
                    pre[:, cols] = total
                else:
                    s = jax.nn.sigmoid(total)
                    slope = s + total * s * (1.0 - s)
                    dpre[:, cols] = (grad_in[:, cols].astype(F32) * slope).astype(BF16)
            return 0

        lax.fori_loop(0, COLS // 256, forward_tile, 0)

    def remote(src, dst, i, to):
        return pltpu.make_async_remote_copy(
            src_ref=src,
            dst_ref=dst,
            send_sem=rs_send.at[i],
            recv_sem=rs_recv.at[i],
            device_id=to,
            device_id_type=MESH,
        )

    def x_copy(d, cls):
        return remote(coded.at[d - 1, cls], xrecv.at[d - 1, cls], (d - 1) * 4 + cls, at(d, 0))

    def x_scale(d):
        return remote(scale_src.at[d - 1], scale_dst.at[d - 1], 12 + d - 1, at(d, 0))

    def near_copy(i):
        return remote(near_coded.at[i], lrecv.at[i], 15 + i, near_peers[i])

    def near_scale(i):
        return remote(scale_src.at[3 + i], scale_dst.at[3 + i], 18 + i, near_peers[i])

    def far_copy(i):
        return remote(far_coded.at[i], frecv.at[i], 21 + i, far_peers[i])

    def far_scale(i):
        return remote(scale_src.at[6 + i], scale_dst.at[6 + i], 24 + i, far_peers[i])

    classes = [lax.rem(z + d, 4) for d in (2, 1, 3, 0)]

    def grad_block(d):
        block = lax.rem(x + d, NX)

        def grad_tile(i, peak):
            rows = pl.ds(pl.multiple_of(block * BLOCK + i * 4 * ROWS, 32), 4 * ROWS)
            term = jnp.dot(masked_t[rows, :], dpre[...], preferred_element_type=F32)
            for j in range(4):
                slot = term[j * ROWS : (j + 1) * ROWS]
                partial[d, j, i] = slot
                peak = jnp.maximum(peak, peak_of(slot))
            return peak

        peak = lax.fori_loop(0, NZ // 4, grad_tile, jnp.zeros((8, COLS), F32))
        if d:
            scale = scale_of(peak)
            scale_src[d - 1] = pack(scale * (1.0 / 32767))
            x_scale(d).start()
            inverses[d - 1] = jnp.broadcast_to(32767.0 / scale, (8, COLS))

    def send_class(d, cls):
        inverse = inverses[d - 1][:1]

        def encode_slot(j, _):
            coded[d - 1, cls, j] = encode(partial[d, cls, j], inverse)
            return 0

        lax.fori_loop(0, 4, encode_slot, 0)
        x_copy(d, cls).start()

    for d in (2, 1, 3):
        grad_block(d)
        send_class(d, classes[0])
    grad_block(0)
    for cls in classes[1:]:
        for d in (2, 1, 3):
            send_class(d, cls)

    for d in (1, 2, 3):
        x_scale(d).wait_recv()
    scales = [unpack(scale_dst[i]) for i in range(3)]
    for n, cls in enumerate(classes):
        for d in (2, 1, 3):
            x_copy(d, cls).wait_recv()

        def add_x(j, peak, cls=cls):
            term = partial[0, cls, j]
            for i in range(3):
                term = term + decode(xrecv[i, cls, j], scales[i])
            summed[j] = term
            return jnp.maximum(peak, peak_of(term))

        peak = lax.fori_loop(0, 4, add_x, jnp.zeros((8, COLS), F32))
        if n < 3:
            i = (2, 0, 1)[n]
            scale = scale_of(peak)
            scale_src[3 + i] = pack(scale * (1.0 / 32767))
            near_scale(i).start()
            inverse = 32767.0 / scale

            def encode_near(j, _, i=i, inverse=inverse):
                near_coded[i, j] = encode(summed[j], inverse)
                return 0

            lax.fori_loop(0, 4, encode_near, 0)
            near_copy(i).start()

    for i in range(3):
        near_scale(i).wait_recv()
    scales = [unpack(scale_dst[3 + i]) for i in range(3)]
    for i in (0, 1, 2):
        near_copy(i).wait_recv()
    for d in (2, 1, 3, 0):
        j = lax.rem(lax.div(z, 4) + d, 4)
        grad = summed[j]
        for i in range(3):
            grad = grad + decode(lrecv[i, j], scales[i])
        if d:
            scale = scale_of(peak_of(grad))
            scale_src[6 + d - 1] = pack(scale * (1.0 / 32767))
            far_scale(d - 1).start()
            far_coded[d - 1] = encode(grad, 32767.0 / scale)
            far_copy(d - 1).start()
    for i in range(3):
        far_scale(i).wait_recv()
        far_copy(i).wait_recv()
        grad = grad + decode(frecv[i], unpack(scale_dst[6 + i]))

    peak = scale_of(peak_of(grad))
    nbuf[dp] = encode(grad, 32767.0 / peak)
    regather = Gather(nbuf, ag2_send, ag2_recv, x, z, mp)
    regather.start()
    squared = grad * grad
    row_lanes = squared[:, :128]
    for i in range(1, COLS // 128):
        row_lanes = row_lanes + squared[:, i * 128 : (i + 1) * 128]
    row_src[...] = row_lanes

    def row_copy(i):
        return pltpu.make_async_remote_copy(
            src_ref=row_src,
            dst_ref=row_dst.at[i - 1],
            send_sem=row_send.at[i - 1],
            recv_sem=row_recv.at[i - 1],
            device_id=plane(i),
            device_id_type=MESH,
        )

    def z_copy(d):
        return pltpu.make_async_remote_copy(
            src_ref=vec.at[0],
            dst_ref=vec_z.at[d - 1],
            send_sem=z_send.at[d - 1],
            recv_sem=z_recv.at[d - 1],
            device_id=at(0, d),
            device_id_type=MESH,
        )

    def plane_copy(i):
        return pltpu.make_async_remote_copy(
            src_ref=vec.at[1],
            dst_ref=vec_p.at[i - 1],
            send_sem=p_send.at[i - 1],
            recv_sem=p_recv.at[i - 1],
            device_id=plane(i),
            device_id_type=MESH,
        )

    def each(low, high, act):
        for i in range(low, high):
            act(i)

    column = jnp.sum(squared, axis=0, keepdims=True)
    vec[0] = pack(column, jnp.sum(row_lanes, axis=0, keepdims=True), moment_lanes)
    each(1, NMP, lambda i: row_copy(i).start())
    each(1, NZ, lambda d: z_copy((d * 7) % NZ).start())
    events = regather.events()
    next(events)

    each(1, NMP, lambda i: row_copy(i).wait_recv())
    for i in range(NMP - 1):
        row_lanes = row_lanes + row_dst[i]
    row_total = jnp.sum(row_lanes, axis=1, keepdims=True)
    retiles = Tiles(ntile, nt_send, nt_recv, x, z, mp)
    ntile[retiles.index(x, z)] = pack(peak * (1.0 / 32767), to_lanes(row_total))
    retiles.far()
    next(events)

    each(1, NZ, lambda d: z_copy(d).wait_recv())
    sums = vec[0]
    for i in range(NZ - 1):
        sums = sums + vec_z[i]
    vec[1] = sums
    each(1, NX * NMP, lambda i: plane_copy(i).start())
    retiles.near()
    next(events)
    retiles.across()
    next(events)

    each(1, NX * NMP, lambda i: plane_copy(i).wait_recv())
    norm = sums[6:7] + jnp.sum(vec_p[:, 6, :], axis=0, keepdims=True)
    for i in range(1, NX):
        sums = sums + vec_p[NMP * i - 1]
    col_total = unpack(sums)
    total = jnp.sum(norm, axis=1, keepdims=True)
    moments = jnp.sum(sums[7:8], axis=1, keepdims=True)

    clip = 1.0 / jnp.maximum(1.0, jnp.sqrt(total / (D * FF)))

    def next_row_state(old, squares):
        return decay_rate * old + (1.0 - decay_rate) * (clip * clip * squares / FF + epsilon)

    row_state = next_row_state(moment, row_total)
    col_state = decay_rate * cmom_ref[...].reshape(1, COLS) + (1.0 - decay_rate) * (clip * clip * col_total / D + epsilon)
    row_mean = decay_rate * moments / D + (1.0 - decay_rate) * (clip * clip * (total / FF) / D + epsilon)
    col_factor = step_rate * clip * lax.rsqrt(col_state)
    new_ref[...] = master_ref[...] - grad * (lax.rsqrt(row_state / row_mean) * col_factor)
    rstate_ref[...] = to_lanes(row_state)[:, :ROWS].reshape(ROWS)
    cstate_ref[...] = col_state.reshape(COLS)
    retiles.arrived(6)

    def updated(slot):
        old, tile = weights(slot)
        retile = ntile[retiles.index(lax.div(slot, NZ), lax.rem(slot, NZ))]
        row_factor = to_rows(lax.rsqrt(next_row_state(tile[6:7], retile[6:7]) / row_mean))
        return old - raw(nbuf[slot]) * (unpack(retile) * col_factor) * row_factor

    def leave(d):
        rows = pl.ds(pl.multiple_of(lax.rem(x + d, NX) * BLOCK, BLOCK), BLOCK)
        return pltpu.make_async_copy(low.at[rows], low_ref.at[rows], load_sem.at[2 + d])

    for d in (0, 1, 3, 2):
        block = lax.rem(x + d, NX)
        if d:
            regather.wait_block(d)

        def update_pair(i, _, block=block):
            slot = block * NZ + 2 * i
            rows = pl.ds(pl.multiple_of(slot * ROWS, 2 * ROWS), 2 * ROWS)
            low[rows, :] = stack(updated(slot), updated(slot + 1))
            return 0

        lax.fori_loop(0, NZ // 2, update_pair, 0)
        leave(d).start()
    tiles.finish()
    retiles.finish()
    each(1, NMP, lambda i: row_copy(i).wait_send())
    each(1, NZ, lambda d: z_copy(d).wait_send())
    each(1, NX * NMP, lambda i: plane_copy(i).wait_send())
    gather.finish()
    regather.finish()
    for d in (1, 2, 3):
        x_scale(d).wait_send()
        for cls in range(4):
            x_copy(d, cls).wait_send()
    for i in range(3):
        near_scale(i).wait_send()
        near_copy(i).wait_send()
        far_scale(i).wait_send()
        far_copy(i).wait_send()
    for d in range(NX):
        leave(d).wait()


def copy_kernel(*refs):
    count = len(refs) // 2
    sources, targets, sem = refs[:count], refs[count : 2 * count], refs[-1]
    copies = [pltpu.make_async_copy(a, b, sem.at[i]) for i, (a, b) in enumerate(zip(sources, targets))]
    for copy in copies:
        copy.start()
    for copy in copies:
        copy.wait()


def per_device(features, frame_start, chan_start, master_weight, row_moment, col_moment, out_grad):
    vmem = pl.BlockSpec(memory_space=pltpu.VMEM)
    smem = pl.BlockSpec(memory_space=pltpu.SMEM)
    out_shape = (
        jax.ShapeDtypeStruct((ROWS, COLS), F32),
        jax.ShapeDtypeStruct((ROWS,), F32),
        jax.ShapeDtypeStruct((COLS,), F32),
        jax.ShapeDtypeStruct((D, COLS), BF16),
    )
    anywhere = pl.BlockSpec(memory_space=pl.ANY)
    results = pl.pallas_call(
        kernel,
        name="adafactor_step",
        out_shape=out_shape,
        in_specs=[smem, smem, anywhere, vmem, vmem, vmem, anywhere],
        out_specs=(vmem, vmem, vmem, anywhere),
        scratch_shapes=[
            pltpu.VMEM((NX * NZ, 2 * ROWS, HALF), I16),
            pltpu.VMEM((NX * NZ, 8, 128), F32),
            pltpu.VMEM((D, COLS), BF16),
            pltpu.VMEM((NX * NZ, 2 * ROWS, HALF), I16),
            pltpu.VMEM((NX * NZ, 8, 128), F32),
            pltpu.VMEM((D, COLS), BF16),
            pltpu.VMEM((TOK, D), BF16),
            pltpu.VMEM((TOK, COLS), BF16),
            pltpu.VMEM((TOK, D), BF16),
            pltpu.VMEM((D, TOK), BF16),
            pltpu.VMEM((TOK, COLS), F32),
            pltpu.VMEM((TOK, COLS), BF16),
            pltpu.VMEM((NX, 4, 4, ROWS, COLS), F32),
            pltpu.VMEM((NX - 1, 8, COLS), F32),
            pltpu.VMEM((NX - 1, 4, 4, 2 * ROWS, HALF), I16),
            pltpu.VMEM((NX - 1, 4, 4, 2 * ROWS, HALF), I16),
            pltpu.VMEM((4, ROWS, COLS), F32),
            pltpu.VMEM((3, 4, 2 * ROWS, HALF), I16),
            pltpu.VMEM((3, 4, 2 * ROWS, HALF), I16),
            pltpu.VMEM((3, 2 * ROWS, HALF), I16),
            pltpu.VMEM((3, 2 * ROWS, HALF), I16),
            pltpu.VMEM((9, 8, 128), F32),
            pltpu.VMEM((9, 8, 128), F32),
            pltpu.VMEM((ROWS, 128), F32),
            pltpu.VMEM((NMP - 1, ROWS, 128), F32),
            pltpu.VMEM((2, 8, 128), F32),
            pltpu.VMEM((NZ - 1, 8, 128), F32),
            pltpu.VMEM((NX * NMP - 1, 8, 128), F32),
            pltpu.SemaphoreType.DMA((NX * NZ,)),
            pltpu.SemaphoreType.DMA((NX * NZ,)),
            pltpu.SemaphoreType.DMA((NX * NZ,)),
            pltpu.SemaphoreType.DMA((NX * NZ,)),
            pltpu.SemaphoreType.DMA((27,)),
            pltpu.SemaphoreType.DMA((27,)),
            pltpu.SemaphoreType.DMA((NMP - 1,)),
            pltpu.SemaphoreType.DMA((NMP - 1,)),
            pltpu.SemaphoreType.DMA((NZ - 1,)),
            pltpu.SemaphoreType.DMA((NZ - 1,)),
            pltpu.SemaphoreType.DMA((NX * NMP - 1,)),
            pltpu.SemaphoreType.DMA((NX * NMP - 1,)),
            pltpu.SemaphoreType.DMA((9,)),
            pltpu.SemaphoreType.DMA((9,)),
            pltpu.SemaphoreType.DMA((9,)),
            pltpu.SemaphoreType.DMA((9,)),
            pltpu.SemaphoreType.DMA((2 + NX,)),
        ],
        compiler_params=pltpu.CompilerParams(collective_id=0, has_side_effects=True, vmem_limit_bytes=56 * 2**20),
    )(frame_start, chan_start, features, master_weight, row_moment, col_moment, out_grad)

    return pl.pallas_call(
        copy_kernel,
        name="results",
        out_shape=out_shape,
        in_specs=[anywhere] * 4,
        out_specs=(anywhere,) * 4,
        scratch_shapes=[pltpu.SemaphoreType.DMA((4,))],
        compiler_params=pltpu.CompilerParams(vmem_limit_bytes=60 * 2**20),
    )(*results)


def solution(mesh):
    placed = (P("dp", None), P("dp"), P("dp"), P("dp", "mp"), P("dp"), P("mp"), P("dp", "mp"))
    return jax.shard_map(
        per_device,
        mesh=mesh,
        in_specs=placed,
        out_specs=(P("dp", "mp"), P("dp"), P("mp"), P(None, "mp")),
        check_vma=False,
    )
```

```python
import functools

import jax
import jax.numpy as jnp
from jax import lax
from jax.experimental import pallas as pl
from jax.experimental.pallas import tpu as pltpu
from jax.sharding import PartitionSpec as P

D = 1536
FF = 6144
TMASK = 128
FMASK = 192
NX = 4
NZ = 16
NMP = 8
TOK = 512
ROWS = D // (NX * NZ)
COLS = FF // NMP
HALF = COLS // 2
BLOCK = ROWS * NZ

epsilon = 1e-06
decay_rate = 0.8
step_rate = 0.01

MESH = pl.DeviceIdType.MESH
F32 = jnp.float32
BF16 = jnp.bfloat16
I16 = jnp.int16


def fold(rows):
    return jnp.concatenate([rows[:, :HALF], rows[:, HALF:]], axis=0)


class Gather:
    def __init__(self, buf, send_sem, recv_sem, x, z, mp):
        self.buf, self.send_sem, self.recv_sem = buf, send_sem, recv_sem
        self.x, self.z, self.mp = x, z, mp
        self.up, self.down = lax.rem(x + 1, NX), lax.rem(x + NX - 1, NX)
        self.line = [lax.rem(z + o, NZ) for o in range(NZ)]
        odd = lax.rem(z, 2)
        self.relay_from = [self.down + (self.up - self.down) * p for p in (odd, 1 - odd)]
        self.relay_to = [self.up + (self.down - self.up) * p for p in (odd, 1 - odd)]
        self.sent = 0

    def copy(self, slot, k, x, z):
        return pltpu.make_async_remote_copy(
            src_ref=self.buf.at[slot],
            dst_ref=self.buf.at[slot],
            send_sem=self.send_sem.at[k],
            recv_sem=self.recv_sem.at[slot],
            device_id=(x * NZ + z, self.mp),
            device_id_type=MESH,
        )

    def send(self, slot, x, z):
        self.copy(slot, self.sent, x, z).start()
        self.sent += 1

    def slot(self, o):
        return self.x * NZ + self.line[o]

    def arrived(self, slot):
        self.copy(slot, 0, self.x, self.z).wait_recv()

    def along_x(self, o):
        self.send(self.slot(o), self.up, self.z)
        self.send(self.slot(o), self.down, self.z)

    def near(self, o):
        for d in (2, 1, 15):
            self.send(self.slot(o), self.x, self.line[d])

    def relay(self, o):
        slot = self.relay_from[o % 2] * NZ + self.line[o]
        self.arrived(slot)
        self.send(slot, self.relay_to[o % 2], self.z)

    def start(self):
        for d in (8, 4, 12):
            self.send(self.slot(0), self.x, self.line[d])
        self.near(0)
        self.along_x(0)

    def far(self, o):
        self.arrived(self.slot(o))
        self.near(o)
        self.along_x(o)

    def pass_on(self, *offsets):
        for o in offsets:
            self.arrived(self.slot(o))
            self.along_x(o)

    def relays(self, *offsets):
        for o in offsets:
            self.relay(o)

    def events(self):
        self.pass_on(15, 1, 14)
        self.relays(0)
        yield
        self.far(4)
        self.far(12)
        self.relays(15, 1, 14)
        self.far(8)
        self.relays(4, 12)
        yield
        self.pass_on(3, 5, 2, 11, 13, 10)
        self.relays(8)
        self.pass_on(7, 9, 6)
        yield
        self.relays(3, 5, 2, 11, 13, 10, 7, 9, 6)
        yield

    def wait_block(self, d):
        x = lax.rem(self.x + d, NX)

        def step(i, _):
            if d == 2:
                owner = i
            else:
                owner = 2 * i + (0 if d == 1 else 1)
            self.arrived(x * NZ + owner)
            return 0

        lax.fori_loop(0, NZ if d == 2 else NZ // 2, step, 0)

    def finish(self):
        def step(k, _):
            self.copy(0, k, self.x, self.z).wait_send()
            return 0

        lax.fori_loop(0, NX * NZ - 1, step, 0)


class Tiles:
    def __init__(self, buf, send_sem, recv_sem, x, z, mp):
        self.buf, self.send_sem, self.recv_sem = buf, send_sem, recv_sem
        self.x, self.z, self.mp = x, z, mp
        self.sent = []

    def index(self, x, z):
        return x * NZ + lax.rem(z, 4) * 4 + lax.div(z, 4)

    def round(self, first, count, k, peers):
        for i, peer in enumerate(peers):
            block = self.buf.at[pl.ds(first, count)]
            copy = pltpu.make_async_remote_copy(
                src_ref=block,
                dst_ref=block,
                send_sem=self.send_sem.at[k + i],
                recv_sem=self.recv_sem.at[k + i],
                device_id=peer,
                device_id_type=MESH,
            )
            copy.start()
            self.sent.append(copy)

    def arrived(self, k):
        for copy in self.sent[k : k + 3]:
            copy.wait_recv()

    def along(self, distances):
        return [(self.x * NZ + lax.rem(self.z + d, NZ), self.mp) for d in distances]

    def far(self):
        self.round(self.index(self.x, self.z), 1, 0, self.along((8, 4, 12)))

    def near(self):
        self.arrived(0)
        self.round(self.x * NZ + lax.rem(self.z, 4) * 4, 4, 3, self.along((2, 1, 15)))

    def across(self):
        self.arrived(3)
        peers = [(lax.rem(self.x + d, NX) * NZ + self.z, self.mp) for d in (2, 1, 3)]
        self.round(self.x * NZ, NZ, 6, peers)

    def finish(self):
        for copy in self.sent:
            copy.wait_send()


def stack(first, second):
    return jnp.concatenate([first, second], axis=0).astype(BF16)


def unfold(slot):
    return jnp.concatenate([slot[:ROWS], slot[ROWS:]], axis=1)


def pack(row, *more):
    pieces = [row[:, i * 128 : (i + 1) * 128] for i in range(COLS // 128)] + list(more)
    if len(pieces) < 8:
        pieces.append(jnp.zeros((8 - len(pieces), 128), F32))
    return jnp.concatenate(pieces, axis=0)


def raw(slot):
    return unfold(slot.astype(jnp.int32).astype(F32))


def unpack(tile):
    return jnp.concatenate([tile[i : i + 1] for i in range(COLS // 128)], axis=1)


def peak_of(rows):
    size = jnp.abs(rows)
    return jnp.maximum(jnp.maximum(size[:8], size[8:16]), size[16:24])


def scale_of(peak):
    return jnp.maximum(jnp.max(peak, axis=0, keepdims=True), 1e-30)


def encode(rows, inverse):
    return jnp.round(fold(rows * inverse)).astype(jnp.int32).astype(I16)


def decode(slot, scale):
    return raw(slot) * scale


def kernel(
    frame_ref, chan_ref, feat_hbm, master_ref, rmom_ref, cmom_ref, grad_hbm,
    new_ref, rstate_ref, cstate_ref, low_ref,
    wbuf, wtile, weight, nbuf, ntile, low, feat, grad_in, masked, masked_t, pre, dpre,
    partial, inverses, coded, xrecv, summed, near_coded, lrecv, far_coded, frecv, scale_src, scale_dst,
    row_src, row_dst, vec, vec_z, vec_p,
    ag_send, ag_recv, ag2_send, ag2_recv, rs_send, rs_recv, row_send, row_recv, z_send, z_recv, p_send, p_recv, wt_send, wt_recv, nt_send, nt_recv, load_sem,
):
    dp, mp = lax.axis_index("dp"), lax.axis_index("mp")
    x, z = lax.div(dp, NZ), lax.rem(dp, NZ)

    def at(dx, dz):
        return (lax.rem(x + dx, NX) * NZ + lax.rem(z + dz, NZ), mp)

    near_peers = [at(0, d) for d in (1, NZ - 1, 2)]
    far_peers = [at(0, d) for d in (4, 8, 12)]

    def plane(i):
        return (lax.rem(x + i // NMP, NX) * NZ + z, lax.rem(mp + i % NMP, NMP))

    barrier = pltpu.get_barrier_semaphore()

    greeted = [at(0, d) for d in range(1, NZ)] + [plane(i) for i in range(1, NX * NMP)]
    for peer in greeted:
        pl.semaphore_signal(barrier, inc=1, device_id=peer, device_id_type=MESH)

    load_feat = pltpu.make_async_copy(feat_hbm, feat, load_sem.at[0])
    load_grad = pltpu.make_async_copy(grad_hbm, grad_in, load_sem.at[1])
    load_feat.start()
    load_grad.start()

    master = master_ref[...]
    peak = jnp.max(scale_of(peak_of(master)), axis=1, keepdims=True)
    diag = lax.broadcasted_iota(jnp.int32, (ROWS, 128), 0) == lax.broadcasted_iota(jnp.int32, (ROWS, 128), 1)

    def to_lanes(column):
        return jnp.sum(jnp.where(diag, column, 0.0), axis=0, keepdims=True)

    def to_rows(lanes):
        return jnp.sum(jnp.where(diag, lanes, 0.0), axis=1, keepdims=True)

    moment_lanes = jnp.concatenate([rmom_ref[...].reshape(1, ROWS), jnp.zeros((1, 128 - ROWS), F32)], axis=1)
    lane = lax.broadcasted_iota(jnp.int32, (1, 128), 1)
    wbuf[dp] = encode(master, 32767.0 / peak)
    tiles = Tiles(wtile, wt_send, wt_recv, x, z, mp)
    wtile[tiles.index(x, z)] = jnp.where(lane == 127, peak * (1.0 / 32767), moment_lanes)

    pl.semaphore_wait(barrier, len(greeted))
    tiles.far()
    gather = Gather(wbuf, ag_send, ag_recv, x, z, mp)
    gather.start()

    load_feat.wait()
    first_frame, first_chan = frame_ref[0], chan_ref[0]
    channel = lax.broadcasted_iota(jnp.int32, (1, D), 1)
    chan_keep = jnp.where((channel < first_chan) | (channel >= first_chan + FMASK), 1.0, 0.0)

    def mask_rows(i, _):
        rows = pl.ds(pl.multiple_of(i * 128, 128), 128)
        offset = lax.broadcasted_iota(jnp.int32, (128, 1), 0) + i * 128
        time_keep = jnp.where((offset < first_frame) | (offset >= first_frame + TMASK), 1.0, 0.0)
        kept = feat[rows, :] * (time_keep * chan_keep).astype(BF16)
        masked[rows, :] = kept
        masked_t[:, rows] = kept.T
        return 0

    lax.fori_loop(0, TOK // 128, mask_rows, 0)
    load_grad.wait()
    moment = to_rows(moment_lanes)
    for part, _ in enumerate(gather.events()):
        if part == 1:
            tiles.near()
        elif part == 2:
            tiles.across()
    tiles.arrived(6)

    def weights(slot):
        tile = wtile[tiles.index(lax.div(slot, NZ), lax.rem(slot, NZ))]
        return decode(wbuf[slot], tile[:, 127:128]), tile

    def weight_block(block):
        def step(i, _):
            slot = block * NZ + 2 * i
            rows = pl.ds(pl.multiple_of(slot * ROWS, 2 * ROWS), 2 * ROWS)
            weight[rows, :] = stack(weights(slot)[0], weights(slot + 1)[0])
            return 0

        lax.fori_loop(0, NZ // 2, step, 0)

    for d in (0, 1, 3, 2):
        block = lax.rem(x + d, NX)
        if d:
            gather.wait_block(d)
        weight_block(block)
        depth = pl.ds(pl.multiple_of(block * BLOCK, BLOCK), BLOCK)

        def forward_tile(i, _, d=d, depth=depth):
            cols = pl.ds(pl.multiple_of(i * 256, 256), 256)
            term = jnp.dot(masked[:, depth], weight[depth, cols], preferred_element_type=F32)
            if d == 0:
                pre[:, cols] = term
            else:
                total = pre[:, cols] + term
                if d != 2:
                    pre[:, cols] = total
                else:
                    s = jax.nn.sigmoid(total)
                    slope = s + total * s * (1.0 - s)
                    dpre[:, cols] = (grad_in[:, cols].astype(F32) * slope).astype(BF16)
            return 0

        lax.fori_loop(0, COLS // 256, forward_tile, 0)

    def remote(src, dst, i, to):
        return pltpu.make_async_remote_copy(
            src_ref=src,
            dst_ref=dst,
            send_sem=rs_send.at[i],
            recv_sem=rs_recv.at[i],
            device_id=to,
            device_id_type=MESH,
        )

    def x_copy(d, cls):
        return remote(coded.at[d - 1, cls], xrecv.at[d - 1, cls], (d - 1) * 4 + cls, at(d, 0))

    def x_scale(d):
        return remote(scale_src.at[d - 1], scale_dst.at[d - 1], 12 + d - 1, at(d, 0))

    def near_copy(i):
        return remote(near_coded.at[i], lrecv.at[i], 15 + i, near_peers[i])

    def near_scale(i):
        return remote(scale_src.at[3 + i], scale_dst.at[3 + i], 18 + i, near_peers[i])

    def far_copy(i):
        return remote(far_coded.at[i], frecv.at[i], 21 + i, far_peers[i])

    def far_scale(i):
        return remote(scale_src.at[6 + i], scale_dst.at[6 + i], 24 + i, far_peers[i])

    classes = [lax.rem(z + d, 4) for d in (2, 1, 3, 0)]

    def grad_block(d):
        block = lax.rem(x + d, NX)

        def grad_tile(i, peak):
            rows = pl.ds(pl.multiple_of(block * BLOCK + i * 4 * ROWS, 32), 4 * ROWS)
            term = jnp.dot(masked_t[rows, :], dpre[...], preferred_element_type=F32)
            for j in range(4):
                slot = term[j * ROWS : (j + 1) * ROWS]
                partial[d, j, i] = slot
                peak = jnp.maximum(peak, peak_of(slot))
            return peak

        peak = lax.fori_loop(0, NZ // 4, grad_tile, jnp.zeros((8, COLS), F32))
        if d:
            scale = scale_of(peak)
            scale_src[d - 1] = pack(scale * (1.0 / 32767))
            x_scale(d).start()
            inverses[d - 1] = jnp.broadcast_to(32767.0 / scale, (8, COLS))

    def send_class(d, cls):
        inverse = inverses[d - 1][:1]

        def encode_slot(j, _):
            coded[d - 1, cls, j] = encode(partial[d, cls, j], inverse)
            return 0

        lax.fori_loop(0, 4, encode_slot, 0)
        x_copy(d, cls).start()

    for d in (2, 1, 3):
        grad_block(d)
        send_class(d, classes[0])
    grad_block(0)
    for cls in classes[1:]:
        for d in (2, 1, 3):
            send_class(d, cls)

    for d in (1, 2, 3):
        x_scale(d).wait_recv()
    scales = [unpack(scale_dst[i]) for i in range(3)]
    for n, cls in enumerate(classes):
        for d in (2, 1, 3):
            x_copy(d, cls).wait_recv()

        def add_x(j, peak, cls=cls):
            term = partial[0, cls, j]
            for i in range(3):
                term = term + decode(xrecv[i, cls, j], scales[i])
            summed[j] = term
            return jnp.maximum(peak, peak_of(term))

        peak = lax.fori_loop(0, 4, add_x, jnp.zeros((8, COLS), F32))
        if n < 3:
            i = (2, 0, 1)[n]
            scale = scale_of(peak)
            scale_src[3 + i] = pack(scale * (1.0 / 32767))
            near_scale(i).start()
            inverse = 32767.0 / scale

            def encode_near(j, _, i=i, inverse=inverse):
                near_coded[i, j] = encode(summed[j], inverse)
                return 0

            lax.fori_loop(0, 4, encode_near, 0)
            near_copy(i).start()

    for i in range(3):
        near_scale(i).wait_recv()
    scales = [unpack(scale_dst[3 + i]) for i in range(3)]
    for i in (0, 1, 2):
        near_copy(i).wait_recv()
    for d in (2, 1, 3, 0):
        j = lax.rem(lax.div(z, 4) + d, 4)
        grad = summed[j]
        for i in range(3):
            grad = grad + decode(lrecv[i, j], scales[i])
        if d:
            scale = scale_of(peak_of(grad))
            scale_src[6 + d - 1] = pack(scale * (1.0 / 32767))
            far_scale(d - 1).start()
            far_coded[d - 1] = encode(grad, 32767.0 / scale)
            far_copy(d - 1).start()
    for i in range(3):
        far_scale(i).wait_recv()
        far_copy(i).wait_recv()
        grad = grad + decode(frecv[i], unpack(scale_dst[6 + i]))

    peak = scale_of(peak_of(grad))
    nbuf[dp] = encode(grad, 32767.0 / peak)
    regather = Gather(nbuf, ag2_send, ag2_recv, x, z, mp)
    regather.start()
    squared = grad * grad
    row_lanes = squared[:, :128]
    for i in range(1, COLS // 128):
        row_lanes = row_lanes + squared[:, i * 128 : (i + 1) * 128]
    row_src[...] = row_lanes

    def row_copy(i):
        return pltpu.make_async_remote_copy(
            src_ref=row_src,
            dst_ref=row_dst.at[i - 1],
            send_sem=row_send.at[i - 1],
            recv_sem=row_recv.at[i - 1],
            device_id=plane(i),
            device_id_type=MESH,
        )

    def z_copy(d):
        return pltpu.make_async_remote_copy(
            src_ref=vec.at[0],
            dst_ref=vec_z.at[d - 1],
            send_sem=z_send.at[d - 1],
            recv_sem=z_recv.at[d - 1],
            device_id=at(0, d),
            device_id_type=MESH,
        )

    def plane_copy(i):
        return pltpu.make_async_remote_copy(
            src_ref=vec.at[1],
            dst_ref=vec_p.at[i - 1],
            send_sem=p_send.at[i - 1],
            recv_sem=p_recv.at[i - 1],
            device_id=plane(i),
            device_id_type=MESH,
        )

    def each(low, high, act):
        for i in range(low, high):
            act(i)

    column = jnp.sum(squared, axis=0, keepdims=True)
    vec[0] = pack(column, jnp.sum(row_lanes, axis=0, keepdims=True), moment_lanes)
    each(1, NMP, lambda i: row_copy(i).start())
    each(1, NZ, lambda d: z_copy((d * 7) % NZ).start())
    events = regather.events()
    next(events)

    each(1, NMP, lambda i: row_copy(i).wait_recv())
    for i in range(NMP - 1):
        row_lanes = row_lanes + row_dst[i]
    row_total = jnp.sum(row_lanes, axis=1, keepdims=True)
    retiles = Tiles(ntile, nt_send, nt_recv, x, z, mp)
    ntile[retiles.index(x, z)] = pack(peak * (1.0 / 32767), to_lanes(row_total))
    retiles.far()
    next(events)

    each(1, NZ, lambda d: z_copy(d).wait_recv())
    sums = vec[0]
    for i in range(NZ - 1):
        sums = sums + vec_z[i]
    vec[1] = sums
    each(1, NX * NMP, lambda i: plane_copy(i).start())
    retiles.near()
    next(events)
    retiles.across()
    next(events)

    each(1, NX * NMP, lambda i: plane_copy(i).wait_recv())
    norm = sums[6:7] + jnp.sum(vec_p[:, 6, :], axis=0, keepdims=True)
    for i in range(1, NX):
        sums = sums + vec_p[NMP * i - 1]
    col_total = unpack(sums)
    total = jnp.sum(norm, axis=1, keepdims=True)
    moments = jnp.sum(sums[7:8], axis=1, keepdims=True)

    clip = 1.0 / jnp.maximum(1.0, jnp.sqrt(total / (D * FF)))

    def next_row_state(old, squares):
        return decay_rate * old + (1.0 - decay_rate) * (clip * clip * squares / FF + epsilon)

    row_state = next_row_state(moment, row_total)
    col_state = decay_rate * cmom_ref[...].reshape(1, COLS) + (1.0 - decay_rate) * (clip * clip * col_total / D + epsilon)
    row_mean = decay_rate * moments / D + (1.0 - decay_rate) * (clip * clip * (total / FF) / D + epsilon)
    col_factor = step_rate * clip * lax.rsqrt(col_state)
    new_ref[...] = master_ref[...] - grad * (lax.rsqrt(row_state / row_mean) * col_factor)
    rstate_ref[...] = to_lanes(row_state)[:, :ROWS].reshape(ROWS)
    cstate_ref[...] = col_state.reshape(COLS)
    retiles.arrived(6)

    def updated(slot):
        old, old_moment = weights(slot)
        retile = ntile[retiles.index(lax.div(slot, NZ), lax.rem(slot, NZ))]
        row_factor = to_rows(lax.rsqrt(next_row_state(old_moment, retile[6:7]) / row_mean))
        return old - raw(nbuf[slot]) * (unpack(retile) * col_factor) * row_factor

    def leave(d):
        rows = pl.ds(pl.multiple_of(lax.rem(x + d, NX) * BLOCK, BLOCK), BLOCK)
        return pltpu.make_async_copy(low.at[rows], low_ref.at[rows], load_sem.at[2 + d])

    for d in (0, 1, 3, 2):
        block = lax.rem(x + d, NX)
        if d:
            regather.wait_block(d)

        def update_pair(i, _, block=block):
            slot = block * NZ + 2 * i
            rows = pl.ds(pl.multiple_of(slot * ROWS, 2 * ROWS), 2 * ROWS)
            low[rows, :] = stack(updated(slot), updated(slot + 1))
            return 0

        lax.fori_loop(0, NZ // 2, update_pair, 0)
        leave(d).start()
    tiles.finish()
    retiles.finish()
    each(1, NMP, lambda i: row_copy(i).wait_send())
    each(1, NZ, lambda d: z_copy(d).wait_send())
    each(1, NX * NMP, lambda i: plane_copy(i).wait_send())
    gather.finish()
    regather.finish()
    for d in (1, 2, 3):
        x_scale(d).wait_send()
        for cls in range(4):
            x_copy(d, cls).wait_send()
    for i in range(3):
        near_scale(i).wait_send()
        near_copy(i).wait_send()
        far_scale(i).wait_send()
        far_copy(i).wait_send()
    for d in range(NX):
        leave(d).wait()


def copy_kernel(new_in, rstate_in, cstate_in, low_in, new_out, rstate_out, cstate_out, low_out, new, rstate, cstate, low, sem):
    pieces = 4
    size = D // pieces
    ways = [(low_in.at[pl.ds(i * size, size)], low.at[pl.ds(i * size, size)], low_out.at[pl.ds(i * size, size)]) for i in range(pieces)]
    ways += [(new_in, new, new_out), (rstate_in, rstate, rstate_out), (cstate_in, cstate, cstate_out)]
    come = [pltpu.make_async_copy(a, b, sem.at[0, i]) for i, (a, b, _) in enumerate(ways)]
    go = [pltpu.make_async_copy(b, c, sem.at[1, i]) for i, (_, b, c) in enumerate(ways)]
    for copy in come:
        copy.start()
    for first, second in zip(come, go):
        first.wait()
        second.start()
    for copy in go:
        copy.wait()


def per_device(features, frame_start, chan_start, master_weight, row_moment, col_moment, out_grad):
    vmem = pl.BlockSpec(memory_space=pltpu.VMEM)
    smem = pl.BlockSpec(memory_space=pltpu.SMEM)
    out_shape = (
        jax.ShapeDtypeStruct((ROWS, COLS), F32),
        jax.ShapeDtypeStruct((ROWS,), F32),
        jax.ShapeDtypeStruct((COLS,), F32),
        jax.ShapeDtypeStruct((D, COLS), BF16),
    )
    anywhere = pl.BlockSpec(memory_space=pl.ANY)
    results = pl.pallas_call(
        kernel,
        name="adafactor_step",
        out_shape=out_shape,
        in_specs=[smem, smem, anywhere, vmem, vmem, vmem, anywhere],
        out_specs=(vmem, vmem, vmem, anywhere),
        scratch_shapes=[
            pltpu.VMEM((NX * NZ, 2 * ROWS, HALF), I16),
            pltpu.VMEM((NX * NZ, 1, 128), F32),
            pltpu.VMEM((D, COLS), BF16),
            pltpu.VMEM((NX * NZ, 2 * ROWS, HALF), I16),
            pltpu.VMEM((NX * NZ, 8, 128), F32),
            pltpu.VMEM((D, COLS), BF16),
            pltpu.VMEM((TOK, D), BF16),
            pltpu.VMEM((TOK, COLS), BF16),
            pltpu.VMEM((TOK, D), BF16),
            pltpu.VMEM((D, TOK), BF16),
            pltpu.VMEM((TOK, COLS), F32),
            pltpu.VMEM((TOK, COLS), BF16),
            pltpu.VMEM((NX, 4, 4, ROWS, COLS), F32),
            pltpu.VMEM((NX - 1, 8, COLS), F32),
            pltpu.VMEM((NX - 1, 4, 4, 2 * ROWS, HALF), I16),
            pltpu.VMEM((NX - 1, 4, 4, 2 * ROWS, HALF), I16),
            pltpu.VMEM((4, ROWS, COLS), F32),
            pltpu.VMEM((3, 4, 2 * ROWS, HALF), I16),
            pltpu.VMEM((3, 4, 2 * ROWS, HALF), I16),
            pltpu.VMEM((3, 2 * ROWS, HALF), I16),
            pltpu.VMEM((3, 2 * ROWS, HALF), I16),
            pltpu.VMEM((9, 8, 128), F32),
            pltpu.VMEM((9, 8, 128), F32),
            pltpu.VMEM((ROWS, 128), F32),
            pltpu.VMEM((NMP - 1, ROWS, 128), F32),
            pltpu.VMEM((2, 8, 128), F32),
            pltpu.VMEM((NZ - 1, 8, 128), F32),
            pltpu.VMEM((NX * NMP - 1, 8, 128), F32),
            pltpu.SemaphoreType.DMA((NX * NZ,)),
            pltpu.SemaphoreType.DMA((NX * NZ,)),
            pltpu.SemaphoreType.DMA((NX * NZ,)),
            pltpu.SemaphoreType.DMA((NX * NZ,)),
            pltpu.SemaphoreType.DMA((27,)),
            pltpu.SemaphoreType.DMA((27,)),
            pltpu.SemaphoreType.DMA((NMP - 1,)),
            pltpu.SemaphoreType.DMA((NMP - 1,)),
            pltpu.SemaphoreType.DMA((NZ - 1,)),
            pltpu.SemaphoreType.DMA((NZ - 1,)),
            pltpu.SemaphoreType.DMA((NX * NMP - 1,)),
            pltpu.SemaphoreType.DMA((NX * NMP - 1,)),
            pltpu.SemaphoreType.DMA((9,)),
            pltpu.SemaphoreType.DMA((9,)),
            pltpu.SemaphoreType.DMA((9,)),
            pltpu.SemaphoreType.DMA((9,)),
            pltpu.SemaphoreType.DMA((2 + NX,)),
        ],
        compiler_params=pltpu.CompilerParams(collective_id=0, has_side_effects=True, vmem_limit_bytes=56 * 2**20),
    )(frame_start, chan_start, features, master_weight, row_moment, col_moment, out_grad)

    return pl.pallas_call(
        copy_kernel,
        name="results",
        out_shape=out_shape,
        in_specs=[anywhere] * 4,
        out_specs=(anywhere,) * 4,
        scratch_shapes=[pltpu.VMEM(out.shape, out.dtype) for out in out_shape] + [pltpu.SemaphoreType.DMA((2, 7))],
        compiler_params=pltpu.CompilerParams(vmem_limit_bytes=60 * 2**20),
    )(*results)


def solution(mesh):
    placed = (P("dp", None), P("dp"), P("dp"), P("dp", "mp"), P("dp"), P("mp"), P("dp", "mp"))
    return jax.shard_map(
        per_device,
        mesh=mesh,
        in_specs=placed,
        out_specs=(P("dp", "mp"), P("dp"), P("mp"), P(None, "mp")),
        check_vma=False,
    )
```

```python
import functools

import jax
import jax.numpy as jnp
from jax import lax
from jax.experimental import pallas as pl
from jax.experimental.pallas import tpu as pltpu
from jax.sharding import PartitionSpec as P

D = 1536
FF = 6144
TMASK = 128
FMASK = 192
NX = 4
NZ = 16
NMP = 8
TOK = 512
ROWS = D // (NX * NZ)
COLS = FF // NMP
HALF = COLS // 2
BLOCK = ROWS * NZ

epsilon = 1e-06
decay_rate = 0.8
step_rate = 0.01

MESH = pl.DeviceIdType.MESH
F32 = jnp.float32
BF16 = jnp.bfloat16
I16 = jnp.int16


def fold(rows):
    return jnp.concatenate([rows[:, :HALF], rows[:, HALF:]], axis=0)


class Gather:
    def __init__(self, buf, send_sem, recv_sem, x, z, mp):
        self.buf, self.send_sem, self.recv_sem = buf, send_sem, recv_sem
        self.x, self.z, self.mp = x, z, mp
        self.up, self.down = lax.rem(x + 1, NX), lax.rem(x + NX - 1, NX)
        self.line = [lax.rem(z + o, NZ) for o in range(NZ)]
        odd = lax.rem(z, 2)
        self.relay_from = [self.down + (self.up - self.down) * p for p in (odd, 1 - odd)]
        self.relay_to = [self.up + (self.down - self.up) * p for p in (odd, 1 - odd)]
        self.sent = 0

    def copy(self, slot, k, x, z):
        return pltpu.make_async_remote_copy(
            src_ref=self.buf.at[slot],
            dst_ref=self.buf.at[slot],
            send_sem=self.send_sem.at[k],
            recv_sem=self.recv_sem.at[slot],
            device_id=(x * NZ + z, self.mp),
            device_id_type=MESH,
        )

    def send(self, slot, x, z):
        self.copy(slot, self.sent, x, z).start()
        self.sent += 1

    def slot(self, o):
        return self.x * NZ + self.line[o]

    def arrived(self, slot):
        self.copy(slot, 0, self.x, self.z).wait_recv()

    def along_x(self, o):
        self.send(self.slot(o), self.up, self.z)
        self.send(self.slot(o), self.down, self.z)

    def near(self, o):
        for d in (2, 1, 15):
            self.send(self.slot(o), self.x, self.line[d])

    def relay(self, o):
        slot = self.relay_from[o % 2] * NZ + self.line[o]
        self.arrived(slot)
        self.send(slot, self.relay_to[o % 2], self.z)

    def start(self):
        for d in (8, 4, 12):
            self.send(self.slot(0), self.x, self.line[d])
        self.near(0)
        self.along_x(0)

    def far(self, o):
        self.arrived(self.slot(o))
        self.near(o)
        self.along_x(o)

    def pass_on(self, *offsets):
        for o in offsets:
            self.arrived(self.slot(o))
            self.along_x(o)

    def relays(self, *offsets):
        for o in offsets:
            self.relay(o)

    def events(self):
        self.pass_on(15, 1, 14)
        self.relays(0)
        yield
        self.far(4)
        self.far(12)
        self.relays(15, 1, 14)
        self.far(8)
        self.relays(4, 12)
        yield
        self.pass_on(3, 5, 2, 11, 13, 10)
        self.relays(8)
        self.pass_on(7, 9, 6)
        yield
        self.relays(3, 5, 2, 11, 13, 10, 7, 9, 6)
        yield

    def wait_block(self, d):
        x = lax.rem(self.x + d, NX)

        def step(i, _):
            if d == 2:
                owner = i
            else:
                owner = 2 * i + (0 if d == 1 else 1)
            self.arrived(x * NZ + owner)
            return 0

        lax.fori_loop(0, NZ if d == 2 else NZ // 2, step, 0)

    def finish(self):
        def step(k, _):
            self.copy(0, k, self.x, self.z).wait_send()
            return 0

        lax.fori_loop(0, NX * NZ - 1, step, 0)


class Tiles:
    def __init__(self, buf, send_sem, recv_sem, x, z, mp):
        self.buf, self.send_sem, self.recv_sem = buf, send_sem, recv_sem
        self.x, self.z, self.mp = x, z, mp
        self.sent = []

    def index(self, x, z):
        return x * NZ + lax.rem(z, 4) * 4 + lax.div(z, 4)

    def round(self, first, count, k, peers):
        for i, peer in enumerate(peers):
            block = self.buf.at[pl.ds(first, count)]
            copy = pltpu.make_async_remote_copy(
                src_ref=block,
                dst_ref=block,
                send_sem=self.send_sem.at[k + i],
                recv_sem=self.recv_sem.at[k + i],
                device_id=peer,
                device_id_type=MESH,
            )
            copy.start()
            self.sent.append(copy)

    def arrived(self, k):
        for copy in self.sent[k : k + 3]:
            copy.wait_recv()

    def along(self, distances):
        return [(self.x * NZ + lax.rem(self.z + d, NZ), self.mp) for d in distances]

    def far(self):
        self.round(self.index(self.x, self.z), 1, 0, self.along((8, 4, 12)))

    def near(self):
        self.arrived(0)
        self.round(self.x * NZ + lax.rem(self.z, 4) * 4, 4, 3, self.along((2, 1, 15)))

    def across(self):
        self.arrived(3)
        peers = [(lax.rem(self.x + d, NX) * NZ + self.z, self.mp) for d in (2, 1, 3)]
        self.round(self.x * NZ, NZ, 6, peers)

    def finish(self):
        for copy in self.sent:
            copy.wait_send()


def stack(first, second):
    return jnp.concatenate([first, second], axis=0).astype(BF16)


def unfold(slot):
    return jnp.concatenate([slot[:ROWS], slot[ROWS:]], axis=1)


def pack(row, *more):
    pieces = [row[:, i * 128 : (i + 1) * 128] for i in range(COLS // 128)] + list(more)
    if len(pieces) < 8:
        pieces.append(jnp.zeros((8 - len(pieces), 128), F32))
    return jnp.concatenate(pieces, axis=0)


def raw(slot):
    return unfold(slot.astype(jnp.int32).astype(F32))


def unpack(tile):
    return jnp.concatenate([tile[i : i + 1] for i in range(COLS // 128)], axis=1)


def peak_of(rows):
    size = jnp.abs(rows)
    return jnp.maximum(jnp.maximum(size[:8], size[8:16]), size[16:24])


def scale_of(peak):
    return jnp.maximum(jnp.max(peak, axis=0, keepdims=True), 1e-30)


def encode(rows, inverse):
    return jnp.round(fold(rows * inverse)).astype(jnp.int32).astype(I16)


def decode(slot, scale):
    return raw(slot) * scale


def kernel(
    frame_ref, chan_ref, feat_hbm, master_ref, rmom_ref, cmom_ref, grad_hbm,
    new_ref, rstate_ref, cstate_ref, low_ref,
    wbuf, wtile, weight, nbuf, ntile, low, feat, grad_in, masked, masked_t, pre, dpre,
    partial, inverses, coded, xrecv, summed, near_coded, lrecv, far_coded, frecv, scale_src, scale_dst,
    row_src, row_dst, vec, vec_in,
    ag_send, ag_recv, ag2_send, ag2_recv, rs_send, rs_recv, row_send, row_recv, vec_send, vec_recv, wt_send, wt_recv, nt_send, nt_recv, load_sem,
):
    dp, mp = lax.axis_index("dp"), lax.axis_index("mp")
    x, z = lax.div(dp, NZ), lax.rem(dp, NZ)

    def at(dx, dz):
        return (lax.rem(x + dx, NX) * NZ + lax.rem(z + dz, NZ), mp)

    x_peers = [at(d, 0) for d in (1, 2, 3)]
    near_peers = [at(0, d) for d in (1, NZ - 1, 2)]
    far_peers = [at(0, d) for d in (4, 8, 12)]
    mp_peers = [(dp, lax.rem(mp + d, NMP)) for d in range(1, NMP)]

    barrier = pltpu.get_barrier_semaphore()
    greeted = far_peers + near_peers + [at(0, NZ - 2)] + x_peers + mp_peers
    for peer in greeted:
        pl.semaphore_signal(barrier, inc=1, device_id=peer, device_id_type=MESH)

    load_feat = pltpu.make_async_copy(feat_hbm, feat, load_sem.at[0])
    load_grad = pltpu.make_async_copy(grad_hbm, grad_in, load_sem.at[1])
    load_feat.start()
    load_grad.start()

    master = master_ref[...]
    peak = jnp.max(scale_of(peak_of(master)), axis=1, keepdims=True)
    diag = lax.broadcasted_iota(jnp.int32, (ROWS, 128), 0) == lax.broadcasted_iota(jnp.int32, (ROWS, 128), 1)

    def to_lanes(column):
        return jnp.sum(jnp.where(diag, column, 0.0), axis=0, keepdims=True)

    def to_rows(lanes):
        return jnp.sum(jnp.where(diag, lanes, 0.0), axis=1, keepdims=True)

    moment_lanes = jnp.concatenate([rmom_ref[...].reshape(1, ROWS), jnp.zeros((1, 128 - ROWS), F32)], axis=1)
    lane = lax.broadcasted_iota(jnp.int32, (1, 128), 1)
    wbuf[dp] = encode(master, 32767.0 / peak)
    tiles = Tiles(wtile, wt_send, wt_recv, x, z, mp)
    wtile[tiles.index(x, z)] = jnp.where(lane == 127, peak * (1.0 / 32767), moment_lanes)

    pl.semaphore_wait(barrier, len(greeted))
    tiles.far()
    gather = Gather(wbuf, ag_send, ag_recv, x, z, mp)
    gather.start()

    load_feat.wait()
    first_frame, first_chan = frame_ref[0], chan_ref[0]
    channel = lax.broadcasted_iota(jnp.int32, (1, D), 1)
    chan_keep = jnp.where((channel < first_chan) | (channel >= first_chan + FMASK), 1.0, 0.0)

    def mask_rows(i, _):
        rows = pl.ds(pl.multiple_of(i * 128, 128), 128)
        offset = lax.broadcasted_iota(jnp.int32, (128, 1), 0) + i * 128
        time_keep = jnp.where((offset < first_frame) | (offset >= first_frame + TMASK), 1.0, 0.0)
        kept = feat[rows, :] * (time_keep * chan_keep).astype(BF16)
        masked[rows, :] = kept
        masked_t[:, rows] = kept.T
        return 0

    lax.fori_loop(0, TOK // 128, mask_rows, 0)
    load_grad.wait()
    moment = to_rows(moment_lanes)
    for part, _ in enumerate(gather.events()):
        if part == 2:
            tiles.near()
        elif part == 3:
            tiles.across()
    tiles.arrived(6)

    def weights(slot):
        tile = wtile[tiles.index(lax.div(slot, NZ), lax.rem(slot, NZ))]
        return decode(wbuf[slot], tile[:, 127:128]), tile

    def weight_block(block):
        def step(i, _):
            slot = block * NZ + 2 * i
            rows = pl.ds(pl.multiple_of(slot * ROWS, 2 * ROWS), 2 * ROWS)
            weight[rows, :] = stack(weights(slot)[0], weights(slot + 1)[0])
            return 0

        lax.fori_loop(0, NZ // 2, step, 0)

    for d in (0, 1, 3, 2):
        block = lax.rem(x + d, NX)
        if d:
            gather.wait_block(d)
        weight_block(block)
        depth = pl.ds(pl.multiple_of(block * BLOCK, BLOCK), BLOCK)

        def forward_tile(i, _, d=d, depth=depth):
            cols = pl.ds(pl.multiple_of(i * 256, 256), 256)
            term = jnp.dot(masked[:, depth], weight[depth, cols], preferred_element_type=F32)
            if d == 0:
                pre[:, cols] = term
            else:
                total = pre[:, cols] + term
                if d != 2:
                    pre[:, cols] = total
                else:
                    s = jax.nn.sigmoid(total)
                    slope = s + total * s * (1.0 - s)
                    dpre[:, cols] = (grad_in[:, cols].astype(F32) * slope).astype(BF16)
            return 0

        lax.fori_loop(0, COLS // 256, forward_tile, 0)

    def remote(src, dst, i, to):
        return pltpu.make_async_remote_copy(
            src_ref=src,
            dst_ref=dst,
            send_sem=rs_send.at[i],
            recv_sem=rs_recv.at[i],
            device_id=to,
            device_id_type=MESH,
        )

    def x_copy(d, cls):
        return remote(coded.at[d - 1, cls], xrecv.at[d - 1, cls], (d - 1) * 4 + cls, at(d, 0))

    def x_scale(d):
        return remote(scale_src.at[d - 1], scale_dst.at[d - 1], 12 + d - 1, at(d, 0))

    def near_copy(i):
        return remote(near_coded.at[i], lrecv.at[i], 15 + i, near_peers[i])

    def near_scale(i):
        return remote(scale_src.at[3 + i], scale_dst.at[3 + i], 18 + i, near_peers[i])

    def far_copy(i):
        return remote(far_coded.at[i], frecv.at[i], 21 + i, far_peers[i])

    def far_scale(i):
        return remote(scale_src.at[6 + i], scale_dst.at[6 + i], 24 + i, far_peers[i])

    classes = [lax.rem(z + d, 4) for d in (2, 1, 3, 0)]

    def grad_block(d):
        block = lax.rem(x + d, NX)

        def grad_tile(i, peak):
            rows = pl.ds(pl.multiple_of(block * BLOCK + i * 4 * ROWS, 32), 4 * ROWS)
            term = jnp.dot(masked_t[rows, :], dpre[...], preferred_element_type=F32)
            for j in range(4):
                slot = term[j * ROWS : (j + 1) * ROWS]
                partial[d, j, i] = slot
                peak = jnp.maximum(peak, peak_of(slot))
            return peak

        peak = lax.fori_loop(0, NZ // 4, grad_tile, jnp.zeros((8, COLS), F32))
        if d:
            scale = scale_of(peak)
            scale_src[d - 1] = pack(scale * (1.0 / 32767))
            x_scale(d).start()
            inverses[d - 1] = jnp.broadcast_to(32767.0 / scale, (8, COLS))

    def send_class(d, cls):
        inverse = inverses[d - 1][:1]

        def encode_slot(j, _):
            coded[d - 1, cls, j] = encode(partial[d, cls, j], inverse)
            return 0

        lax.fori_loop(0, 4, encode_slot, 0)
        x_copy(d, cls).start()

    for d in (2, 1, 3):
        grad_block(d)
        send_class(d, classes[0])
    grad_block(0)
    for cls in classes[1:]:
        for d in (2, 1, 3):
            send_class(d, cls)

    for d in (1, 2, 3):
        x_scale(d).wait_recv()
    scales = [unpack(scale_dst[i]) for i in range(3)]
    for n, cls in enumerate(classes):
        for d in (2, 1, 3):
            x_copy(d, cls).wait_recv()

        def add_x(j, peak, cls=cls):
            term = partial[0, cls, j]
            for i in range(3):
                term = term + decode(xrecv[i, cls, j], scales[i])
            summed[j] = term
            return jnp.maximum(peak, peak_of(term))

        peak = lax.fori_loop(0, 4, add_x, jnp.zeros((8, COLS), F32))
        if n < 3:
            i = (2, 0, 1)[n]
            scale = scale_of(peak)
            scale_src[3 + i] = pack(scale * (1.0 / 32767))
            near_scale(i).start()
            inverse = 32767.0 / scale

            def encode_near(j, _, i=i, inverse=inverse):
                near_coded[i, j] = encode(summed[j], inverse)
                return 0

            lax.fori_loop(0, 4, encode_near, 0)
            near_copy(i).start()

    for i in range(3):
        near_scale(i).wait_recv()
    scales = [unpack(scale_dst[3 + i]) for i in range(3)]
    for i in (0, 1, 2):
        near_copy(i).wait_recv()
    for d in (2, 1, 3, 0):
        j = lax.rem(lax.div(z, 4) + d, 4)
        grad = summed[j]
        for i in range(3):
            grad = grad + decode(lrecv[i, j], scales[i])
        if d:
            scale = scale_of(peak_of(grad))
            scale_src[6 + d - 1] = pack(scale * (1.0 / 32767))
            far_scale(d - 1).start()
            far_coded[d - 1] = encode(grad, 32767.0 / scale)
            far_copy(d - 1).start()
    for i in range(3):
        far_scale(i).wait_recv()
        far_copy(i).wait_recv()
        grad = grad + decode(frecv[i], unpack(scale_dst[6 + i]))

    peak = scale_of(peak_of(grad))
    nbuf[dp] = encode(grad, 32767.0 / peak)
    regather = Gather(nbuf, ag2_send, ag2_recv, x, z, mp)
    regather.start()
    squared = grad * grad
    row_lanes = squared[:, :128]
    for i in range(1, COLS // 128):
        row_lanes = row_lanes + squared[:, i * 128 : (i + 1) * 128]
    row_src[...] = row_lanes

    def row_copy(i):
        return pltpu.make_async_remote_copy(
            src_ref=row_src,
            dst_ref=row_dst.at[i],
            send_sem=row_send.at[i],
            recv_sem=row_recv.at[i],
            device_id=mp_peers[i],
            device_id_type=MESH,
        )

    def vec_copy(step, i):
        return pltpu.make_async_remote_copy(
            src_ref=vec.at[step],
            dst_ref=vec_in.at[step, i],
            send_sem=vec_send.at[step, i],
            recv_sem=vec_recv.at[step, i],
            device_id=(x_peers, far_peers, near_peers)[step][i],
            device_id_type=MESH,
        )

    def vec_start(step):
        for i in range(3):
            vec_copy(step, i).start()

    def vec_sum(step):
        sums = vec[step]
        for i in range(3):
            vec_copy(step, i).wait_recv()
            sums = sums + vec_in[step, i]
        return sums

    for i in range(NMP - 1):
        row_copy(i).start()
    column = jnp.sum(squared, axis=0, keepdims=True)
    events = regather.events()
    next(events)

    for i in range(NMP - 1):
        row_copy(i).wait_recv()
        row_lanes = row_lanes + row_dst[i]
    vec[0] = pack(column, jnp.sum(row_lanes, axis=0, keepdims=True), moment_lanes)
    vec_start(0)
    row_total = jnp.sum(row_lanes, axis=1, keepdims=True)
    retiles = Tiles(ntile, nt_send, nt_recv, x, z, mp)
    ntile[retiles.index(x, z)] = pack(peak * (1.0 / 32767), to_lanes(row_total))
    retiles.far()
    next(events)

    vec[1] = vec_sum(0)
    vec_start(1)
    next(events)
    vec[2] = vec_sum(1)
    vec_start(2)
    retiles.near()
    next(events)
    retiles.across()

    sums = vec_sum(2)
    col_total = unpack(sums)
    total = jnp.sum(sums[6:7], axis=1, keepdims=True)
    moments = jnp.sum(sums[7:8], axis=1, keepdims=True)

    clip = 1.0 / jnp.maximum(1.0, jnp.sqrt(total / (D * FF)))

    def next_row_state(old, squares):
        return decay_rate * old + (1.0 - decay_rate) * (clip * clip * squares / FF + epsilon)

    row_state = next_row_state(moment, row_total)
    col_state = decay_rate * cmom_ref[...].reshape(1, COLS) + (1.0 - decay_rate) * (clip * clip * col_total / D + epsilon)
    row_mean = decay_rate * moments / D + (1.0 - decay_rate) * (clip * clip * (total / FF) / D + epsilon)
    col_factor = step_rate * clip * lax.rsqrt(col_state)
    new_ref[...] = master_ref[...] - grad * (lax.rsqrt(row_state / row_mean) * col_factor)
    rstate_ref[...] = to_lanes(row_state)[:, :ROWS].reshape(ROWS)
    cstate_ref[...] = col_state.reshape(COLS)
    retiles.arrived(6)

    def updated(slot):
        old, old_moment = weights(slot)
        retile = ntile[retiles.index(lax.div(slot, NZ), lax.rem(slot, NZ))]
        row_factor = to_rows(lax.rsqrt(next_row_state(old_moment, retile[6:7]) / row_mean))
        return old - raw(nbuf[slot]) * (unpack(retile) * col_factor) * row_factor

    def leave(d):
        rows = pl.ds(pl.multiple_of(lax.rem(x + d, NX) * BLOCK, BLOCK), BLOCK)
        return pltpu.make_async_copy(low.at[rows], low_ref.at[rows], load_sem.at[2 + d])

    for d in (0, 1, 3, 2):
        block = lax.rem(x + d, NX)
        if d:
            regather.wait_block(d)

        def update_pair(i, _, block=block):
            slot = block * NZ + 2 * i
            rows = pl.ds(pl.multiple_of(slot * ROWS, 2 * ROWS), 2 * ROWS)
            low[rows, :] = stack(updated(slot), updated(slot + 1))
            return 0

        lax.fori_loop(0, NZ // 2, update_pair, 0)
        leave(d).start()
    tiles.finish()
    retiles.finish()
    for i in range(NMP - 1):
        row_copy(i).wait_send()
    for step in range(3):
        for i in range(3):
            vec_copy(step, i).wait_send()
    gather.finish()
    regather.finish()
    for d in (1, 2, 3):
        x_scale(d).wait_send()
        for cls in range(4):
            x_copy(d, cls).wait_send()
    for i in range(3):
        near_scale(i).wait_send()
        near_copy(i).wait_send()
        far_scale(i).wait_send()
        far_copy(i).wait_send()
    for d in range(NX):
        leave(d).wait()


def copy_kernel(new_in, rstate_in, cstate_in, low_in, new_out, rstate_out, cstate_out, low_out, new, rstate, cstate, low, sem):
    pieces = 4
    size = D // pieces
    ways = [(low_in.at[pl.ds(i * size, size)], low.at[pl.ds(i * size, size)], low_out.at[pl.ds(i * size, size)]) for i in range(pieces)]
    ways += [(new_in, new, new_out), (rstate_in, rstate, rstate_out), (cstate_in, cstate, cstate_out)]
    come = [pltpu.make_async_copy(a, b, sem.at[0, i]) for i, (a, b, _) in enumerate(ways)]
    go = [pltpu.make_async_copy(b, c, sem.at[1, i]) for i, (_, b, c) in enumerate(ways)]
    for copy in come:
        copy.start()
    for first, second in zip(come, go):
        first.wait()
        second.start()
    for copy in go:
        copy.wait()


def per_device(features, frame_start, chan_start, master_weight, row_moment, col_moment, out_grad):
    vmem = pl.BlockSpec(memory_space=pltpu.VMEM)
    smem = pl.BlockSpec(memory_space=pltpu.SMEM)
    out_shape = (
        jax.ShapeDtypeStruct((ROWS, COLS), F32),
        jax.ShapeDtypeStruct((ROWS,), F32),
        jax.ShapeDtypeStruct((COLS,), F32),
        jax.ShapeDtypeStruct((D, COLS), BF16),
    )
    anywhere = pl.BlockSpec(memory_space=pl.ANY)
    results = pl.pallas_call(
        kernel,
        name="adafactor_step",
        out_shape=out_shape,
        in_specs=[smem, smem, anywhere, vmem, vmem, vmem, anywhere],
        out_specs=(vmem, vmem, vmem, anywhere),
        scratch_shapes=[
            pltpu.VMEM((NX * NZ, 2 * ROWS, HALF), I16),
            pltpu.VMEM((NX * NZ, 1, 128), F32),
            pltpu.VMEM((D, COLS), BF16),
            pltpu.VMEM((NX * NZ, 2 * ROWS, HALF), I16),
            pltpu.VMEM((NX * NZ, 8, 128), F32),
            pltpu.VMEM((D, COLS), BF16),
            pltpu.VMEM((TOK, D), BF16),
            pltpu.VMEM((TOK, COLS), BF16),
            pltpu.VMEM((TOK, D), BF16),
            pltpu.VMEM((D, TOK), BF16),
            pltpu.VMEM((TOK, COLS), F32),
            pltpu.VMEM((TOK, COLS), BF16),
            pltpu.VMEM((NX, 4, 4, ROWS, COLS), F32),
            pltpu.VMEM((NX - 1, 8, COLS), F32),
            pltpu.VMEM((NX - 1, 4, 4, 2 * ROWS, HALF), I16),
            pltpu.VMEM((NX - 1, 4, 4, 2 * ROWS, HALF), I16),
            pltpu.VMEM((4, ROWS, COLS), F32),
            pltpu.VMEM((3, 4, 2 * ROWS, HALF), I16),
            pltpu.VMEM((3, 4, 2 * ROWS, HALF), I16),
            pltpu.VMEM((3, 2 * ROWS, HALF), I16),
            pltpu.VMEM((3, 2 * ROWS, HALF), I16),
            pltpu.VMEM((9, 8, 128), F32),
            pltpu.VMEM((9, 8, 128), F32),
            pltpu.VMEM((ROWS, 128), F32),
            pltpu.VMEM((NMP - 1, ROWS, 128), F32),
            pltpu.VMEM((3, 8, 128), F32),
            pltpu.VMEM((3, 3, 8, 128), F32),
            pltpu.SemaphoreType.DMA((NX * NZ,)),
            pltpu.SemaphoreType.DMA((NX * NZ,)),
            pltpu.SemaphoreType.DMA((NX * NZ,)),
            pltpu.SemaphoreType.DMA((NX * NZ,)),
            pltpu.SemaphoreType.DMA((27,)),
            pltpu.SemaphoreType.DMA((27,)),
            pltpu.SemaphoreType.DMA((NMP - 1,)),
            pltpu.SemaphoreType.DMA((NMP - 1,)),
            pltpu.SemaphoreType.DMA((3, 3)),
            pltpu.SemaphoreType.DMA((3, 3)),
            pltpu.SemaphoreType.DMA((9,)),
            pltpu.SemaphoreType.DMA((9,)),
            pltpu.SemaphoreType.DMA((9,)),
            pltpu.SemaphoreType.DMA((9,)),
            pltpu.SemaphoreType.DMA((2 + NX,)),
        ],
        compiler_params=pltpu.CompilerParams(collective_id=0, has_side_effects=True, vmem_limit_bytes=56 * 2**20),
    )(frame_start, chan_start, features, master_weight, row_moment, col_moment, out_grad)

    return pl.pallas_call(
        copy_kernel,
        name="results",
        out_shape=out_shape,
        in_specs=[anywhere] * 4,
        out_specs=(anywhere,) * 4,
        scratch_shapes=[pltpu.VMEM(out.shape, out.dtype) for out in out_shape] + [pltpu.SemaphoreType.DMA((2, 7))],
        compiler_params=pltpu.CompilerParams(vmem_limit_bytes=60 * 2**20),
    )(*results)


def solution(mesh):
    placed = (P("dp", None), P("dp"), P("dp"), P("dp", "mp"), P("dp"), P("mp"), P("dp", "mp"))
    return jax.shard_map(
        per_device,
        mesh=mesh,
        in_specs=placed,
        out_specs=(P("dp", "mp"), P("dp"), P("mp"), P(None, "mp")),
        check_vma=False,
    )
```

```python
import functools

import jax
import jax.numpy as jnp
from jax import lax
from jax.experimental import pallas as pl
from jax.experimental.pallas import tpu as pltpu
from jax.sharding import PartitionSpec as P

D = 1536
FF = 6144
TMASK = 128
FMASK = 192
NX = 4
NZ = 16
NMP = 8
TOK = 512
ROWS = D // (NX * NZ)
COLS = FF // NMP
HALF = COLS // 2
BLOCK = ROWS * NZ

epsilon = 1e-06
decay_rate = 0.8
step_rate = 0.01

MESH = pl.DeviceIdType.MESH
F32 = jnp.float32
BF16 = jnp.bfloat16
I16 = jnp.int16


def fold(rows):
    return jnp.concatenate([rows[:, :HALF], rows[:, HALF:]], axis=0)


class Gather:
    def __init__(self, buf, send_sem, recv_sem, x, z, mp):
        self.buf, self.send_sem, self.recv_sem = buf, send_sem, recv_sem
        self.x, self.z, self.mp = x, z, mp
        self.up, self.down = lax.rem(x + 1, NX), lax.rem(x + NX - 1, NX)
        self.line = [lax.rem(z + o, NZ) for o in range(NZ)]
        odd = lax.rem(z, 2)
        self.relay_from = [self.down + (self.up - self.down) * p for p in (odd, 1 - odd)]
        self.relay_to = [self.up + (self.down - self.up) * p for p in (odd, 1 - odd)]
        self.sent = 0

    def copy(self, slot, k, x, z):
        return pltpu.make_async_remote_copy(
            src_ref=self.buf.at[slot],
            dst_ref=self.buf.at[slot],
            send_sem=self.send_sem.at[k],
            recv_sem=self.recv_sem.at[slot],
            device_id=(x * NZ + z, self.mp),
            device_id_type=MESH,
        )

    def send(self, slot, x, z):
        self.copy(slot, self.sent, x, z).start()
        self.sent += 1

    def slot(self, o):
        return self.x * NZ + self.line[o]

    def arrived(self, slot):
        self.copy(slot, 0, self.x, self.z).wait_recv()

    def along_x(self, o):
        self.send(self.slot(o), self.up, self.z)
        self.send(self.slot(o), self.down, self.z)

    def near(self, o):
        for d in (2, 1, 15):
            self.send(self.slot(o), self.x, self.line[d])

    def relay(self, o):
        slot = self.relay_from[o % 2] * NZ + self.line[o]
        self.arrived(slot)
        self.send(slot, self.relay_to[o % 2], self.z)

    def start(self):
        for d in (8, 4, 12):
            self.send(self.slot(0), self.x, self.line[d])
        self.near(0)
        self.along_x(0)

    def far(self, o):
        self.arrived(self.slot(o))
        self.near(o)
        self.along_x(o)

    def pass_on(self, *offsets):
        for o in offsets:
            self.arrived(self.slot(o))
            self.along_x(o)

    def relays(self, *offsets):
        for o in offsets:
            self.relay(o)

    def events(self):
        self.pass_on(15, 1, 14)
        self.relays(0)
        yield
        self.far(4)
        self.far(12)
        self.relays(15, 1, 14)
        self.far(8)
        self.relays(4, 12)
        yield
        self.pass_on(3, 5, 2, 11, 13, 10)
        self.relays(8)
        self.pass_on(7, 9, 6)
        yield
        self.relays(3, 5, 2, 11, 13, 10, 7, 9, 6)
        yield

    def wait_block(self, d):
        x = lax.rem(self.x + d, NX)

        def step(i, _):
            if d == 2:
                owner = i
            else:
                owner = 2 * i + (0 if d == 1 else 1)
            self.arrived(x * NZ + owner)
            return 0

        lax.fori_loop(0, NZ if d == 2 else NZ // 2, step, 0)

    def finish(self):
        def step(k, _):
            self.copy(0, k, self.x, self.z).wait_send()
            return 0

        lax.fori_loop(0, NX * NZ - 1, step, 0)


class Tiles:
    def __init__(self, buf, send_sem, recv_sem, x, z, mp):
        self.buf, self.send_sem, self.recv_sem = buf, send_sem, recv_sem
        self.x, self.z, self.mp = x, z, mp
        self.sent = []

    def index(self, x, z):
        return lax.rem(z, 4) * 16 + lax.div(z, 4) * 4 + x

    def round(self, first, count, k, peers):
        for i, peer in enumerate(peers):
            block = self.buf.at[pl.ds(first, count)]
            copy = pltpu.make_async_remote_copy(
                src_ref=block,
                dst_ref=block,
                send_sem=self.send_sem.at[k + i],
                recv_sem=self.recv_sem.at[k + i],
                device_id=peer,
                device_id_type=MESH,
            )
            copy.start()
            self.sent.append(copy)

    def arrived(self, k):
        for copy in self.sent[k : k + 3]:
            copy.wait_recv()

    def along(self, distances):
        return [(self.x * NZ + lax.rem(self.z + d, NZ), self.mp) for d in distances]

    def across(self):
        peers = [(lax.rem(self.x + d, NX) * NZ + self.z, self.mp) for d in (2, 1, 3)]
        self.round(self.index(self.x, self.z), 1, 0, peers)

    def far(self):
        self.arrived(0)
        self.round(self.index(0, self.z), 4, 3, self.along((8, 4, 12)))

    def near(self):
        self.arrived(3)
        self.round(lax.rem(self.z, 4) * 16, 16, 6, self.along((2, 1, 15)))

    def finish(self):
        for copy in self.sent:
            copy.wait_send()


def stack(first, second):
    return jnp.concatenate([first, second], axis=0).astype(BF16)


def unfold(slot):
    return jnp.concatenate([slot[:ROWS], slot[ROWS:]], axis=1)


def pack(row, *more):
    pieces = [row[:, i * 128 : (i + 1) * 128] for i in range(COLS // 128)] + list(more)
    if len(pieces) < 8:
        pieces.append(jnp.zeros((8 - len(pieces), 128), F32))
    return jnp.concatenate(pieces, axis=0)


def raw(slot):
    return unfold(slot.astype(jnp.int32).astype(F32))


def unpack(tile):
    return jnp.concatenate([tile[i : i + 1] for i in range(COLS // 128)], axis=1)


def peak_of(rows):
    size = jnp.abs(rows)
    return jnp.maximum(jnp.maximum(size[:8], size[8:16]), size[16:24])


def scale_of(peak):
    return jnp.maximum(jnp.max(peak, axis=0, keepdims=True), 1e-30)


def encode(rows, inverse):
    return jnp.round(fold(rows * inverse)).astype(jnp.int32).astype(I16)


def decode(slot, scale):
    return raw(slot) * scale


def kernel(
    frame_ref, chan_ref, feat_hbm, master_ref, rmom_ref, cmom_ref, grad_hbm,
    new_ref, rstate_ref, cstate_ref, low_ref,
    wbuf, wtile, weight, nbuf, ntile, low, feat, grad_in, masked, masked_t, pre, dpre,
    partial, inverses, coded, xrecv, summed, near_coded, lrecv, far_coded, frecv, scale_src, scale_dst,
    row_src, row_dst, vec, vec_x, vec_z, vec_m,
    ag_send, ag_recv, ag2_send, ag2_recv, rs_send, rs_recv, row_send, row_recv, vx_sem, vz_sem, vm_sem, wt_send, wt_recv, nt_send, nt_recv, load_sem,
):
    dp, mp = lax.axis_index("dp"), lax.axis_index("mp")
    x, z = lax.div(dp, NZ), lax.rem(dp, NZ)

    def at(dx, dz):
        return (lax.rem(x + dx, NX) * NZ + lax.rem(z + dz, NZ), mp)

    x_peers = [at(d, 0) for d in (1, 2, 3)]
    near_peers = [at(0, d) for d in (1, NZ - 1, 2)]
    far_peers = [at(0, d) for d in (4, 8, 12)]
    mp_peers = [(dp, lax.rem(mp + d, NMP)) for d in range(1, NMP)]

    barrier = pltpu.get_barrier_semaphore()
    z_peers = [at(0, d) for d in range(1, NZ)]
    greeted = z_peers + x_peers + mp_peers
    for peer in greeted:
        pl.semaphore_signal(barrier, inc=1, device_id=peer, device_id_type=MESH)

    load_feat = pltpu.make_async_copy(feat_hbm, feat, load_sem.at[0])
    load_grad = pltpu.make_async_copy(grad_hbm, grad_in, load_sem.at[1])
    load_feat.start()
    load_grad.start()

    master = master_ref[...]
    peak = jnp.max(scale_of(peak_of(master)), axis=1, keepdims=True)
    diag = lax.broadcasted_iota(jnp.int32, (ROWS, 128), 0) == lax.broadcasted_iota(jnp.int32, (ROWS, 128), 1)

    def to_lanes(column):
        return jnp.sum(jnp.where(diag, column, 0.0), axis=0, keepdims=True)

    def to_rows(lanes):
        return jnp.sum(jnp.where(diag, lanes, 0.0), axis=1, keepdims=True)

    moment_lanes = jnp.concatenate([rmom_ref[...].reshape(1, ROWS), jnp.zeros((1, 128 - ROWS), F32)], axis=1)
    lane = lax.broadcasted_iota(jnp.int32, (1, 128), 1)
    wbuf[dp] = encode(master, 32767.0 / peak)
    tiles = Tiles(wtile, wt_send, wt_recv, x, z, mp)
    wtile[tiles.index(x, z)] = jnp.where(lane == 127, peak * (1.0 / 32767), moment_lanes)

    pl.semaphore_wait(barrier, len(greeted))
    tiles.across()
    gather = Gather(wbuf, ag_send, ag_recv, x, z, mp)
    gather.start()

    load_feat.wait()
    first_frame, first_chan = frame_ref[0], chan_ref[0]
    channel = lax.broadcasted_iota(jnp.int32, (1, D), 1)
    chan_keep = jnp.where((channel < first_chan) | (channel >= first_chan + FMASK), 1.0, 0.0)

    def mask_rows(i, _):
        rows = pl.ds(pl.multiple_of(i * 128, 128), 128)
        offset = lax.broadcasted_iota(jnp.int32, (128, 1), 0) + i * 128
        time_keep = jnp.where((offset < first_frame) | (offset >= first_frame + TMASK), 1.0, 0.0)
        kept = feat[rows, :] * (time_keep * chan_keep).astype(BF16)
        masked[rows, :] = kept
        masked_t[:, rows] = kept.T
        return 0

    lax.fori_loop(0, TOK // 128, mask_rows, 0)
    load_grad.wait()
    moment = to_rows(moment_lanes)
    for part, _ in enumerate(gather.events()):
        if part == 0:
            tiles.far()
        elif part == 2:
            tiles.near()
    tiles.arrived(6)

    def weights(slot):
        tile = wtile[tiles.index(lax.div(slot, NZ), lax.rem(slot, NZ))]
        return decode(wbuf[slot], tile[:, 127:128]), tile

    def weight_block(block):
        def step(i, _):
            slot = block * NZ + 2 * i
            rows = pl.ds(pl.multiple_of(slot * ROWS, 2 * ROWS), 2 * ROWS)
            weight[rows, :] = stack(weights(slot)[0], weights(slot + 1)[0])
            return 0

        lax.fori_loop(0, NZ // 2, step, 0)

    for d in (0, 1, 3, 2):
        block = lax.rem(x + d, NX)
        if d:
            gather.wait_block(d)
        weight_block(block)
        depth = pl.ds(pl.multiple_of(block * BLOCK, BLOCK), BLOCK)

        def forward_tile(i, _, d=d, depth=depth):
            cols = pl.ds(pl.multiple_of(i * 256, 256), 256)
            term = jnp.dot(masked[:, depth], weight[depth, cols], preferred_element_type=F32)
            if d == 0:
                pre[:, cols] = term
            else:
                total = pre[:, cols] + term
                if d != 2:
                    pre[:, cols] = total
                else:
                    s = jax.nn.sigmoid(total)
                    slope = s + total * s * (1.0 - s)
                    dpre[:, cols] = (grad_in[:, cols].astype(F32) * slope).astype(BF16)
            return 0

        lax.fori_loop(0, COLS // 256, forward_tile, 0)

    def remote(src, dst, i, to):
        return pltpu.make_async_remote_copy(
            src_ref=src,
            dst_ref=dst,
            send_sem=rs_send.at[i],
            recv_sem=rs_recv.at[i],
            device_id=to,
            device_id_type=MESH,
        )

    def x_copy(d, cls):
        return remote(coded.at[d - 1, cls], xrecv.at[d - 1, cls], (d - 1) * 4 + cls, at(d, 0))

    def x_scale(d):
        return remote(scale_src.at[d - 1], scale_dst.at[d - 1], 12 + d - 1, at(d, 0))

    def near_copy(i):
        return remote(near_coded.at[i], lrecv.at[i], 15 + i, near_peers[i])

    def near_scale(i):
        return remote(scale_src.at[3 + i], scale_dst.at[3 + i], 18 + i, near_peers[i])

    def far_copy(i):
        return remote(far_coded.at[i], frecv.at[i], 21 + i, far_peers[i])

    def far_scale(i):
        return remote(scale_src.at[6 + i], scale_dst.at[6 + i], 24 + i, far_peers[i])

    classes = [lax.rem(z + d, 4) for d in (2, 1, 3, 0)]

    def grad_block(d):
        block = lax.rem(x + d, NX)

        def grad_tile(i, peak):
            rows = pl.ds(pl.multiple_of(block * BLOCK + i * 4 * ROWS, 32), 4 * ROWS)
            term = jnp.dot(masked_t[rows, :], dpre[...], preferred_element_type=F32)
            for j in range(4):
                slot = term[j * ROWS : (j + 1) * ROWS]
                partial[d, j, i] = slot
                peak = jnp.maximum(peak, peak_of(slot))
            return peak

        peak = lax.fori_loop(0, NZ // 4, grad_tile, jnp.zeros((8, COLS), F32))
        if d:
            scale = scale_of(peak)
            scale_src[d - 1] = pack(scale * (1.0 / 32767))
            x_scale(d).start()
            inverses[d - 1] = jnp.broadcast_to(32767.0 / scale, (8, COLS))

    def send_class(d, cls):
        inverse = inverses[d - 1][:1]

        def encode_slot(j, _):
            coded[d - 1, cls, j] = encode(partial[d, cls, j], inverse)
            return 0

        lax.fori_loop(0, 4, encode_slot, 0)
        x_copy(d, cls).start()

    for d in (2, 1, 3):
        grad_block(d)
        send_class(d, classes[0])
    grad_block(0)
    for cls in classes[1:]:
        for d in (2, 1, 3):
            send_class(d, cls)

    for d in (1, 2, 3):
        x_scale(d).wait_recv()
    scales = [unpack(scale_dst[i]) for i in range(3)]
    for n, cls in enumerate(classes):
        for d in (2, 1, 3):
            x_copy(d, cls).wait_recv()

        def add_x(j, peak, cls=cls):
            term = partial[0, cls, j]
            for i in range(3):
                term = term + decode(xrecv[i, cls, j], scales[i])
            summed[j] = term
            return jnp.maximum(peak, peak_of(term))

        peak = lax.fori_loop(0, 4, add_x, jnp.zeros((8, COLS), F32))
        if n < 3:
            i = (2, 0, 1)[n]
            scale = scale_of(peak)
            scale_src[3 + i] = pack(scale * (1.0 / 32767))
            near_scale(i).start()
            inverse = 32767.0 / scale

            def encode_near(j, _, i=i, inverse=inverse):
                near_coded[i, j] = encode(summed[j], inverse)
                return 0

            lax.fori_loop(0, 4, encode_near, 0)
            near_copy(i).start()

    for i in range(3):
        near_scale(i).wait_recv()
    scales = [unpack(scale_dst[3 + i]) for i in range(3)]
    for i in (0, 1, 2):
        near_copy(i).wait_recv()
    for d in (2, 1, 3, 0):
        j = lax.rem(lax.div(z, 4) + d, 4)
        grad = summed[j]
        for i in range(3):
            grad = grad + decode(lrecv[i, j], scales[i])
        if d:
            scale = scale_of(peak_of(grad))
            scale_src[6 + d - 1] = pack(scale * (1.0 / 32767))
            far_scale(d - 1).start()
            far_coded[d - 1] = encode(grad, 32767.0 / scale)
            far_copy(d - 1).start()
    for i in range(3):
        far_scale(i).wait_recv()
        far_copy(i).wait_recv()
        grad = grad + decode(frecv[i], unpack(scale_dst[6 + i]))

    squared = grad * grad
    row_lanes = squared[:, :128]
    for i in range(1, COLS // 128):
        row_lanes = row_lanes + squared[:, i * 128 : (i + 1) * 128]
    row_src[...] = row_lanes

    def row_copy(i):
        return pltpu.make_async_remote_copy(
            src_ref=row_src,
            dst_ref=row_dst.at[i],
            send_sem=row_send.at[i],
            recv_sem=row_recv.at[i],
            device_id=mp_peers[i],
            device_id_type=MESH,
        )

    def vec_copies(step, landing, sems, peers):
        return [
            pltpu.make_async_remote_copy(
                src_ref=vec.at[step],
                dst_ref=landing.at[i],
                send_sem=sems.at[0, i],
                recv_sem=sems.at[1, i],
                device_id=peer,
                device_id_type=MESH,
            )
            for i, peer in enumerate(peers)
        ]

    rounds = [
        vec_copies(0, vec_x, vx_sem, x_peers),
        vec_copies(1, vec_z, vz_sem, z_peers),
        vec_copies(2, vec_m, vm_sem, mp_peers),
    ]

    def begin(step):
        for copy in rounds[step]:
            copy.start()

    def total_of(step, landing):
        sums = vec[step]
        for i, copy in enumerate(rounds[step]):
            copy.wait_recv()
            sums = sums + landing[i]
        return sums

    column = jnp.sum(squared, axis=0, keepdims=True)
    vec[0] = pack(column, jnp.sum(row_lanes, axis=0, keepdims=True), moment_lanes)
    begin(0)
    for i in range(NMP - 1):
        row_copy(i).start()
    peak = scale_of(peak_of(grad))
    nbuf[dp] = encode(grad, 32767.0 / peak)
    regather = Gather(nbuf, ag2_send, ag2_recv, x, z, mp)
    regather.start()
    events = regather.events()
    next(events)

    vec[1] = total_of(0, vec_x)
    begin(1)
    for i in range(NMP - 1):
        row_copy(i).wait_recv()
        row_lanes = row_lanes + row_dst[i]
    row_total = jnp.sum(row_lanes, axis=1, keepdims=True)
    retiles = Tiles(ntile, nt_send, nt_recv, x, z, mp)
    ntile[retiles.index(x, z)] = pack(peak * (1.0 / 32767), to_lanes(row_total))
    retiles.across()
    next(events)

    retiles.far()
    next(events)
    sums = total_of(1, vec_z)
    vec[2] = sums
    begin(2)
    retiles.near()
    next(events)
    norm = total_of(2, vec_m)[6:7]
    col_total = unpack(sums)
    total = jnp.sum(norm, axis=1, keepdims=True)
    moments = jnp.sum(sums[7:8], axis=1, keepdims=True)

    clip = 1.0 / jnp.maximum(1.0, jnp.sqrt(total / (D * FF)))

    def next_row_state(old, squares):
        return decay_rate * old + (1.0 - decay_rate) * (clip * clip * squares / FF + epsilon)

    row_state = next_row_state(moment, row_total)
    col_state = decay_rate * cmom_ref[...].reshape(1, COLS) + (1.0 - decay_rate) * (clip * clip * col_total / D + epsilon)
    row_mean = decay_rate * moments / D + (1.0 - decay_rate) * (clip * clip * (total / FF) / D + epsilon)
    col_factor = step_rate * clip * lax.rsqrt(col_state)
    new_ref[...] = master_ref[...] - grad * (lax.rsqrt(row_state / row_mean) * col_factor)
    rstate_ref[...] = to_lanes(row_state)[:, :ROWS].reshape(ROWS)
    cstate_ref[...] = col_state.reshape(COLS)
    retiles.arrived(6)

    def updated(slot):
        old, old_moment = weights(slot)
        retile = ntile[retiles.index(lax.div(slot, NZ), lax.rem(slot, NZ))]
        row_factor = to_rows(lax.rsqrt(next_row_state(old_moment, retile[6:7]) / row_mean))
        return old - raw(nbuf[slot]) * (unpack(retile) * col_factor) * row_factor

    def leave(d):
        rows = pl.ds(pl.multiple_of(lax.rem(x + d, NX) * BLOCK, BLOCK), BLOCK)
        return pltpu.make_async_copy(low.at[rows], low_ref.at[rows], load_sem.at[2 + d])

    for d in (0, 1, 3, 2):
        block = lax.rem(x + d, NX)
        if d:
            regather.wait_block(d)

        def update_pair(i, _, block=block):
            slot = block * NZ + 2 * i
            rows = pl.ds(pl.multiple_of(slot * ROWS, 2 * ROWS), 2 * ROWS)
            low[rows, :] = stack(updated(slot), updated(slot + 1))
            return 0

        lax.fori_loop(0, NZ // 2, update_pair, 0)
        leave(d).start()
    tiles.finish()
    retiles.finish()
    for i in range(NMP - 1):
        row_copy(i).wait_send()
    for copies in rounds:
        for copy in copies:
            copy.wait_send()
    gather.finish()
    regather.finish()
    for d in (1, 2, 3):
        x_scale(d).wait_send()
        for cls in range(4):
            x_copy(d, cls).wait_send()
    for i in range(3):
        near_scale(i).wait_send()
        near_copy(i).wait_send()
        far_scale(i).wait_send()
        far_copy(i).wait_send()
    for d in range(NX):
        leave(d).wait()


def copy_kernel(new_in, rstate_in, cstate_in, low_in, new_out, rstate_out, cstate_out, low_out, new, rstate, cstate, low, sem):
    pieces = 4
    size = D // pieces
    ways = [(low_in.at[pl.ds(i * size, size)], low.at[pl.ds(i * size, size)], low_out.at[pl.ds(i * size, size)]) for i in range(pieces)]
    ways += [(new_in, new, new_out), (rstate_in, rstate, rstate_out), (cstate_in, cstate, cstate_out)]
    come = [pltpu.make_async_copy(a, b, sem.at[0, i]) for i, (a, b, _) in enumerate(ways)]
    go = [pltpu.make_async_copy(b, c, sem.at[1, i]) for i, (_, b, c) in enumerate(ways)]
    for copy in come:
        copy.start()
    for first, second in zip(come, go):
        first.wait()
        second.start()
    for copy in go:
        copy.wait()


def per_device(features, frame_start, chan_start, master_weight, row_moment, col_moment, out_grad):
    vmem = pl.BlockSpec(memory_space=pltpu.VMEM)
    smem = pl.BlockSpec(memory_space=pltpu.SMEM)
    out_shape = (
        jax.ShapeDtypeStruct((ROWS, COLS), F32),
        jax.ShapeDtypeStruct((ROWS,), F32),
        jax.ShapeDtypeStruct((COLS,), F32),
        jax.ShapeDtypeStruct((D, COLS), BF16),
    )
    anywhere = pl.BlockSpec(memory_space=pl.ANY)
    results = pl.pallas_call(
        kernel,
        name="adafactor_step",
        out_shape=out_shape,
        in_specs=[smem, smem, anywhere, vmem, vmem, vmem, anywhere],
        out_specs=(vmem, vmem, vmem, anywhere),
        scratch_shapes=[
            pltpu.VMEM((NX * NZ, 2 * ROWS, HALF), I16),
            pltpu.VMEM((NX * NZ, 1, 128), F32),
            pltpu.VMEM((D, COLS), BF16),
            pltpu.VMEM((NX * NZ, 2 * ROWS, HALF), I16),
            pltpu.VMEM((NX * NZ, 8, 128), F32),
            pltpu.VMEM((D, COLS), BF16),
            pltpu.VMEM((TOK, D), BF16),
            pltpu.VMEM((TOK, COLS), BF16),
            pltpu.VMEM((TOK, D), BF16),
            pltpu.VMEM((D, TOK), BF16),
            pltpu.VMEM((TOK, COLS), F32),
            pltpu.VMEM((TOK, COLS), BF16),
            pltpu.VMEM((NX, 4, 4, ROWS, COLS), F32),
            pltpu.VMEM((NX - 1, 8, COLS), F32),
            pltpu.VMEM((NX - 1, 4, 4, 2 * ROWS, HALF), I16),
            pltpu.VMEM((NX - 1, 4, 4, 2 * ROWS, HALF), I16),
            pltpu.VMEM((4, ROWS, COLS), F32),
            pltpu.VMEM((3, 4, 2 * ROWS, HALF), I16),
            pltpu.VMEM((3, 4, 2 * ROWS, HALF), I16),
            pltpu.VMEM((3, 2 * ROWS, HALF), I16),
            pltpu.VMEM((3, 2 * ROWS, HALF), I16),
            pltpu.VMEM((9, 8, 128), F32),
            pltpu.VMEM((9, 8, 128), F32),
            pltpu.VMEM((ROWS, 128), F32),
            pltpu.VMEM((NMP - 1, ROWS, 128), F32),
            pltpu.VMEM((3, 8, 128), F32),
            pltpu.VMEM((NX - 1, 8, 128), F32),
            pltpu.VMEM((NZ - 1, 8, 128), F32),
            pltpu.VMEM((NMP - 1, 8, 128), F32),
            pltpu.SemaphoreType.DMA((NX * NZ,)),
            pltpu.SemaphoreType.DMA((NX * NZ,)),
            pltpu.SemaphoreType.DMA((NX * NZ,)),
            pltpu.SemaphoreType.DMA((NX * NZ,)),
            pltpu.SemaphoreType.DMA((27,)),
            pltpu.SemaphoreType.DMA((27,)),
            pltpu.SemaphoreType.DMA((NMP - 1,)),
            pltpu.SemaphoreType.DMA((NMP - 1,)),
            pltpu.SemaphoreType.DMA((2, NX - 1)),
            pltpu.SemaphoreType.DMA((2, NZ - 1)),
            pltpu.SemaphoreType.DMA((2, NMP - 1)),
            pltpu.SemaphoreType.DMA((9,)),
            pltpu.SemaphoreType.DMA((9,)),
            pltpu.SemaphoreType.DMA((9,)),
            pltpu.SemaphoreType.DMA((9,)),
            pltpu.SemaphoreType.DMA((2 + NX,)),
        ],
        compiler_params=pltpu.CompilerParams(collective_id=0, has_side_effects=True, vmem_limit_bytes=56 * 2**20),
    )(frame_start, chan_start, features, master_weight, row_moment, col_moment, out_grad)

    return pl.pallas_call(
        copy_kernel,
        name="results",
        out_shape=out_shape,
        in_specs=[anywhere] * 4,
        out_specs=(anywhere,) * 4,
        scratch_shapes=[pltpu.VMEM(out.shape, out.dtype) for out in out_shape] + [pltpu.SemaphoreType.DMA((2, 7))],
        compiler_params=pltpu.CompilerParams(vmem_limit_bytes=60 * 2**20),
    )(*results)


def solution(mesh):
    placed = (P("dp", None), P("dp"), P("dp"), P("dp", "mp"), P("dp"), P("mp"), P("dp", "mp"))
    return jax.shard_map(
        per_device,
        mesh=mesh,
        in_specs=placed,
        out_specs=(P("dp", "mp"), P("dp"), P("mp"), P(None, "mp")),
        check_vma=False,
    )
```

```python
import functools

import jax
import jax.numpy as jnp
from jax import lax
from jax.experimental import pallas as pl
from jax.experimental.pallas import tpu as pltpu
from jax.sharding import PartitionSpec as P

D = 1536
FF = 6144
TMASK = 128
FMASK = 192
NX = 4
NZ = 16
NMP = 8
TOK = 512
ROWS = D // (NX * NZ)
COLS = FF // NMP
HALF = COLS // 2
BLOCK = ROWS * NZ

epsilon = 1e-06
decay_rate = 0.8
step_rate = 0.01

MESH = pl.DeviceIdType.MESH
F32 = jnp.float32
BF16 = jnp.bfloat16
I16 = jnp.int16


def fold(rows):
    return jnp.concatenate([rows[:, :HALF], rows[:, HALF:]], axis=0)


class Gather:
    def __init__(self, buf, send_sem, recv_sem, x, z, mp):
        self.buf, self.send_sem, self.recv_sem = buf, send_sem, recv_sem
        self.x, self.z, self.mp = x, z, mp
        self.up, self.down = lax.rem(x + 1, NX), lax.rem(x + NX - 1, NX)
        self.line = [lax.rem(z + o, NZ) for o in range(NZ)]
        odd = lax.rem(z, 2)
        self.relay_from = [self.down + (self.up - self.down) * p for p in (odd, 1 - odd)]
        self.relay_to = [self.up + (self.down - self.up) * p for p in (odd, 1 - odd)]
        self.sent = 0

    def copy(self, slot, k, x, z):
        return pltpu.make_async_remote_copy(
            src_ref=self.buf.at[slot],
            dst_ref=self.buf.at[slot],
            send_sem=self.send_sem.at[k],
            recv_sem=self.recv_sem.at[slot],
            device_id=(x * NZ + z, self.mp),
            device_id_type=MESH,
        )

    def send(self, slot, x, z):
        self.copy(slot, self.sent, x, z).start()
        self.sent += 1

    def slot(self, o):
        return self.x * NZ + self.line[o]

    def arrived(self, slot):
        self.copy(slot, 0, self.x, self.z).wait_recv()

    def along_x(self, o):
        self.send(self.slot(o), self.up, self.z)
        self.send(self.slot(o), self.down, self.z)

    def near(self, o):
        for d in (2, 1, 15):
            self.send(self.slot(o), self.x, self.line[d])

    def relay(self, o):
        slot = self.relay_from[o % 2] * NZ + self.line[o]
        self.arrived(slot)
        self.send(slot, self.relay_to[o % 2], self.z)

    def start(self):
        for d in (8, 4, 12):
            self.send(self.slot(0), self.x, self.line[d])
        self.near(0)
        self.along_x(0)

    def far(self, o):
        self.arrived(self.slot(o))
        self.near(o)
        self.along_x(o)

    def pass_on(self, *offsets):
        for o in offsets:
            self.arrived(self.slot(o))
            self.along_x(o)

    def relays(self, *offsets):
        for o in offsets:
            self.relay(o)

    def events(self):
        self.pass_on(15, 1, 14)
        self.relays(0)
        yield
        self.far(4)
        self.far(12)
        self.relays(15, 1, 14)
        self.far(8)
        self.relays(4, 12)
        yield
        self.pass_on(3, 5, 2, 11, 13, 10)
        self.relays(8)
        self.pass_on(7, 9, 6)
        yield
        self.relays(3, 5, 2, 11, 13, 10, 7, 9, 6)
        yield

    def wait_pair(self, d, slot):
        if d in (1, 2):
            self.arrived(slot)
        if d in (3, 2):
            self.arrived(slot + 1)

    def finish(self):
        def step(k, _):
            self.copy(0, k, self.x, self.z).wait_send()
            return 0

        lax.fori_loop(0, NX * NZ - 1, step, 0)


class Tiles:
    def __init__(self, buf, send_sem, recv_sem, x, z, mp):
        self.buf, self.send_sem, self.recv_sem = buf, send_sem, recv_sem
        self.x, self.z, self.mp = x, z, mp
        self.sent = []

    def index(self, x, z):
        return lax.rem(z, 4) * 16 + lax.div(z, 4) * 4 + x

    def round(self, first, count, k, peers):
        for i, peer in enumerate(peers):
            block = self.buf.at[pl.ds(first, count)]
            copy = pltpu.make_async_remote_copy(
                src_ref=block,
                dst_ref=block,
                send_sem=self.send_sem.at[k + i],
                recv_sem=self.recv_sem.at[k + i],
                device_id=peer,
                device_id_type=MESH,
            )
            copy.start()
            self.sent.append(copy)

    def arrived(self, k):
        for copy in self.sent[k : k + 3]:
            copy.wait_recv()

    def along(self, distances):
        return [(self.x * NZ + lax.rem(self.z + d, NZ), self.mp) for d in distances]

    def across(self):
        peers = [(lax.rem(self.x + d, NX) * NZ + self.z, self.mp) for d in (2, 1, 3)]
        self.round(self.index(self.x, self.z), 1, 0, peers)

    def far(self):
        self.arrived(0)
        self.round(self.index(0, self.z), 4, 3, self.along((8, 4, 12)))

    def near(self):
        self.arrived(3)
        self.round(lax.rem(self.z, 4) * 16, 16, 6, self.along((2, 1, 15)))

    def finish(self):
        for copy in self.sent:
            copy.wait_send()


def stack(first, second):
    return jnp.concatenate([first, second], axis=0).astype(BF16)


def unfold(slot):
    return jnp.concatenate([slot[:ROWS], slot[ROWS:]], axis=1)


def pack(row, *more):
    pieces = [row[:, i * 128 : (i + 1) * 128] for i in range(COLS // 128)] + list(more)
    if len(pieces) < 8:
        pieces.append(jnp.zeros((8 - len(pieces), 128), F32))
    return jnp.concatenate(pieces, axis=0)


def raw(slot):
    return unfold(slot.astype(jnp.int32).astype(F32))


def unpack(tile):
    return jnp.concatenate([tile[i : i + 1] for i in range(COLS // 128)], axis=1)


def peak_of(rows):
    size = jnp.abs(rows)
    return jnp.maximum(jnp.maximum(size[:8], size[8:16]), size[16:24])


def scale_of(peak):
    return jnp.maximum(jnp.max(peak, axis=0, keepdims=True), 1e-30)


def encode(rows, inverse):
    return jnp.round(fold(rows * inverse)).astype(jnp.int32).astype(I16)


def decode(slot, scale):
    return raw(slot) * scale


def kernel(
    frame_ref, chan_ref, feat_hbm, master_hbm, rmom_hbm, cmom_hbm, grad_hbm,
    new_ref, rstate_ref, cstate_ref, low_ref,
    master_ref, rmom_ref, cmom_ref, wbuf, wtile, weight, nbuf, ntile, low, feat, grad_in, masked, masked_t, pre, dpre,
    partial, inverses, coded, xrecv, summed, near_coded, lrecv, far_coded, frecv, scale_src, scale_dst,
    row_src, row_dst, vec, vec_x, vec_z, vec_m,
    ag_send, ag_recv, ag2_send, ag2_recv, rs_send, rs_recv, row_send, row_recv, vx_sem, vz_sem, vm_sem, wt_send, wt_recv, nt_send, nt_recv, load_sem, own_sem,
):
    dp, mp = lax.axis_index("dp"), lax.axis_index("mp")
    x, z = lax.div(dp, NZ), lax.rem(dp, NZ)

    def at(dx, dz):
        return (lax.rem(x + dx, NX) * NZ + lax.rem(z + dz, NZ), mp)

    x_peers = [at(d, 0) for d in (1, 2, 3)]
    near_peers = [at(0, d) for d in (1, NZ - 1, 2)]
    far_peers = [at(0, d) for d in (4, 8, 12)]
    mp_peers = [(dp, lax.rem(mp + d, NMP)) for d in range(1, NMP)]

    barrier = pltpu.get_barrier_semaphore()
    z_peers = [at(0, d) for d in range(1, NZ)]
    greeted = z_peers + x_peers + mp_peers
    for peer in greeted:
        pl.semaphore_signal(barrier, inc=1, device_id=peer, device_id_type=MESH)

    own_loads = [
        pltpu.make_async_copy(source, target, own_sem.at[i])
        for i, (source, target) in enumerate(((master_hbm, master_ref), (rmom_hbm, rmom_ref), (cmom_hbm, cmom_ref)))
    ]
    for load in own_loads:
        load.start()
    load_feat = pltpu.make_async_copy(feat_hbm, feat, load_sem.at[0])
    load_grad = pltpu.make_async_copy(grad_hbm, grad_in, load_sem.at[1])
    load_feat.start()
    load_grad.start()

    for load in own_loads:
        load.wait()
    master = master_ref[...]
    peak = jnp.max(scale_of(peak_of(master)), axis=1, keepdims=True)
    diag = lax.broadcasted_iota(jnp.int32, (ROWS, 128), 0) == lax.broadcasted_iota(jnp.int32, (ROWS, 128), 1)

    def to_lanes(column):
        return jnp.sum(jnp.where(diag, column, 0.0), axis=0, keepdims=True)

    def to_rows(lanes):
        return jnp.sum(jnp.where(diag, lanes, 0.0), axis=1, keepdims=True)

    moment_lanes = jnp.concatenate([rmom_ref[...].reshape(1, ROWS), jnp.zeros((1, 128 - ROWS), F32)], axis=1)
    lane = lax.broadcasted_iota(jnp.int32, (1, 128), 1)
    wbuf[dp] = encode(master, 32767.0 / peak)
    tiles = Tiles(wtile, wt_send, wt_recv, x, z, mp)
    wtile[tiles.index(x, z)] = jnp.where(lane == 127, peak * (1.0 / 32767), moment_lanes)

    pl.semaphore_wait(barrier, len(greeted))
    tiles.across()
    gather = Gather(wbuf, ag_send, ag_recv, x, z, mp)
    gather.start()

    load_feat.wait()
    first_frame, first_chan = frame_ref[0], chan_ref[0]
    channel = lax.broadcasted_iota(jnp.int32, (1, D), 1)
    chan_keep = jnp.where((channel < first_chan) | (channel >= first_chan + FMASK), 1.0, 0.0)

    def mask_rows(i, _):
        rows = pl.ds(pl.multiple_of(i * 128, 128), 128)
        offset = lax.broadcasted_iota(jnp.int32, (128, 1), 0) + i * 128
        time_keep = jnp.where((offset < first_frame) | (offset >= first_frame + TMASK), 1.0, 0.0)
        kept = feat[rows, :] * (time_keep * chan_keep).astype(BF16)
        masked[rows, :] = kept
        masked_t[:, rows] = kept.T
        return 0

    lax.fori_loop(0, TOK // 128, mask_rows, 0)
    load_grad.wait()
    moment = to_rows(moment_lanes)
    for part, _ in enumerate(gather.events()):
        if part == 0:
            tiles.far()
        elif part == 2:
            tiles.near()
    tiles.arrived(6)

    def weights(slot):
        tile = wtile[tiles.index(lax.div(slot, NZ), lax.rem(slot, NZ))]
        return decode(wbuf[slot], tile[:, 127:128]), tile

    def weight_block(d, block):
        def step(i, _):
            slot = block * NZ + 2 * i
            gather.wait_pair(d, slot)
            rows = pl.ds(pl.multiple_of(slot * ROWS, 2 * ROWS), 2 * ROWS)
            weight[rows, :] = stack(weights(slot)[0], weights(slot + 1)[0])
            return 0

        lax.fori_loop(0, NZ // 2, step, 0)

    for d in (0, 1, 3, 2):
        block = lax.rem(x + d, NX)
        weight_block(d, block)
        depth = pl.ds(pl.multiple_of(block * BLOCK, BLOCK), BLOCK)

        def forward_tile(i, _, d=d, depth=depth):
            cols = pl.ds(pl.multiple_of(i * 256, 256), 256)
            term = jnp.dot(masked[:, depth], weight[depth, cols], preferred_element_type=F32)
            if d == 0:
                pre[:, cols] = term
            else:
                total = pre[:, cols] + term
                if d != 2:
                    pre[:, cols] = total
                else:
                    s = jax.nn.sigmoid(total)
                    slope = s + total * s * (1.0 - s)
                    dpre[:, cols] = (grad_in[:, cols].astype(F32) * slope).astype(BF16)
            return 0

        lax.fori_loop(0, COLS // 256, forward_tile, 0)

    def remote(src, dst, i, to):
        return pltpu.make_async_remote_copy(
            src_ref=src,
            dst_ref=dst,
            send_sem=rs_send.at[i],
            recv_sem=rs_recv.at[i],
            device_id=to,
            device_id_type=MESH,
        )

    def x_copy(d, cls):
        return remote(coded.at[d - 1, cls], xrecv.at[d - 1, cls], (d - 1) * 4 + cls, at(d, 0))

    def x_scale(d):
        return remote(scale_src.at[d - 1], scale_dst.at[d - 1], 12 + d - 1, at(d, 0))

    def near_copy(i):
        return remote(near_coded.at[i], lrecv.at[i], 15 + i, near_peers[i])

    def near_scale(i):
        return remote(scale_src.at[3 + i], scale_dst.at[3 + i], 18 + i, near_peers[i])

    def far_copy(i):
        return remote(far_coded.at[i], frecv.at[i], 21 + i, far_peers[i])

    def far_scale(i):
        return remote(scale_src.at[6 + i], scale_dst.at[6 + i], 24 + i, far_peers[i])

    classes = [lax.rem(z + d, 4) for d in (2, 1, 3, 0)]

    def grad_block(d):
        block = lax.rem(x + d, NX)

        def grad_tile(i, peak):
            rows = pl.ds(pl.multiple_of(block * BLOCK + i * 4 * ROWS, 32), 4 * ROWS)
            term = jnp.dot(masked_t[rows, :], dpre[...], preferred_element_type=F32)
            for j in range(4):
                slot = term[j * ROWS : (j + 1) * ROWS]
                partial[d, j, i] = slot
                peak = jnp.maximum(peak, peak_of(slot))
            return peak

        peak = lax.fori_loop(0, NZ // 4, grad_tile, jnp.zeros((8, COLS), F32))
        if d:
            scale = scale_of(peak)
            scale_src[d - 1] = pack(scale * (1.0 / 32767))
            x_scale(d).start()
            inverses[d - 1] = jnp.broadcast_to(32767.0 / scale, (8, COLS))

    def send_class(d, cls):
        inverse = inverses[d - 1][:1]

        def encode_slot(j, _):
            coded[d - 1, cls, j] = encode(partial[d, cls, j], inverse)
            return 0

        lax.fori_loop(0, 4, encode_slot, 0)
        x_copy(d, cls).start()

    for d in (2, 1, 3):
        grad_block(d)
        send_class(d, classes[0])
    grad_block(0)
    for cls in classes[1:]:
        for d in (2, 1, 3):
            send_class(d, cls)

    for d in (1, 2, 3):
        x_scale(d).wait_recv()
    scales = [unpack(scale_dst[i]) for i in range(3)]
    for n, cls in enumerate(classes):
        for d in (2, 1, 3):
            x_copy(d, cls).wait_recv()

        def add_x(j, peak, cls=cls):
            term = partial[0, cls, j]
            for i in range(3):
                term = term + decode(xrecv[i, cls, j], scales[i])
            summed[j] = term
            return jnp.maximum(peak, peak_of(term))

        peak = lax.fori_loop(0, 4, add_x, jnp.zeros((8, COLS), F32))
        if n < 3:
            i = (2, 0, 1)[n]
            scale = scale_of(peak)
            scale_src[3 + i] = pack(scale * (1.0 / 32767))
            near_scale(i).start()
            inverse = 32767.0 / scale

            def encode_near(j, _, i=i, inverse=inverse):
                near_coded[i, j] = encode(summed[j], inverse)
                return 0

            lax.fori_loop(0, 4, encode_near, 0)
            near_copy(i).start()

    for i in range(3):
        near_scale(i).wait_recv()
    scales = [unpack(scale_dst[3 + i]) for i in range(3)]
    for i in (0, 1, 2):
        near_copy(i).wait_recv()
    for d in (2, 1, 3, 0):
        j = lax.rem(lax.div(z, 4) + d, 4)
        grad = summed[j]
        for i in range(3):
            grad = grad + decode(lrecv[i, j], scales[i])
        if d:
            scale = scale_of(peak_of(grad))
            scale_src[6 + d - 1] = pack(scale * (1.0 / 32767))
            far_scale(d - 1).start()
            far_coded[d - 1] = encode(grad, 32767.0 / scale)
            far_copy(d - 1).start()
    for i in range(3):
        far_scale(i).wait_recv()
        far_copy(i).wait_recv()
        grad = grad + decode(frecv[i], unpack(scale_dst[6 + i]))

    squared = grad * grad
    row_lanes = squared[:, :128]
    for i in range(1, COLS // 128):
        row_lanes = row_lanes + squared[:, i * 128 : (i + 1) * 128]
    row_src[...] = row_lanes

    def row_copy(i):
        return pltpu.make_async_remote_copy(
            src_ref=row_src,
            dst_ref=row_dst.at[i],
            send_sem=row_send.at[i],
            recv_sem=row_recv.at[i],
            device_id=mp_peers[i],
            device_id_type=MESH,
        )

    def vec_copies(step, landing, sems, peers):
        return [
            pltpu.make_async_remote_copy(
                src_ref=vec.at[step],
                dst_ref=landing.at[i],
                send_sem=sems.at[0, i],
                recv_sem=sems.at[1, i],
                device_id=peer,
                device_id_type=MESH,
            )
            for i, peer in enumerate(peers)
        ]

    rounds = [
        vec_copies(0, vec_x, vx_sem, x_peers),
        vec_copies(1, vec_z, vz_sem, z_peers),
        vec_copies(2, vec_m, vm_sem, mp_peers),
    ]

    def begin(step):
        for copy in rounds[step]:
            copy.start()

    def total_of(step, landing):
        sums = vec[step]
        for i, copy in enumerate(rounds[step]):
            copy.wait_recv()
            sums = sums + landing[i]
        return sums

    column = jnp.sum(squared, axis=0, keepdims=True)
    vec[0] = pack(column, jnp.sum(row_lanes, axis=0, keepdims=True), moment_lanes)
    begin(0)
    for i in range(NMP - 1):
        row_copy(i).start()
    peak = scale_of(peak_of(grad))
    nbuf[dp] = encode(grad, 32767.0 / peak)
    regather = Gather(nbuf, ag2_send, ag2_recv, x, z, mp)
    regather.start()
    events = regather.events()
    next(events)

    vec[1] = total_of(0, vec_x)
    begin(1)
    for i in range(NMP - 1):
        row_copy(i).wait_recv()
        row_lanes = row_lanes + row_dst[i]
    row_total = jnp.sum(row_lanes, axis=1, keepdims=True)
    retiles = Tiles(ntile, nt_send, nt_recv, x, z, mp)
    ntile[retiles.index(x, z)] = pack(peak * (1.0 / 32767), to_lanes(row_total))
    retiles.across()
    next(events)

    retiles.far()
    next(events)
    sums = total_of(1, vec_z)
    vec[2] = sums
    begin(2)
    retiles.near()
    next(events)
    norm = total_of(2, vec_m)[6:7]
    col_total = unpack(sums)
    total = jnp.sum(norm, axis=1, keepdims=True)
    moments = jnp.sum(sums[7:8], axis=1, keepdims=True)

    clip = 1.0 / jnp.maximum(1.0, jnp.sqrt(total / (D * FF)))

    def next_row_state(old, squares):
        return decay_rate * old + (1.0 - decay_rate) * (clip * clip * squares / FF + epsilon)

    row_state = next_row_state(moment, row_total)
    col_state = decay_rate * cmom_ref[...].reshape(1, COLS) + (1.0 - decay_rate) * (clip * clip * col_total / D + epsilon)
    row_mean = decay_rate * moments / D + (1.0 - decay_rate) * (clip * clip * (total / FF) / D + epsilon)
    col_factor = step_rate * clip * lax.rsqrt(col_state)
    new_ref[...] = master_ref[...] - grad * (lax.rsqrt(row_state / row_mean) * col_factor)
    rstate_ref[...] = to_lanes(row_state)[:, :ROWS].reshape(ROWS)
    cstate_ref[...] = col_state.reshape(COLS)
    retiles.arrived(6)

    def updated(slot):
        old, old_moment = weights(slot)
        retile = ntile[retiles.index(lax.div(slot, NZ), lax.rem(slot, NZ))]
        row_factor = to_rows(lax.rsqrt(next_row_state(old_moment, retile[6:7]) / row_mean))
        return old - raw(nbuf[slot]) * (unpack(retile) * col_factor) * row_factor

    def leave(d):
        rows = pl.ds(pl.multiple_of(lax.rem(x + d, NX) * BLOCK, BLOCK), BLOCK)
        return pltpu.make_async_copy(low.at[rows], low_ref.at[rows], load_sem.at[2 + d])

    for d in (0, 1, 3, 2):
        block = lax.rem(x + d, NX)

        def update_pair(i, _, d=d, block=block):
            slot = block * NZ + 2 * i
            regather.wait_pair(d, slot)
            rows = pl.ds(pl.multiple_of(slot * ROWS, 2 * ROWS), 2 * ROWS)
            low[rows, :] = stack(updated(slot), updated(slot + 1))
            return 0

        lax.fori_loop(0, NZ // 2, update_pair, 0)
        leave(d).start()
    tiles.finish()
    retiles.finish()
    for i in range(NMP - 1):
        row_copy(i).wait_send()
    for copies in rounds:
        for copy in copies:
            copy.wait_send()
    gather.finish()
    regather.finish()
    for d in (1, 2, 3):
        x_scale(d).wait_send()
        for cls in range(4):
            x_copy(d, cls).wait_send()
    for i in range(3):
        near_scale(i).wait_send()
        near_copy(i).wait_send()
        far_scale(i).wait_send()
        far_copy(i).wait_send()
    for d in range(NX):
        leave(d).wait()


def copy_kernel(new_in, rstate_in, cstate_in, low_in, new_out, rstate_out, cstate_out, low_out, new, rstate, cstate, low, sem):
    pieces = 4
    size = D // pieces
    ways = [(low_in.at[pl.ds(i * size, size)], low.at[pl.ds(i * size, size)], low_out.at[pl.ds(i * size, size)]) for i in range(pieces)]
    ways += [(new_in, new, new_out), (rstate_in, rstate, rstate_out), (cstate_in, cstate, cstate_out)]
    come = [pltpu.make_async_copy(a, b, sem.at[0, i]) for i, (a, b, _) in enumerate(ways)]
    go = [pltpu.make_async_copy(b, c, sem.at[1, i]) for i, (_, b, c) in enumerate(ways)]
    for copy in come:
        copy.start()
    for first, second in zip(come, go):
        first.wait()
        second.start()
    for copy in go:
        copy.wait()


def per_device(features, frame_start, chan_start, master_weight, row_moment, col_moment, out_grad):
    vmem = pl.BlockSpec(memory_space=pltpu.VMEM)
    smem = pl.BlockSpec(memory_space=pltpu.SMEM)
    out_shape = (
        jax.ShapeDtypeStruct((ROWS, COLS), F32),
        jax.ShapeDtypeStruct((ROWS,), F32),
        jax.ShapeDtypeStruct((COLS,), F32),
        jax.ShapeDtypeStruct((D, COLS), BF16),
    )
    anywhere = pl.BlockSpec(memory_space=pl.ANY)
    results = pl.pallas_call(
        kernel,
        name="adafactor_step",
        out_shape=out_shape,
        in_specs=[smem, smem, anywhere, anywhere, anywhere, anywhere, anywhere],
        out_specs=(vmem, vmem, vmem, anywhere),
        scratch_shapes=[
            pltpu.VMEM((ROWS, COLS), F32),
            pltpu.VMEM((ROWS,), F32),
            pltpu.VMEM((COLS,), F32),
            pltpu.VMEM((NX * NZ, 2 * ROWS, HALF), I16),
            pltpu.VMEM((NX * NZ, 1, 128), F32),
            pltpu.VMEM((D, COLS), BF16),
            pltpu.VMEM((NX * NZ, 2 * ROWS, HALF), I16),
            pltpu.VMEM((NX * NZ, 8, 128), F32),
            pltpu.VMEM((D, COLS), BF16),
            pltpu.VMEM((TOK, D), BF16),
            pltpu.VMEM((TOK, COLS), BF16),
            pltpu.VMEM((TOK, D), BF16),
            pltpu.VMEM((D, TOK), BF16),
            pltpu.VMEM((TOK, COLS), F32),
            pltpu.VMEM((TOK, COLS), BF16),
            pltpu.VMEM((NX, 4, 4, ROWS, COLS), F32),
            pltpu.VMEM((NX - 1, 8, COLS), F32),
            pltpu.VMEM((NX - 1, 4, 4, 2 * ROWS, HALF), I16),
            pltpu.VMEM((NX - 1, 4, 4, 2 * ROWS, HALF), I16),
            pltpu.VMEM((4, ROWS, COLS), F32),
            pltpu.VMEM((3, 4, 2 * ROWS, HALF), I16),
            pltpu.VMEM((3, 4, 2 * ROWS, HALF), I16),
            pltpu.VMEM((3, 2 * ROWS, HALF), I16),
            pltpu.VMEM((3, 2 * ROWS, HALF), I16),
            pltpu.VMEM((9, 8, 128), F32),
            pltpu.VMEM((9, 8, 128), F32),
            pltpu.VMEM((ROWS, 128), F32),
            pltpu.VMEM((NMP - 1, ROWS, 128), F32),
            pltpu.VMEM((3, 8, 128), F32),
            pltpu.VMEM((NX - 1, 8, 128), F32),
            pltpu.VMEM((NZ - 1, 8, 128), F32),
            pltpu.VMEM((NMP - 1, 8, 128), F32),
            pltpu.SemaphoreType.DMA((NX * NZ,)),
            pltpu.SemaphoreType.DMA((NX * NZ,)),
            pltpu.SemaphoreType.DMA((NX * NZ,)),
            pltpu.SemaphoreType.DMA((NX * NZ,)),
            pltpu.SemaphoreType.DMA((27,)),
            pltpu.SemaphoreType.DMA((27,)),
            pltpu.SemaphoreType.DMA((NMP - 1,)),
            pltpu.SemaphoreType.DMA((NMP - 1,)),
            pltpu.SemaphoreType.DMA((2, NX - 1)),
            pltpu.SemaphoreType.DMA((2, NZ - 1)),
            pltpu.SemaphoreType.DMA((2, NMP - 1)),
            pltpu.SemaphoreType.DMA((9,)),
            pltpu.SemaphoreType.DMA((9,)),
            pltpu.SemaphoreType.DMA((9,)),
            pltpu.SemaphoreType.DMA((9,)),
            pltpu.SemaphoreType.DMA((2 + NX,)),
            pltpu.SemaphoreType.DMA((3,)),
        ],
        compiler_params=pltpu.CompilerParams(collective_id=0, has_side_effects=True, vmem_limit_bytes=56 * 2**20),
    )(frame_start, chan_start, features, master_weight, row_moment, col_moment, out_grad)

    return pl.pallas_call(
        copy_kernel,
        name="results",
        out_shape=out_shape,
        in_specs=[anywhere] * 4,
        out_specs=(anywhere,) * 4,
        scratch_shapes=[pltpu.VMEM(out.shape, out.dtype) for out in out_shape] + [pltpu.SemaphoreType.DMA((2, 7))],
        compiler_params=pltpu.CompilerParams(vmem_limit_bytes=60 * 2**20),
    )(*results)


def solution(mesh):
    placed = (P("dp", None), P("dp"), P("dp"), P("dp", "mp"), P("dp"), P("mp"), P("dp", "mp"))
    return jax.shard_map(
        per_device,
        mesh=mesh,
        in_specs=placed,
        out_specs=(P("dp", "mp"), P("dp"), P("mp"), P(None, "mp")),
        check_vma=False,
    )
```

```python
import functools

import jax
import jax.numpy as jnp
from jax import lax
from jax.experimental import pallas as pl
from jax.experimental.pallas import tpu as pltpu
from jax.sharding import PartitionSpec as P

D = 1536
FF = 6144
TMASK = 128
FMASK = 192
NX = 4
NZ = 16
NMP = 8
TOK = 512
ROWS = D // (NX * NZ)
COLS = FF // NMP
HALF = COLS // 2
BLOCK = ROWS * NZ

epsilon = 1e-06
decay_rate = 0.8
step_rate = 0.01

MESH = pl.DeviceIdType.MESH
F32 = jnp.float32
BF16 = jnp.bfloat16
I16 = jnp.int16


def fold(rows):
    return jnp.concatenate([rows[:, :HALF], rows[:, HALF:]], axis=0)


class Gather:
    def __init__(self, buf, send_sem, recv_sem, x, z, mp):
        self.buf, self.send_sem, self.recv_sem = buf, send_sem, recv_sem
        self.x, self.z, self.mp = x, z, mp
        self.up, self.down = lax.rem(x + 1, NX), lax.rem(x + NX - 1, NX)
        self.line = [lax.rem(z + o, NZ) for o in range(NZ)]
        odd = lax.rem(z, 2)
        self.relay_from = [self.down + (self.up - self.down) * p for p in (odd, 1 - odd)]
        self.relay_to = [self.up + (self.down - self.up) * p for p in (odd, 1 - odd)]
        self.sent = 0

    def copy(self, slot, k, x, z):
        return pltpu.make_async_remote_copy(
            src_ref=self.buf.at[slot],
            dst_ref=self.buf.at[slot],
            send_sem=self.send_sem.at[k],
            recv_sem=self.recv_sem.at[slot],
            device_id=(x * NZ + z, self.mp),
            device_id_type=MESH,
        )

    def send(self, slot, x, z):
        self.copy(slot, self.sent, x, z).start()
        self.sent += 1

    def slot(self, o):
        return self.x * NZ + self.line[o]

    def arrived(self, slot):
        self.copy(slot, 0, self.x, self.z).wait_recv()

    def along_x(self, o):
        self.send(self.slot(o), self.up, self.z)
        self.send(self.slot(o), self.down, self.z)

    def near(self, o):
        for d in (2, 1, 15):
            self.send(self.slot(o), self.x, self.line[d])

    def relay(self, o):
        slot = self.relay_from[o % 2] * NZ + self.line[o]
        self.arrived(slot)
        self.send(slot, self.relay_to[o % 2], self.z)

    def start(self):
        for d in (8, 4, 12):
            self.send(self.slot(0), self.x, self.line[d])
        self.near(0)
        self.along_x(0)

    def far(self, o):
        self.arrived(self.slot(o))
        self.near(o)
        self.along_x(o)

    def pass_on(self, *offsets):
        for o in offsets:
            self.arrived(self.slot(o))
            self.along_x(o)

    def relays(self, *offsets):
        for o in offsets:
            self.relay(o)

    def events(self):
        self.pass_on(15, 1, 14)
        self.relays(0)
        yield
        self.far(4)
        self.far(12)
        self.relays(15, 1, 14)
        self.far(8)
        self.relays(4, 12)
        yield
        self.pass_on(3, 5, 2, 11, 13, 10)
        self.relays(8)
        self.pass_on(7, 9, 6)
        yield
        self.relays(3, 5, 2, 11, 13, 10, 7, 9, 6)
        yield

    def wait_pair(self, d, slot):
        if d in (1, 2):
            self.arrived(slot)
        if d in (3, 2):
            self.arrived(slot + 1)

    def finish(self):
        def step(k, _):
            self.copy(0, k, self.x, self.z).wait_send()
            return 0

        lax.fori_loop(0, NX * NZ - 1, step, 0)


class Tiles:
    def __init__(self, buf, send_sem, recv_sem, x, z, mp):
        self.buf, self.send_sem, self.recv_sem = buf, send_sem, recv_sem
        self.x, self.z, self.mp = x, z, mp
        self.sent = []

    def index(self, x, z):
        return lax.rem(z, 4) * 16 + lax.div(z, 4) * 4 + x

    def round(self, first, count, k, peers):
        for i, peer in enumerate(peers):
            block = self.buf.at[pl.ds(first, count)]
            copy = pltpu.make_async_remote_copy(
                src_ref=block,
                dst_ref=block,
                send_sem=self.send_sem.at[k + i],
                recv_sem=self.recv_sem.at[k + i],
                device_id=peer,
                device_id_type=MESH,
            )
            copy.start()
            self.sent.append(copy)

    def arrived(self, k):
        for copy in self.sent[k : k + 3]:
            copy.wait_recv()

    def along(self, distances):
        return [(self.x * NZ + lax.rem(self.z + d, NZ), self.mp) for d in distances]

    def across(self):
        peers = [(lax.rem(self.x + d, NX) * NZ + self.z, self.mp) for d in (2, 1, 3)]
        self.round(self.index(self.x, self.z), 1, 0, peers)

    def far(self):
        self.arrived(0)
        self.round(self.index(0, self.z), 4, 3, self.along((8, 4, 12)))

    def near(self):
        self.arrived(3)
        self.round(lax.rem(self.z, 4) * 16, 16, 6, self.along((2, 1, 15)))

    def finish(self):
        for copy in self.sent:
            copy.wait_send()


def stack(first, second):
    return jnp.concatenate([first, second], axis=0).astype(BF16)


def unfold(slot):
    return jnp.concatenate([slot[:ROWS], slot[ROWS:]], axis=1)


def pack(row, *more):
    pieces = [row[:, i * 128 : (i + 1) * 128] for i in range(COLS // 128)] + list(more)
    if len(pieces) < 8:
        pieces.append(jnp.zeros((8 - len(pieces), 128), F32))
    return jnp.concatenate(pieces, axis=0)


def raw(slot):
    return unfold(slot.astype(jnp.int32).astype(F32))


def unpack(tile):
    return jnp.concatenate([tile[i : i + 1] for i in range(COLS // 128)], axis=1)


def peak_of(rows):
    size = jnp.abs(rows)
    return jnp.maximum(jnp.maximum(size[:8], size[8:16]), size[16:24])


def scale_of(peak):
    return jnp.maximum(jnp.max(peak, axis=0, keepdims=True), 1e-30)


def encode(rows, inverse):
    return jnp.round(fold(rows * inverse)).astype(jnp.int32).astype(I16)


def decode(slot, scale):
    return raw(slot) * scale


def kernel(
    frame_ref, chan_ref, feat_hbm, master_hbm, rmom_hbm, cmom_hbm, grad_hbm,
    new_hbm, rstate_hbm, cstate_hbm, low_ref,
    new_ref, rstate_ref, cstate_ref,
    master_ref, rmom_ref, cmom_ref, wbuf, wtile, weight, nbuf, ntile, low, feat, grad_in, masked, masked_t, pre, dpre,
    partial, inverses, coded, xrecv, summed, near_coded, lrecv, far_coded, frecv, scale_src, scale_dst,
    row_src, row_dst, vec, vec_x, vec_z, vec_m,
    ag_send, ag_recv, ag2_send, ag2_recv, rs_send, rs_recv, row_send, row_recv, vx_sem, vz_sem, vm_sem, wt_send, wt_recv, nt_send, nt_recv, load_sem, own_sem,
):
    dp, mp = lax.axis_index("dp"), lax.axis_index("mp")
    x, z = lax.div(dp, NZ), lax.rem(dp, NZ)

    def at(dx, dz):
        return (lax.rem(x + dx, NX) * NZ + lax.rem(z + dz, NZ), mp)

    x_peers = [at(d, 0) for d in (1, 2, 3)]
    near_peers = [at(0, d) for d in (1, NZ - 1, 2)]
    far_peers = [at(0, d) for d in (4, 8, 12)]
    mp_peers = [(dp, lax.rem(mp + d, NMP)) for d in range(1, NMP)]

    barrier = pltpu.get_barrier_semaphore()
    z_peers = [at(0, d) for d in range(1, NZ)]
    greeted = z_peers + x_peers + mp_peers
    for peer in greeted:
        pl.semaphore_signal(barrier, inc=1, device_id=peer, device_id_type=MESH)

    own_loads = [
        pltpu.make_async_copy(source, target, own_sem.at[i])
        for i, (source, target) in enumerate(((master_hbm, master_ref), (rmom_hbm, rmom_ref), (cmom_hbm, cmom_ref)))
    ]
    for load in own_loads:
        load.start()
    load_feat = pltpu.make_async_copy(feat_hbm, feat, load_sem.at[0])
    load_grad = pltpu.make_async_copy(grad_hbm, grad_in, load_sem.at[1])
    load_feat.start()
    load_grad.start()

    for load in own_loads:
        load.wait()
    master = master_ref[...]
    peak = jnp.max(scale_of(peak_of(master)), axis=1, keepdims=True)
    diag = lax.broadcasted_iota(jnp.int32, (ROWS, 128), 0) == lax.broadcasted_iota(jnp.int32, (ROWS, 128), 1)

    def to_lanes(column):
        return jnp.sum(jnp.where(diag, column, 0.0), axis=0, keepdims=True)

    def to_rows(lanes):
        return jnp.sum(jnp.where(diag, lanes, 0.0), axis=1, keepdims=True)

    moment_lanes = jnp.concatenate([rmom_ref[...].reshape(1, ROWS), jnp.zeros((1, 128 - ROWS), F32)], axis=1)
    lane = lax.broadcasted_iota(jnp.int32, (1, 128), 1)
    wbuf[dp] = encode(master, 32767.0 / peak)
    tiles = Tiles(wtile, wt_send, wt_recv, x, z, mp)
    wtile[tiles.index(x, z)] = jnp.where(lane == 127, peak * (1.0 / 32767), moment_lanes)

    pl.semaphore_wait(barrier, len(greeted))
    tiles.across()
    gather = Gather(wbuf, ag_send, ag_recv, x, z, mp)
    gather.start()

    load_feat.wait()
    first_frame, first_chan = frame_ref[0], chan_ref[0]
    channel = lax.broadcasted_iota(jnp.int32, (1, D), 1)
    chan_keep = jnp.where((channel < first_chan) | (channel >= first_chan + FMASK), 1.0, 0.0)

    def mask_rows(i, _):
        rows = pl.ds(pl.multiple_of(i * 128, 128), 128)
        offset = lax.broadcasted_iota(jnp.int32, (128, 1), 0) + i * 128
        time_keep = jnp.where((offset < first_frame) | (offset >= first_frame + TMASK), 1.0, 0.0)
        kept = feat[rows, :] * (time_keep * chan_keep).astype(BF16)
        masked[rows, :] = kept
        masked_t[:, rows] = kept.T
        return 0

    lax.fori_loop(0, TOK // 128, mask_rows, 0)
    load_grad.wait()
    moment = to_rows(moment_lanes)
    for part, _ in enumerate(gather.events()):
        if part == 0:
            tiles.far()
        elif part == 2:
            tiles.near()
    tiles.arrived(6)

    def weights(slot):
        tile = wtile[tiles.index(lax.div(slot, NZ), lax.rem(slot, NZ))]
        return decode(wbuf[slot], tile[:, 127:128]), tile

    def weight_block(d, block):
        def step(i, _):
            slot = block * NZ + 2 * i
            gather.wait_pair(d, slot)
            rows = pl.ds(pl.multiple_of(slot * ROWS, 2 * ROWS), 2 * ROWS)
            weight[rows, :] = stack(weights(slot)[0], weights(slot + 1)[0])
            return 0

        lax.fori_loop(0, NZ // 2, step, 0)

    for d in (0, 1, 3, 2):
        block = lax.rem(x + d, NX)
        weight_block(d, block)
        depth = pl.ds(pl.multiple_of(block * BLOCK, BLOCK), BLOCK)

        def forward_tile(i, _, d=d, depth=depth):
            cols = pl.ds(pl.multiple_of(i * 256, 256), 256)
            term = jnp.dot(masked[:, depth], weight[depth, cols], preferred_element_type=F32)
            if d == 0:
                pre[:, cols] = term
            else:
                total = pre[:, cols] + term
                if d != 2:
                    pre[:, cols] = total
                else:
                    s = jax.nn.sigmoid(total)
                    slope = s + total * s * (1.0 - s)
                    dpre[:, cols] = (grad_in[:, cols].astype(F32) * slope).astype(BF16)
            return 0

        lax.fori_loop(0, COLS // 256, forward_tile, 0)

    def remote(src, dst, i, to):
        return pltpu.make_async_remote_copy(
            src_ref=src,
            dst_ref=dst,
            send_sem=rs_send.at[i],
            recv_sem=rs_recv.at[i],
            device_id=to,
            device_id_type=MESH,
        )

    def x_copy(d, cls):
        return remote(coded.at[d - 1, cls], xrecv.at[d - 1, cls], (d - 1) * 4 + cls, at(d, 0))

    def x_scale(d):
        return remote(scale_src.at[d - 1], scale_dst.at[d - 1], 12 + d - 1, at(d, 0))

    def near_copy(i):
        return remote(near_coded.at[i], lrecv.at[i], 15 + i, near_peers[i])

    def near_scale(i):
        return remote(scale_src.at[3 + i], scale_dst.at[3 + i], 18 + i, near_peers[i])

    def far_copy(i):
        return remote(far_coded.at[i], frecv.at[i], 21 + i, far_peers[i])

    def far_scale(i):
        return remote(scale_src.at[6 + i], scale_dst.at[6 + i], 24 + i, far_peers[i])

    classes = [lax.rem(z + d, 4) for d in (2, 1, 3, 0)]

    def grad_block(d):
        block = lax.rem(x + d, NX)

        def grad_tile(i, peak):
            rows = pl.ds(pl.multiple_of(block * BLOCK + i * 4 * ROWS, 32), 4 * ROWS)
            term = jnp.dot(masked_t[rows, :], dpre[...], preferred_element_type=F32)
            for j in range(4):
                slot = term[j * ROWS : (j + 1) * ROWS]
                partial[d, j, i] = slot
                peak = jnp.maximum(peak, peak_of(slot))
            return peak

        peak = lax.fori_loop(0, NZ // 4, grad_tile, jnp.zeros((8, COLS), F32))
        if d:
            scale = scale_of(peak)
            scale_src[d - 1] = pack(scale * (1.0 / 32767))
            x_scale(d).start()
            inverses[d - 1] = jnp.broadcast_to(32767.0 / scale, (8, COLS))

    def send_class(d, cls):
        inverse = inverses[d - 1][:1]

        def encode_slot(j, _):
            coded[d - 1, cls, j] = encode(partial[d, cls, j], inverse)
            return 0

        lax.fori_loop(0, 4, encode_slot, 0)
        x_copy(d, cls).start()

    for d in (2, 1, 3):
        grad_block(d)
        send_class(d, classes[0])
    grad_block(0)
    for cls in classes[1:]:
        for d in (2, 1, 3):
            send_class(d, cls)

    for d in (1, 2, 3):
        x_scale(d).wait_recv()
    scales = [unpack(scale_dst[i]) for i in range(3)]
    for n, cls in enumerate(classes):
        for d in (2, 1, 3):
            x_copy(d, cls).wait_recv()

        def add_x(j, peak, cls=cls):
            term = partial[0, cls, j]
            for i in range(3):
                term = term + decode(xrecv[i, cls, j], scales[i])
            summed[j] = term
            return jnp.maximum(peak, peak_of(term))

        peak = lax.fori_loop(0, 4, add_x, jnp.zeros((8, COLS), F32))
        if n < 3:
            i = (2, 0, 1)[n]
            scale = scale_of(peak)
            scale_src[3 + i] = pack(scale * (1.0 / 32767))
            near_scale(i).start()
            inverse = 32767.0 / scale

            def encode_near(j, _, i=i, inverse=inverse):
                near_coded[i, j] = encode(summed[j], inverse)
                return 0

            lax.fori_loop(0, 4, encode_near, 0)
            near_copy(i).start()

    for i in range(3):
        near_scale(i).wait_recv()
    scales = [unpack(scale_dst[3 + i]) for i in range(3)]
    for i in (0, 1, 2):
        near_copy(i).wait_recv()
    for d in (2, 1, 3, 0):
        j = lax.rem(lax.div(z, 4) + d, 4)
        grad = summed[j]
        for i in range(3):
            grad = grad + decode(lrecv[i, j], scales[i])
        if d:
            scale = scale_of(peak_of(grad))
            scale_src[6 + d - 1] = pack(scale * (1.0 / 32767))
            far_scale(d - 1).start()
            far_coded[d - 1] = encode(grad, 32767.0 / scale)
            far_copy(d - 1).start()
    for i in range(3):
        far_scale(i).wait_recv()
        far_copy(i).wait_recv()
        grad = grad + decode(frecv[i], unpack(scale_dst[6 + i]))

    squared = grad * grad
    row_lanes = squared[:, :128]
    for i in range(1, COLS // 128):
        row_lanes = row_lanes + squared[:, i * 128 : (i + 1) * 128]
    row_src[...] = row_lanes

    def row_copy(i):
        return pltpu.make_async_remote_copy(
            src_ref=row_src,
            dst_ref=row_dst.at[i],
            send_sem=row_send.at[i],
            recv_sem=row_recv.at[i],
            device_id=mp_peers[i],
            device_id_type=MESH,
        )

    def vec_copies(step, landing, sems, peers):
        return [
            pltpu.make_async_remote_copy(
                src_ref=vec.at[step],
                dst_ref=landing.at[i],
                send_sem=sems.at[0, i],
                recv_sem=sems.at[1, i],
                device_id=peer,
                device_id_type=MESH,
            )
            for i, peer in enumerate(peers)
        ]

    rounds = [
        vec_copies(0, vec_x, vx_sem, x_peers),
        vec_copies(1, vec_z, vz_sem, z_peers),
        vec_copies(2, vec_m, vm_sem, mp_peers),
    ]

    def begin(step):
        for copy in rounds[step]:
            copy.start()

    def total_of(step, landing):
        sums = vec[step]
        for i, copy in enumerate(rounds[step]):
            copy.wait_recv()
            sums = sums + landing[i]
        return sums

    column = jnp.sum(squared, axis=0, keepdims=True)
    vec[0] = pack(column, jnp.sum(row_lanes, axis=0, keepdims=True), moment_lanes)
    begin(0)
    for i in range(NMP - 1):
        row_copy(i).start()
    peak = scale_of(peak_of(grad))
    nbuf[dp] = encode(grad, 32767.0 / peak)
    regather = Gather(nbuf, ag2_send, ag2_recv, x, z, mp)
    regather.start()
    events = regather.events()
    next(events)

    vec[1] = total_of(0, vec_x)
    begin(1)
    for i in range(NMP - 1):
        row_copy(i).wait_recv()
        row_lanes = row_lanes + row_dst[i]
    row_total = jnp.sum(row_lanes, axis=1, keepdims=True)
    retiles = Tiles(ntile, nt_send, nt_recv, x, z, mp)
    ntile[retiles.index(x, z)] = pack(peak * (1.0 / 32767), to_lanes(row_total))
    retiles.across()
    next(events)

    retiles.far()
    next(events)
    sums = total_of(1, vec_z)
    vec[2] = sums
    begin(2)
    retiles.near()
    next(events)
    norm = total_of(2, vec_m)[6:7]
    col_total = unpack(sums)
    total = jnp.sum(norm, axis=1, keepdims=True)
    moments = jnp.sum(sums[7:8], axis=1, keepdims=True)

    clip = 1.0 / jnp.maximum(1.0, jnp.sqrt(total / (D * FF)))

    def next_row_state(old, squares):
        return decay_rate * old + (1.0 - decay_rate) * (clip * clip * squares / FF + epsilon)

    row_state = next_row_state(moment, row_total)
    col_state = decay_rate * cmom_ref[...].reshape(1, COLS) + (1.0 - decay_rate) * (clip * clip * col_total / D + epsilon)
    row_mean = decay_rate * moments / D + (1.0 - decay_rate) * (clip * clip * (total / FF) / D + epsilon)
    col_factor = step_rate * clip * lax.rsqrt(col_state)
    new_ref[...] = master_ref[...] - grad * (lax.rsqrt(row_state / row_mean) * col_factor)
    rstate_ref[...] = to_lanes(row_state)[:, :ROWS].reshape(ROWS)
    cstate_ref[...] = col_state.reshape(COLS)
    own_stores = [
        pltpu.make_async_copy(source, target, own_sem.at[3 + i])
        for i, (source, target) in enumerate(((new_ref, new_hbm), (rstate_ref, rstate_hbm), (cstate_ref, cstate_hbm)))
    ]
    for store in own_stores:
        store.start()
    retiles.arrived(6)

    def updated(slot):
        old, old_moment = weights(slot)
        retile = ntile[retiles.index(lax.div(slot, NZ), lax.rem(slot, NZ))]
        row_factor = to_rows(lax.rsqrt(next_row_state(old_moment, retile[6:7]) / row_mean))
        return old - raw(nbuf[slot]) * (unpack(retile) * col_factor) * row_factor

    def leave(d):
        rows = pl.ds(pl.multiple_of(lax.rem(x + d, NX) * BLOCK, BLOCK), BLOCK)
        return pltpu.make_async_copy(low.at[rows], low_ref.at[rows], load_sem.at[2 + d])

    for d in (0, 1, 3, 2):
        block = lax.rem(x + d, NX)

        def update_pair(i, _, d=d, block=block):
            slot = block * NZ + 2 * i
            regather.wait_pair(d, slot)
            rows = pl.ds(pl.multiple_of(slot * ROWS, 2 * ROWS), 2 * ROWS)
            low[rows, :] = stack(updated(slot), updated(slot + 1))
            return 0

        lax.fori_loop(0, NZ // 2, update_pair, 0)
        leave(d).start()
    tiles.finish()
    retiles.finish()
    for i in range(NMP - 1):
        row_copy(i).wait_send()
    for copies in rounds:
        for copy in copies:
            copy.wait_send()
    gather.finish()
    regather.finish()
    for d in (1, 2, 3):
        x_scale(d).wait_send()
        for cls in range(4):
            x_copy(d, cls).wait_send()
    for i in range(3):
        near_scale(i).wait_send()
        near_copy(i).wait_send()
        far_scale(i).wait_send()
        far_copy(i).wait_send()
    for d in range(NX):
        leave(d).wait()
    for store in own_stores:
        store.wait()


def copy_kernel(new_in, rstate_in, cstate_in, low_in, new_out, rstate_out, cstate_out, low_out, new, rstate, cstate, low, sem):
    pieces = 4
    size = D // pieces
    ways = [(low_in.at[pl.ds(i * size, size)], low.at[pl.ds(i * size, size)], low_out.at[pl.ds(i * size, size)]) for i in range(pieces)]
    ways += [(new_in, new, new_out), (rstate_in, rstate, rstate_out), (cstate_in, cstate, cstate_out)]
    come = [pltpu.make_async_copy(a, b, sem.at[0, i]) for i, (a, b, _) in enumerate(ways)]
    go = [pltpu.make_async_copy(b, c, sem.at[1, i]) for i, (_, b, c) in enumerate(ways)]
    for copy in come:
        copy.start()
    for first, second in zip(come, go):
        first.wait()
        second.start()
    for copy in go:
        copy.wait()


def per_device(features, frame_start, chan_start, master_weight, row_moment, col_moment, out_grad):
    smem = pl.BlockSpec(memory_space=pltpu.SMEM)
    out_shape = (
        jax.ShapeDtypeStruct((ROWS, COLS), F32),
        jax.ShapeDtypeStruct((ROWS,), F32),
        jax.ShapeDtypeStruct((COLS,), F32),
        jax.ShapeDtypeStruct((D, COLS), BF16),
    )
    anywhere = pl.BlockSpec(memory_space=pl.ANY)
    results = pl.pallas_call(
        kernel,
        name="adafactor_step",
        out_shape=out_shape,
        in_specs=[smem, smem, anywhere, anywhere, anywhere, anywhere, anywhere],
        out_specs=(anywhere,) * 4,
        scratch_shapes=[
            pltpu.VMEM((ROWS, COLS), F32),
            pltpu.VMEM((ROWS,), F32),
            pltpu.VMEM((COLS,), F32),
            pltpu.VMEM((ROWS, COLS), F32),
            pltpu.VMEM((ROWS,), F32),
            pltpu.VMEM((COLS,), F32),
            pltpu.VMEM((NX * NZ, 2 * ROWS, HALF), I16),
            pltpu.VMEM((NX * NZ, 1, 128), F32),
            pltpu.VMEM((D, COLS), BF16),
            pltpu.VMEM((NX * NZ, 2 * ROWS, HALF), I16),
            pltpu.VMEM((NX * NZ, 8, 128), F32),
            pltpu.VMEM((D, COLS), BF16),
            pltpu.VMEM((TOK, D), BF16),
            pltpu.VMEM((TOK, COLS), BF16),
            pltpu.VMEM((TOK, D), BF16),
            pltpu.VMEM((D, TOK), BF16),
            pltpu.VMEM((TOK, COLS), F32),
            pltpu.VMEM((TOK, COLS), BF16),
            pltpu.VMEM((NX, 4, 4, ROWS, COLS), F32),
            pltpu.VMEM((NX - 1, 8, COLS), F32),
            pltpu.VMEM((NX - 1, 4, 4, 2 * ROWS, HALF), I16),
            pltpu.VMEM((NX - 1, 4, 4, 2 * ROWS, HALF), I16),
            pltpu.VMEM((4, ROWS, COLS), F32),
            pltpu.VMEM((3, 4, 2 * ROWS, HALF), I16),
            pltpu.VMEM((3, 4, 2 * ROWS, HALF), I16),
            pltpu.VMEM((3, 2 * ROWS, HALF), I16),
            pltpu.VMEM((3, 2 * ROWS, HALF), I16),
            pltpu.VMEM((9, 8, 128), F32),
            pltpu.VMEM((9, 8, 128), F32),
            pltpu.VMEM((ROWS, 128), F32),
            pltpu.VMEM((NMP - 1, ROWS, 128), F32),
            pltpu.VMEM((3, 8, 128), F32),
            pltpu.VMEM((NX - 1, 8, 128), F32),
            pltpu.VMEM((NZ - 1, 8, 128), F32),
            pltpu.VMEM((NMP - 1, 8, 128), F32),
            pltpu.SemaphoreType.DMA((NX * NZ,)),
            pltpu.SemaphoreType.DMA((NX * NZ,)),
            pltpu.SemaphoreType.DMA((NX * NZ,)),
            pltpu.SemaphoreType.DMA((NX * NZ,)),
            pltpu.SemaphoreType.DMA((27,)),
            pltpu.SemaphoreType.DMA((27,)),
            pltpu.SemaphoreType.DMA((NMP - 1,)),
            pltpu.SemaphoreType.DMA((NMP - 1,)),
            pltpu.SemaphoreType.DMA((2, NX - 1)),
            pltpu.SemaphoreType.DMA((2, NZ - 1)),
            pltpu.SemaphoreType.DMA((2, NMP - 1)),
            pltpu.SemaphoreType.DMA((9,)),
            pltpu.SemaphoreType.DMA((9,)),
            pltpu.SemaphoreType.DMA((9,)),
            pltpu.SemaphoreType.DMA((9,)),
            pltpu.SemaphoreType.DMA((2 + NX,)),
            pltpu.SemaphoreType.DMA((6,)),
        ],
        compiler_params=pltpu.CompilerParams(collective_id=0, has_side_effects=True, vmem_limit_bytes=56 * 2**20),
    )(frame_start, chan_start, features, master_weight, row_moment, col_moment, out_grad)

    return pl.pallas_call(
        copy_kernel,
        name="results",
        out_shape=out_shape,
        in_specs=[anywhere] * 4,
        out_specs=(anywhere,) * 4,
        scratch_shapes=[pltpu.VMEM(out.shape, out.dtype) for out in out_shape] + [pltpu.SemaphoreType.DMA((2, 7))],
        compiler_params=pltpu.CompilerParams(vmem_limit_bytes=60 * 2**20),
    )(*results)


def solution(mesh):
    placed = (P("dp", None), P("dp"), P("dp"), P("dp", "mp"), P("dp"), P("mp"), P("dp", "mp"))
    return jax.shard_map(
        per_device,
        mesh=mesh,
        in_specs=placed,
        out_specs=(P("dp", "mp"), P("dp"), P("mp"), P(None, "mp")),
        check_vma=False,
    )
```
